256 devices in a mesh: prompt: 8 (over z), sample: 4 (over y), head: 8 (over x, core).
Axes of the slice: x: 4, y: 4, z: 8, core: 2. Of those that a mesh axis runs over, the one named last changes fastest.
Arguments:
- q_nope: bfloat16 [384, 2, 12288], P(('prompt', 'sample'), None, 'head'), may hold values from -3 to 3
- q_rope: bfloat16 [384, 2, 6144], P(('prompt', 'sample'), None, 'head'), may hold values from -24 to 24
- new_latent: bfloat16 [384, 2, 512], P(('prompt', 'sample')), may hold values from -4 to 4
- new_rope: bfloat16 [384, 2, 64], P(('prompt', 'sample')), may hold values from -4 to 4
- prompt_latent: bfloat16 [32, 2048, 512], P(('prompt', 'sample')), may hold values from -4 to 4
- prompt_rope: bfloat16 [32, 64, 2048], P(('prompt', 'sample')), may hold values from -4 to 4
- suffix_latent: bfloat16 [384, 128, 512], P(('prompt', 'sample')), may hold values from -4 to 4
- suffix_rope: bfloat16 [384, 64, 128], P(('prompt', 'sample')), may hold values from -4 to 4
- sample_prompt: int32 [384], P(('prompt', 'sample')), may hold values from 0 to 31, as said below
- suffix_len: int32 [384], P(('prompt', 'sample')), may hold values from 1 to 128, 24576 in all
- w_uk: bfloat16 [96, 128, 512], P('head'), may hold values from -0.5 to 0.5
- w_uv: bfloat16 [96, 512, 128], P('head'), may hold values from -1 to 1
- w_out: bfloat16 [12288, 7168], P('head', 'sample'), may hold values from -0.109375 to 0.109375
Outputs:
- layer_output: bfloat16 [384, 2, 7168], P('prompt', None, ('sample', 'head'))
The draws below stay inside these ranges and needn't reach their ends.
Inputs may be any that keep to these rules, and one draw needn't show every extreme that they name: `sample_prompt`: the rows of one device of prompt and sample name 12 different prompts. A prompt is named by at most 16 samples, and some prompt by exactly that many.
All inputs are finite; a program needn't handle non-finite values. No bound on the sum of `suffix_len` on one device may be relied on, other than what follows from the above.
Results may differ from the reference program's by a relative error of at most 0.0066.
Values may be sent and summed in bfloat16 or wider, within the bound.
A program may use at most 64 MiB of HBM per device.

```python
import math
import jax
import jax.numpy as jnp
import numpy as np
from jax import lax

D = 7168
H = 96
NOPE = 128
ROPE = 64
LAT = 512
VDIM = 128
PLEN = 2048
SUF = 128
SAMP_DEV = 12
PROMPTS = 32
SAMPLES = 384


def own_rope_keys(key):
    return jnp.clip(jax.random.normal(jax.random.fold_in(key, 223), (SAMPLES, 2, ROPE), jnp.float32), -4.0, 4.0)


def draw_new_rope(key, part):
    return own_rope_keys(key).astype(jnp.bfloat16)


def draw_q_rope(key, part):
    own_keys = own_rope_keys(key)
    key = jax.random.fold_in(key, 3)
    noise_key, pull_key = jax.random.split(key, 2)
    noise = 0.6 * jnp.clip(jax.random.normal(noise_key, (SAMPLES, 2, H, ROPE), jnp.float32), -4.0, 4.0)
    pull = jnp.exp(jax.random.uniform(pull_key, (H,), jnp.float32, jnp.log(0.8), jnp.log(1.6)))
    values = noise + pull[None, None, :, None] * own_keys[:, :, None, :]
    return values.reshape(SAMPLES, 2, H * ROPE).astype(jnp.bfloat16)


def draw_prompt_rope(key, part):
    key = jax.random.fold_in(key, 5)
    noise_key = jax.random.fold_in(key, 0)
    values = jnp.clip(jax.random.normal(noise_key, (PROMPTS, ROPE, PLEN), jnp.float32), -4.0, 4.0)
    return values.astype(jnp.bfloat16)


def draw_suffix_rope(key, part):
    key = jax.random.fold_in(key, 7)
    values = jnp.clip(jax.random.normal(key, (SAMPLES, ROPE, SUF), jnp.float32), -4.0, 4.0)
    return values.astype(jnp.bfloat16)


def draw_sample_prompt(key, part):
    key = jax.random.fold_in(key, 11)
    delta_key, order_key, label_key = jax.random.split(key, 3)
    reach = SAMP_DEV // 3
    delta = jax.random.randint(delta_key, (PROMPTS // 2,), -reach, reach + 1)
    delta = delta.at[0].set(reach)
    group_sizes = jnp.concatenate([SAMP_DEV + delta, SAMP_DEV - delta])
    group_ends = jnp.cumsum(group_sizes)
    row_order = jax.vmap(lambda row_key: jax.random.permutation(row_key, SAMP_DEV))(jax.random.split(order_key, PROMPTS))
    position = row_order * PROMPTS + jnp.arange(PROMPTS)[:, None]
    group_index = jnp.sum((group_ends[None, None, :] <= position[:, :, None]).astype(jnp.int32), axis=-1)
    labels = jax.random.permutation(label_key, PROMPTS)
    return labels[group_index].reshape(SAMPLES).astype(jnp.int32)


def shard_levels(key, extent, cuts, least, top_value):
    loudness, own = 1.0, jax.random.fold_in(key, 6)
    for axis_at, parts in cuts:
        draws = jnp.exp(jax.random.uniform(jax.random.fold_in(own, axis_at), (parts,), jnp.float32, least / len(cuts), top_value / len(cuts)))
        loudness = loudness * jnp.repeat(draws, extent[axis_at] // parts).reshape([-1 if axis == axis_at else 1 for axis in range(len(extent))])
    return loudness


def profile(count, total, most, skew):
    weights = [(1 << 20) // math.isqrt(rank ** skew) + 1 for rank in range(2, count + 1)]
    rest, given = total - most - (count - 1), [1] * (count - 1)
    while rest > 0:
        candidates = [i for i in range(count - 1) if given[i] < most]
        pool, budget = sum([weights[i] for i in candidates]), rest
        for i in candidates:
            extra = min(most - given[i], max(1, budget * weights[i] // pool), rest)
            given[i] = given[i] + extra
            rest = rest - extra
    return np.array([most] + given)


def ragged_sizes(key, amount, total, bound, lean):
    if amount == 2:
        one = jax.random.randint(key, (), max(1, total - bound), min(bound, total - 1) + 1)
        return jnp.stack([one, total - one])
    lengths = jnp.asarray(profile(amount, total, bound, lean), jnp.int32)
    twos = (amount - 1) // 2
    donor, sink = lengths[1:1 + 2 * twos:2], lengths[2:2 + 2 * twos:2]
    margin = jnp.minimum(donor - 1, bound - sink)
    shifted = jax.random.randint(jax.random.fold_in(key, 1), (twos,), 0, 1 << 20) % (margin + 1)
    lengths = lengths.at[1:1 + 2 * twos:2].set(donor - shifted).at[2:2 + 2 * twos:2].set(sink + shifted)
    return lengths[jax.random.permutation(jax.random.fold_in(key, 2), amount)]


def centred(own_key, dims, deviation, most, cuts=(), kind=jnp.bfloat16):
    array = jax.random.normal(own_key, dims, jnp.float32) * deviation
    if len(cuts) > 0:
        array = shard_levels(own_key, dims, cuts, -0.22, 0.18) * array
    return jnp.clip(array, min=-most, max=most).astype(kind)


def setup_inputs(seed: int = 0) -> dict:
    key_list = jax.random.split(jax.random.key(seed), 14)
    return {
        "q_nope": centred(key_list[0], (SAMPLES, 2, H * NOPE), 0.5, 3.0, ((0, 32), (2, 8))),
        "q_rope": draw_q_rope(jax.random.fold_in(key_list[13], 71), 0),
        "new_latent": centred(key_list[2], (SAMPLES, 2, LAT), 1.0, 4.0, ((0, 32),)),
        "new_rope": draw_new_rope(jax.random.fold_in(key_list[13], 71), 0),
        "prompt_latent": centred(key_list[4], (PROMPTS, PLEN, LAT), 1.0, 4.0, ((0, 32),)),
        "prompt_rope": draw_prompt_rope(jax.random.fold_in(key_list[13], 71), 0),
        "suffix_latent": centred(key_list[6], (SAMPLES, SUF, LAT), 1.0, 4.0, ((0, 32),)),
        "suffix_rope": draw_suffix_rope(jax.random.fold_in(key_list[13], 71), 0),
        "sample_prompt": draw_sample_prompt(jax.random.fold_in(key_list[13], 71), 0),
        "suffix_len": ragged_sizes(key_list[9], SAMPLES, SAMPLES * SUF // 2, SUF, 2).astype(jnp.int32),
        "w_uk": centred(key_list[10], (H, NOPE, LAT), NOPE ** -0.5, 0.5, ((0, 8),)),
        "w_uv": centred(key_list[11], (H, LAT, VDIM), (LAT // 16) ** -0.5, 1.0, ((0, 8),)),
        "w_out": centred(key_list[12], (H * VDIM, D), (H * VDIM // 4) ** -0.5, 0.109375, ((0, 8), (1, 4))),
    }


def reference(q_nope, q_rope, new_latent, new_rope, prompt_latent, prompt_rope, suffix_latent, suffix_rope, sample_prompt, suffix_len, w_uk, w_uv, w_out):
    score_scale = 1.0 / math.sqrt(NOPE + ROPE)
    queries_lat = jnp.einsum('sthn,hnl->sthl', q_nope.reshape(SAMPLES, 2, H, NOPE).astype(jnp.float32), w_uk.astype(jnp.float32)).astype(jnp.bfloat16).reshape(SAMPLES, 2 * H, LAT)
    queries_rope = q_rope.reshape(SAMPLES, 2 * H, ROPE)
    token_of = jnp.arange(2 * H, dtype=jnp.int32) // H
    new_valid = jnp.arange(2, dtype=jnp.int32)[None, :] <= token_of[:, None]
    suffix_pos = jnp.arange(SUF, dtype=jnp.int32)
    floor_value = -1e+30

    def one_sample(sample_index):
        lat_rows = queries_lat[sample_index]
        rope_rows = queries_rope[sample_index]
        owner_prompt = sample_prompt[sample_index]
        cache_latent = prompt_latent[owner_prompt]
        cache_rope = prompt_rope[owner_prompt]
        prefix_scores = (jnp.dot(lat_rows, cache_latent.T, preferred_element_type=jnp.float32) + jnp.dot(rope_rows, cache_rope, preferred_element_type=jnp.float32)) * score_scale
        prefix_peak = lax.optimization_barrier(jnp.max(prefix_scores, axis=-1))
        prefix_exp = jnp.exp(prefix_scores - prefix_peak[:, None])
        prefix_total = lax.optimization_barrier(jnp.sum(prefix_exp, axis=-1))
        prefix_out = jnp.dot(prefix_exp.astype(jnp.bfloat16), cache_latent, preferred_element_type=jnp.float32)
        own_latent = suffix_latent[sample_index]
        suffix_scores = (jnp.dot(lat_rows, own_latent.T, preferred_element_type=jnp.float32) + jnp.dot(rope_rows, suffix_rope[sample_index], preferred_element_type=jnp.float32)) * score_scale
        fresh_latent = new_latent[sample_index]
        new_scores = (jnp.dot(lat_rows, fresh_latent.T, preferred_element_type=jnp.float32) + jnp.dot(rope_rows, new_rope[sample_index].T, preferred_element_type=jnp.float32)) * score_scale
        suffix_valid = jnp.broadcast_to(suffix_pos[None, :] < suffix_len[sample_index], suffix_scores.shape)
        local_peak = jnp.maximum(lax.optimization_barrier(jnp.max(jnp.where(suffix_valid, suffix_scores, floor_value), axis=-1)), lax.optimization_barrier(jnp.max(jnp.where(new_valid, new_scores, floor_value), axis=-1)))
        suffix_exp = jnp.where(suffix_valid, jnp.exp(suffix_scores - local_peak[:, None]), 0.0)
        new_exp = jnp.where(new_valid, jnp.exp(new_scores - local_peak[:, None]), 0.0)
        local_total = lax.optimization_barrier(jnp.sum(suffix_exp, axis=-1)) + lax.optimization_barrier(jnp.sum(new_exp, axis=-1))
        local_out = jnp.dot(suffix_exp.astype(jnp.bfloat16), own_latent, preferred_element_type=jnp.float32) + jnp.dot(new_exp.astype(jnp.bfloat16), fresh_latent, preferred_element_type=jnp.float32)
        peak = jnp.maximum(prefix_peak, local_peak)
        prefix_factor = jnp.exp(prefix_peak - peak)
        local_factor = jnp.exp(local_peak - peak)
        merged = (prefix_factor[:, None] * prefix_out + local_factor[:, None] * local_out) / (prefix_factor * prefix_total + local_factor * local_total)[:, None]
        return merged.astype(jnp.bfloat16)
    attended = lax.map(one_sample, jnp.arange(SAMPLES, dtype=jnp.int32))
    values = jnp.einsum('sthl,hlv->sthv', attended.reshape(SAMPLES, 2, H, LAT).astype(jnp.float32), w_uv.astype(jnp.float32)).astype(jnp.bfloat16)
    layer_output = jnp.dot(values.reshape(SAMPLES * 2, H * VDIM), w_out, preferred_element_type=jnp.float32)
    return layer_output.astype(jnp.bfloat16).reshape(SAMPLES, 2, D)
```

```python
import functools
import math

import jax
import jax.numpy as jnp
from jax import lax
from jax.experimental import pallas as pl
from jax.experimental.pallas import tpu as pltpu
from jax.sharding import PartitionSpec as P

NOPE = 128
ROPE = 64
LAT = 512
VDIM = 128
F32 = jnp.float32
BF16 = jnp.bfloat16
MESH = pl.DeviceIdType.MESH
FLOOR = -1e30
SCALE = 1.0 / math.sqrt(NOPE + ROPE)
EXP2_SCALE = SCALE * math.log2(math.e)
CHUNKS = 2
NT = (((1,), (1,)), ((), ()))


def dot(left, right):
    return jnp.dot(left, right, preferred_element_type=F32)


def dot_nt(left, right):
    return lax.dot_general(left, right, NT, preferred_element_type=F32)


def put(ref, first, count, stride, value):
    for tile in range(ref.shape[0]):
        ref[tile, pl.ds(first, count, stride=stride), :] = value[:, 128 * tile : 128 * (tile + 1)]


def take(ref, first, count, stride):
    tiles = [ref[tile, pl.ds(first, count, stride=stride), :] for tile in range(ref.shape[0])]
    return jnp.concatenate(tiles, axis=1)


def whole(ref, rows=slice(None)):
    return jnp.concatenate([ref[tile, rows, :] for tile in range(ref.shape[0])], axis=1)


def fill(ref, value, rows=slice(None)):
    for tile in range(ref.shape[0]):
        ref[tile, rows, :] = value[:, 128 * tile : 128 * (tile + 1)]


def iota(shape, axis):
    return lax.broadcasted_iota(jnp.int32, shape, axis)


def kernel(
    sizes,
    sp_ref,
    len_ref,
    q_ref,
    r_ref,
    nl_ref,
    nr_ref,
    plat_hbm,
    prope_hbm,
    slat_hbm,
    srope_hbm,
    wuk_hbm,
    wuv_hbm,
    wout_hbm,
    out_ref,
    plat,
    prope,
    slat,
    srope,
    wuk,
    wuv,
    wout,
    tok,
    ntok,
    qf,
    qb,
    sb,
    rb,
    xf,
    lqf,
    lrf,
    lsc,
    lof,
    lvf,
    lse_col,
    plf,
    prf,
    sc,
    pb,
    pof,
    rvf,
    back,
    rr,
    cf,
    vg,
    lhs,
    part,
    blocks,
    sums,
    load_sem,
    q_send,
    q_recv,
    b_send,
    b_recv,
    v_send,
    v_recv,
    o_send,
    o_recv,
):
    nz, ny, nh = sizes
    slots = nz * ny
    samples = q_ref.shape[0]
    pairs = 2 * samples
    heads = wuk.shape[0]
    wide = 2 * heads
    z = lax.axis_index("prompt")
    y = lax.axis_index("sample")
    head = lax.axis_index("head")
    here = z * ny + y

    loads = [
        pltpu.make_async_copy(source, target, load_sem.at[index])
        for index, (source, target) in enumerate(
            (
                (wuk_hbm, wuk),
                (slat_hbm, slat),
                (srope_hbm, srope),
                (wuv_hbm, wuv),
                (plat_hbm.at[0], plat),
                (prope_hbm.at[0], prope),
                (wout_hbm, wout),
            )
        )
    ]
    for load in loads:
        load.start()
    load_wuk, load_slat, load_srope, load_wuv, load_plat, load_prope, load_wout = loads

    def ahead(k):
        step = k // ny
        half = (step + 1) // 2
        shift = jnp.where(step % 2 == 1, half, nz - half)
        return lax.rem(z + shift, nz), lax.rem(y + k % ny, ny)

    def behind(k):
        step = k // ny
        half = (step + 1) // 2
        shift = jnp.where(step % 2 == 1, nz - half, half)
        return lax.rem(z + shift, nz), lax.rem(y + ny - k % ny, ny)

    barrier = pltpu.get_barrier_semaphore()

    @pl.loop(1, slots)
    def _(k):
        to_z, to_y = ahead(k)
        pl.semaphore_signal(
            barrier, inc=1, device_id={"prompt": to_z, "sample": to_y}, device_id_type=MESH
        )

    @pl.loop(1, nh)
    def _(d):
        pl.semaphore_signal(
            barrier, inc=1, device_id={"head": lax.rem(head + d, nh)}, device_id_type=MESH
        )

    for s in range(samples):
        tok[2 * s : 2 * s + 2, :] = q_ref[s].astype(F32)
        ntok[2 * s : 2 * s + 2, :LAT] = nl_ref[s].astype(F32)
        ntok[2 * s : 2 * s + 2, LAT:] = jnp.zeros((2, NOPE), F32)
        ntok[2 * s : 2 * s + 2, LAT : LAT + ROPE] = nr_ref[s].astype(F32)
    for h in range(heads):
        qf[pl.ds(h, pairs, stride=wide), :] = tok[:, h * NOPE : (h + 1) * NOPE]
    for s in range(samples):
        tok[2 * s : 2 * s + 2, : heads * ROPE] = r_ref[s].astype(F32)
    low = iota((pairs, NOPE), 1) < ROPE
    for h in range(heads):
        both = tok[:, h // 2 * NOPE : (h // 2 + 1) * NOPE]
        if h % 2 == 1:
            both = pltpu.roll(both, ROPE, 1)
        rope_rows = jnp.where(low, both, 0.0)
        qf[pl.ds(heads + h, pairs, stride=wide), :] = rope_rows
        lrf[pl.ds(h, pairs, stride=16), :] = rope_rows
    for h in range(heads, 16):
        lrf[pl.ds(h, pairs, stride=16), :] = jnp.zeros((pairs, NOPE), F32)
        put(lqf, h, pairs, 16, jnp.zeros((pairs, LAT), F32))
    for s in range(samples):
        qb[s] = qf[2 * wide * s : 2 * wide * (s + 1), :].astype(BF16)

    pl.semaphore_wait(barrier, slots - 1 + nh - 1)

    def query_copy(k):
        to_z, to_y = ahead(k)
        return pltpu.make_async_remote_copy(
            src_ref=sb.at[k],
            dst_ref=rb.at[k],
            send_sem=q_send.at[k],
            recv_sem=q_recv.at[k],
            device_id={"prompt": to_z, "sample": to_y},
            device_id_type=MESH,
        )

    def sample_for(owner):
        found = 0
        for s in range(samples):
            found = jnp.where(sp_ref[s] == owner, s, found)
        return found

    rb[0] = qb[sample_for(here)]

    @pl.loop(1, slots)
    def _(k):
        to_z, to_y = ahead(k)
        sb[k] = qb[sample_for(to_z * ny + to_y)]
        query_copy(k).start()

    load_wuk.wait()
    for h in range(heads):
        rows = qf[pl.ds(h, pairs, stride=wide), :].astype(BF16)
        put(lqf, h, pairs, 16, dot(rows, wuk[h]))
    load_slat.wait()
    load_srope.wait()
    lane = iota((32, 128), 1)
    for s in range(samples):
        rows = slice(32 * s, 32 * s + 32)
        part_scores = dot_nt(whole(lqf, rows).astype(BF16), slat[s]) + dot(
            lrf[rows, :].astype(BF16)[:, :ROPE], srope[s]
        )
        lsc[rows, :] = jnp.where(lane < len_ref[s], part_scores, FLOOR)
    new_latent = ntok[:, :LAT].astype(BF16)
    new_rope = ntok[:, LAT:].astype(BF16)
    count = 16 * pairs
    new_scores = dot_nt(whole(lqf).astype(BF16), new_latent) + dot_nt(
        lrf[...].astype(BF16), new_rope
    )
    row, key = iota((count, pairs), 0), iota((count, pairs), 1)
    valid = ((key >> 1) == (row >> 5)) & ((key & 1) <= ((row >> 4) & 1))
    new_scores = jnp.where(valid, new_scores, FLOOR)
    old_scores = lsc[...]
    peak = jnp.maximum(
        jnp.max(old_scores, axis=1, keepdims=True), jnp.max(new_scores, axis=1, keepdims=True)
    )
    old_exp = jnp.exp2((old_scores - peak) * EXP2_SCALE)
    new_exp = jnp.exp2((new_scores - peak) * EXP2_SCALE)
    total = jnp.sum(old_exp, axis=1, keepdims=True) + jnp.sum(new_exp, axis=1, keepdims=True)
    lse_col[...] = jnp.broadcast_to(peak * SCALE + jnp.log(total), lse_col.shape)
    lsc[...] = old_exp
    new_out = dot(new_exp.astype(BF16), new_latent)
    inverse = 1.0 / total
    for s in range(samples):
        rows = slice(32 * s, 32 * s + 32)
        own_out = new_out[rows] + dot(lsc[rows, :].astype(BF16), slat[s])
        fill(lof, own_out * inverse[rows], rows)
    load_wuv.wait()
    for h in range(heads):
        rows = take(lof, h, pairs, 16).astype(BF16)
        lvf[pl.ds(h, pairs, stride=16), :] = dot(rows, wuv[h])
    for h in range(heads, 16):
        lvf[pl.ds(h, pairs, stride=16), :] = jnp.zeros((pairs, VDIM), F32)

    load_plat.wait()
    load_prope.wait()
    size = slots // CHUNKS
    duo = 2 * size
    rows_all = wide * size
    for h in range(heads, 16):
        rvf[pl.ds(h, duo, stride=16), :] = jnp.zeros((duo, VDIM), F32)

    def back_copy(k):
        to_z, to_y = behind(k)
        return pltpu.make_async_remote_copy(
            src_ref=back.at[k],
            dst_ref=rr.at[here],
            send_sem=b_send.at[k],
            recv_sem=b_recv.at[k],
            device_id={"prompt": to_z, "sample": to_y},
            device_id_type=MESH,
        )

    @pl.loop(0, CHUNKS)
    def _(chunk):
        base = chunk * size

        @pl.loop(0, size)
        def _(i):
            @pl.when(base + i > 0)
            def _():
                query_copy(base + i).wait_recv()

        xf[...] = rb[pl.ds(base, size)].astype(F32).reshape(xf.shape)
        for h in range(heads):
            rows = xf[pl.ds(h, duo, stride=wide), :].astype(BF16)
            put(plf, h, duo, heads, dot(rows, wuk[h]))
            prf[pl.ds(h, duo, stride=heads), :] = xf[pl.ds(heads + h, duo, stride=wide), :]
        lat_rows = whole(plf).astype(BF16)
        rope_rows = prf[...].astype(BF16)[:, :ROPE]
        length = plat.shape[0]
        tile = min(512, length)
        peak = None
        for at in range(0, length, tile):
            scores = dot_nt(lat_rows, plat[at : at + tile, :]) + dot(
                rope_rows, prope[:, at : at + tile]
            )
            sc[:, at : at + tile] = scores
            top = jnp.max(scores, axis=1, keepdims=True)
            peak = top if peak is None else jnp.maximum(peak, top)
        total = jnp.zeros_like(peak)
        for at in range(0, length, tile):
            probs = jnp.exp2((sc[:, at : at + tile] - peak) * EXP2_SCALE)
            total = total + jnp.sum(probs, axis=1, keepdims=True)
            pb[:, at : at + tile] = probs.astype(BF16)
        fill(pof, dot(pb[...], plat[...]) * (1.0 / total))
        for h in range(heads):
            rows = take(pof, h, duo, heads).astype(BF16)
            rvf[pl.ds(h, duo, stride=16), :] = dot(rows, wuv[h])
        lse = peak * SCALE + jnp.log(total)
        first = lse.astype(BF16).astype(F32)
        second = (lse - first).astype(BF16).astype(F32)
        third = lse - first - second
        row, lane = iota((rows_all, 128), 0), iota((rows_all, 128), 1)
        place = row - heads * ((row * 43691) >> 19)
        spread = (
            jnp.where(lane == place, first, 0.0)
            + jnp.where(lane == place + 16, second, 0.0)
            + jnp.where(lane == place + 32, third, 0.0)
        ).astype(BF16)
        at, of = iota((duo, rows_all), 0) * heads, iota((duo, rows_all), 1)
        pick = jnp.where((of >= at) & (of < at + heads), 1.0, 0.0).astype(BF16)
        rvf[pl.ds(heads, duo, stride=16), :] = dot(pick, spread)
        back[pl.ds(base, size)] = rvf[...].reshape(size, 32, VDIM).astype(BF16)

        @pl.loop(0, size)
        def _(i):
            @pl.when(base + i > 0)
            def _():
                back_copy(base + i).start()

    rr[here] = back[0]

    @pl.loop(1, slots)
    def _(k):
        back_copy(k).wait_recv()

    for s in range(samples):
        cf[32 * s : 32 * s + 32, :] = rr[sp_ref[s]].astype(F32)
    row, lane = iota((16, 128), 0), iota((16, 128), 1)
    mine = (lane == row) | (lane == row + 16) | (lane == row + 32)
    for pair in range(pairs):
        rows = slice(16 * pair, 16 * pair + 16)
        stat = jnp.broadcast_to(cf[16 * pair + heads : 16 * pair + heads + 1, :], (16, 128))
        lse_prompt = jnp.sum(jnp.where(mine, stat, 0.0), axis=1, keepdims=True)
        lse_local = lse_col[rows, :]
        top = jnp.maximum(lse_prompt, lse_local)
        weight_prompt = jnp.exp(lse_prompt - top)
        weight_local = jnp.exp(lse_local - top)
        lvf[rows, :] = (weight_prompt * cf[rows, :] + weight_local * lvf[rows, :]) / (
            weight_prompt + weight_local
        )
    half = heads // 2
    columns = [
        jnp.concatenate(
            [lvf[pl.ds(h, pairs, stride=16), :], lvf[pl.ds(h + half, pairs, stride=16), :]], axis=0
        )
        for h in range(half)
    ]
    vg[y] = jnp.concatenate(columns, axis=1).astype(BF16)

    def value_copy(d):
        return pltpu.make_async_remote_copy(
            src_ref=vg.at[y],
            dst_ref=vg.at[y],
            send_sem=v_send.at[d],
            recv_sem=v_recv.at[d],
            device_id={"sample": lax.rem(y + d, ny)},
            device_id_type=MESH,
        )

    for d in range(1, ny):
        value_copy(d).start()
    load_wout.wait()
    for d in range(1, ny):
        value_copy(d).wait_recv()

    for d in range(ny):
        gathered = vg[d].astype(F32)
        lhs[pairs * d : pairs * (d + 1), : half * VDIM] = gathered[:pairs]
        lhs[pairs * d : pairs * (d + 1), half * VDIM :] = gathered[pairs:]
    left = lhs[...].astype(BF16)
    columns_all = wout.shape[1]
    width = columns_all // nh

    def sum_copy(j):
        return pltpu.make_async_remote_copy(
            src_ref=blocks.at[j],
            dst_ref=sums.at[head],
            send_sem=o_send.at[j],
            recv_sem=o_recv.at[head],
            device_id={"head": j},
            device_id_type=MESH,
        )

    done = 0
    tile = 256
    for at in range(0, columns_all, tile):
        stop = min(at + tile, columns_all)
        part[:, at:stop] = dot(left, wout[:, at:stop])
        while done < nh and (done + 1) * width <= stop:
            start = done * width
            floor = start // 128 * 128
            ceil = -(-(start + width) // 128) * 128
            block = part[:, floor:ceil]
            if start > floor:
                block = pltpu.roll(block, ceil - start, 1)
            blocks[done] = block[:, :width].astype(BF16)

            @pl.when(head != done)
            def _(j=done):
                sum_copy(j).start()

            done += 1
    result = blocks[head].astype(F32)
    for d in range(1, nh):
        source = lax.rem(head + d, nh)
        pltpu.make_async_remote_copy(
            src_ref=blocks.at[source],
            dst_ref=sums.at[source],
            send_sem=o_send.at[source],
            recv_sem=o_recv.at[source],
            device_id={"head": source},
            device_id_type=MESH,
        ).wait_recv()
        result = result + sums[source].astype(F32)
    out_ref[...] = result.astype(BF16)

    @pl.loop(1, slots)
    def _(k):
        query_copy(k).wait_send()
        back_copy(k).wait_send()

    for d in range(1, ny):
        value_copy(d).wait_send()

    @pl.loop(1, nh)
    def _(d):
        sum_copy(lax.rem(head + d, nh)).wait_send()


def shards(
    q_nope,
    q_rope,
    new_latent,
    new_rope,
    prompt_latent,
    prompt_rope,
    suffix_latent,
    suffix_rope,
    sample_prompt,
    suffix_len,
    w_uk,
    w_uv,
    w_out,
):
    nz, ny, nh = (lax.axis_size(name) for name in ("prompt", "sample", "head"))
    slots = nz * ny
    samples = q_nope.shape[0]
    pairs = 2 * samples
    heads = w_uk.shape[0]
    length = prompt_latent.shape[1]
    width = w_out.shape[1] // nh
    size = slots // CHUNKS
    duo = 2 * size
    rows_all = 2 * heads * size
    count = 16 * pairs
    vmem = pltpu.VMEM
    dma = pltpu.SemaphoreType.DMA
    in_vmem = pl.BlockSpec(memory_space=pltpu.VMEM)
    in_smem = pl.BlockSpec(memory_space=pltpu.SMEM)
    in_hbm = pl.BlockSpec(memory_space=pl.ANY)
    result = pl.pallas_call(
        functools.partial(kernel, (nz, ny, nh)),
        out_shape=jax.ShapeDtypeStruct((pairs * ny, width), BF16),
        in_specs=[in_smem] * 2 + [in_vmem] * 4 + [in_hbm] * 7,
        out_specs=in_vmem,
        scratch_shapes=[
            vmem(prompt_latent.shape[1:], BF16),
            vmem(prompt_rope.shape[1:], BF16),
            vmem(suffix_latent.shape, BF16),
            vmem(suffix_rope.shape, BF16),
            vmem(w_uk.shape, BF16),
            vmem(w_uv.shape, BF16),
            vmem(w_out.shape, BF16),
            vmem((pairs, heads * NOPE), F32),
            vmem((pairs, LAT + NOPE), F32),
            vmem((pairs * 2 * heads, NOPE), F32),
            vmem((samples, 4 * heads, NOPE), BF16),
            vmem((slots, 4 * heads, NOPE), BF16),
            vmem((slots, 4 * heads, NOPE), BF16),
            vmem((size * 4 * heads, NOPE), F32),
            vmem((LAT // 128, count, 128), F32),
            vmem((count, NOPE), F32),
            vmem((count, suffix_latent.shape[1]), F32),
            vmem((LAT // 128, count, 128), F32),
            vmem((count, VDIM), F32),
            vmem((count, VDIM), F32),
            vmem((LAT // 128, rows_all, 128), F32),
            vmem((rows_all, NOPE), F32),
            vmem((rows_all, length), F32),
            vmem((rows_all, length), BF16),
            vmem((LAT // 128, rows_all, 128), F32),
            vmem((16 * duo, VDIM), F32),
            vmem((slots, 32, VDIM), BF16),
            vmem((slots, 32, VDIM), BF16),
            vmem((count, VDIM), F32),
            vmem((ny, 2 * pairs, heads * VDIM // 2), BF16),
            vmem((ny * pairs, heads * VDIM), F32),
            vmem((ny * pairs, w_out.shape[1]), F32),
            vmem((nh, ny * pairs, width), BF16),
            vmem((nh, ny * pairs, width), BF16),
            dma((7,)),
            dma((slots,)),
            dma((slots,)),
            dma((slots,)),
            dma((slots,)),
            dma((ny,)),
            dma((ny,)),
            dma((nh,)),
            dma((nh,)),
        ],
        compiler_params=pltpu.CompilerParams(
            collective_id=0, has_side_effects=True, vmem_limit_bytes=56 * 1024 * 1024
        ),
        cost_estimate=pl.CostEstimate(
            flops=5 * 10**9, bytes_accessed=13 * 10**6, transcendentals=2 * 10**6
        ),
    )(
        sample_prompt,
        suffix_len,
        q_nope,
        q_rope,
        new_latent,
        new_rope,
        prompt_latent,
        prompt_rope,
        suffix_latent,
        suffix_rope,
        w_uk,
        w_uv,
        w_out,
    )
    return result.reshape(ny * samples, 2, width)


def solution(mesh):
    placed = (
        P(("prompt", "sample"), None, "head"),
        P(("prompt", "sample"), None, "head"),
        P(("prompt", "sample"), None, None),
        P(("prompt", "sample"), None, None),
        P(("prompt", "sample"), None, None),
        P(("prompt", "sample"), None, None),
        P(("prompt", "sample"), None, None),
        P(("prompt", "sample"), None, None),
        P(("prompt", "sample")),
        P(("prompt", "sample")),
        P("head", None, None),
        P("head", None, None),
        P("head", "sample"),
    )
    return jax.shard_map(
        shards,
        mesh=mesh,
        in_specs=placed,
        out_specs=P("prompt", None, ("sample", "head")),
        check_vma=False,
    )
```

```python
import functools
import math

import jax
import jax.numpy as jnp
from jax import lax
from jax.experimental import pallas as pl
from jax.experimental.pallas import tpu as pltpu
from jax.sharding import PartitionSpec as P

NOPE = 128
ROPE = 64
LAT = 512
VDIM = 128
F32 = jnp.float32
BF16 = jnp.bfloat16
MESH = pl.DeviceIdType.MESH
FLOOR = -1e30
SCALE = 1.0 / math.sqrt(NOPE + ROPE)
EXP2_SCALE = SCALE * math.log2(math.e)
MOST = 16
NT = (((1,), (1,)), ((), ()))


def dot(left, right):
    return jnp.dot(left, right, preferred_element_type=F32)


def dot_nt(left, right):
    return lax.dot_general(left, right, NT, preferred_element_type=F32)


def put(ref, first, count, stride, value):
    for tile in range(ref.shape[0]):
        ref[tile, pl.ds(first, count, stride=stride), :] = value[:, 128 * tile : 128 * (tile + 1)]


def take(ref, first, count, stride):
    tiles = [ref[tile, pl.ds(first, count, stride=stride), :] for tile in range(ref.shape[0])]
    return jnp.concatenate(tiles, axis=1)


def whole(ref, rows=slice(None)):
    return jnp.concatenate([ref[tile, rows, :] for tile in range(ref.shape[0])], axis=1)


def fill(ref, value, rows=slice(None)):
    for tile in range(ref.shape[0]):
        ref[tile, rows, :] = value[:, 128 * tile : 128 * (tile + 1)]


def iota(shape, axis):
    return lax.broadcasted_iota(jnp.int32, shape, axis)


def kernel(
    sizes,
    sp_ref,
    len_ref,
    q_ref,
    r_ref,
    nl_ref,
    nr_ref,
    plat_hbm,
    prope_hbm,
    slat_hbm,
    srope_hbm,
    wuk_hbm,
    wuv_hbm,
    wout_hbm,
    out_ref,
    plat,
    prope,
    slat,
    srope,
    wuk,
    wuv,
    wout,
    tok,
    ntok,
    qf,
    qb,
    sb,
    rb,
    xf,
    lqf,
    lrf,
    lsc,
    lof,
    lvf,
    lse_col,
    plf,
    prf,
    sc,
    pb,
    pof,
    rvf,
    back,
    rr0,
    rr1,
    cf,
    vg,
    lhs,
    part,
    blocks,
    sums,
    final,
    load_sem,
    q_send,
    q_recv,
    b_send,
    b_recv,
    v_send,
    v_recv,
    o_send,
    o_recv,
):
    nz, ny, nh = sizes
    slots = nz * ny
    samples = q_ref.shape[0]
    pairs = 2 * samples
    heads = wuk.shape[0]
    half = heads // 2
    wide = 2 * heads
    spots = 2 * slots
    used = 2 * min(MOST, slots)
    z = lax.axis_index("prompt")
    y = lax.axis_index("sample")
    head = lax.axis_index("head")
    here = z * ny + y
    z_at = [lax.rem(z + d, nz) for d in range(nz)]
    y_at = [lax.rem(y + d, ny) for d in range(ny)]
    head_at = [lax.rem(head + d, nh) for d in range(nh)]

    def ahead(k):
        step = k // ny
        away = (step + 1) // 2
        return z_at[away if step % 2 == 1 else (nz - away) % nz], y_at[k % ny]

    def behind(k):
        step = k // ny
        away = (step + 1) // 2
        return z_at[(nz - away) % nz if step % 2 == 1 else away], y_at[(ny - k % ny) % ny]

    barrier = pltpu.get_barrier_semaphore()
    for k in range(1, slots):
        to_z, to_y = ahead(k)
        pl.semaphore_signal(
            barrier, inc=1, device_id={"prompt": to_z, "sample": to_y}, device_id_type=MESH
        )
    for d in range(1, nh):
        pl.semaphore_signal(
            barrier, inc=1, device_id={"head": head_at[d]}, device_id_type=MESH
        )

    loads = [
        pltpu.make_async_copy(source, target, load_sem.at[index])
        for index, (source, target) in enumerate(
            (
                (wuk_hbm, wuk),
                (slat_hbm, slat),
                (srope_hbm, srope),
                (wuv_hbm, wuv),
                (plat_hbm.at[0], plat),
                (prope_hbm.at[0], prope),
                (wout_hbm, wout),
            )
        )
    ]
    for load in loads:
        load.start()
    load_wuk, load_slat, load_srope, load_wuv, load_plat, load_prope, load_wout = loads

    for s in range(samples):
        tok[2 * s : 2 * s + 2, :] = q_ref[s].astype(F32)
    for h in range(heads):
        qf[pl.ds(h, pairs, stride=wide), :] = tok[:, h * NOPE : (h + 1) * NOPE]
    for s in range(samples):
        tok[2 * s : 2 * s + 2, : heads * ROPE] = r_ref[s].astype(F32)
    low = iota((pairs, NOPE), 1) < ROPE
    for h in range(heads):
        both = tok[:, h // 2 * NOPE : (h // 2 + 1) * NOPE]
        if h % 2 == 1:
            both = pltpu.roll(both, ROPE, 1)
        qf[pl.ds(heads + h, pairs, stride=wide), :] = jnp.where(low, both, 1.0)
    for s in range(samples):
        qb[s] = qf[2 * wide * s : 2 * wide * (s + 1), :].astype(BF16)
    qb[samples] = jnp.zeros(qb.shape[1:], BF16)

    pl.semaphore_wait(barrier, slots - 1 + nh - 1)

    def query_copy(k):
        to_z, to_y = ahead(k)
        return pltpu.make_async_remote_copy(
            src_ref=sb.at[k],
            dst_ref=rb.at[k],
            send_sem=q_send.at[k],
            recv_sem=q_recv.at[k],
            device_id={"prompt": to_z, "sample": to_y},
            device_id_type=MESH,
        )

    names = [sp_ref[s] for s in range(samples)]

    def sample_for(owner):
        found = samples
        for s in range(samples):
            found = jnp.where(names[s] == owner, s, found)
        return found

    for k in range(1, slots):
        to_z, to_y = ahead(k)
        sb[k] = qb[sample_for(to_z * ny + to_y)]
        query_copy(k).start()
    rb[0] = qb[sample_for(here)]

    side = 8 * pairs
    for s in range(samples):
        ntok[2 * s : 2 * s + 2, :LAT] = nl_ref[s].astype(F32)
        ntok[2 * s : 2 * s + 2, LAT:] = jnp.zeros((2, NOPE), F32)
        ntok[2 * s : 2 * s + 2, LAT : LAT + ROPE] = nr_ref[s].astype(F32)
    for g in range(2):
        for h in range(half, 8):
            lrf[pl.ds(g * side + h, pairs, stride=8), :] = jnp.zeros((pairs, NOPE), F32)
            put(lqf, g * side + h, pairs, 8, jnp.zeros((pairs, LAT), F32))
    load_wuk.wait()
    for g in range(2):
        for h in range(half):
            rows = qf[pl.ds(g * half + h, pairs, stride=wide), :].astype(BF16)
            put(lqf, g * side + h, pairs, 8, dot(rows, wuk[g * half + h]))
            rope_rows = qf[pl.ds(heads + g * half + h, pairs, stride=wide), :]
            lrf[pl.ds(g * side + h, pairs, stride=8), :] = jnp.where(low, rope_rows, 0.0)
    load_slat.wait()
    load_srope.wait()
    lane = iota((32, 128), 1)
    spans = [(slice(16 * s, 16 * s + 16), slice(side + 16 * s, side + 16 * s + 16)) for s in range(samples)]
    for s, (top, bottom) in enumerate(spans):
        lat_rows = jnp.concatenate([whole(lqf, top), whole(lqf, bottom)], axis=0).astype(BF16)
        rope_rows = jnp.concatenate([lrf[top, :], lrf[bottom, :]], axis=0).astype(BF16)[:, :ROPE]
        scores = dot_nt(lat_rows, slat[s]) + dot(rope_rows, srope[s])
        scores = jnp.where(lane < len_ref[s], scores, FLOOR)
        lsc[top, :] = scores[:16]
        lsc[bottom, :] = scores[16:]
    new_latent = ntok[:, :LAT].astype(BF16)
    new_rope = ntok[:, LAT:].astype(BF16)
    count = 2 * side
    new_scores = dot_nt(whole(lqf).astype(BF16), new_latent) + dot_nt(
        lrf[...].astype(BF16), new_rope
    )
    row, key = iota((count, pairs), 0), iota((count, pairs), 1)
    row = jnp.where(row >= side, row - side, row)
    valid = ((key >> 1) == (row >> 4)) & ((key & 1) <= ((row >> 3) & 1))
    new_scores = jnp.where(valid, new_scores, FLOOR)
    old_scores = lsc[...]
    peak = jnp.maximum(
        jnp.max(old_scores, axis=1, keepdims=True), jnp.max(new_scores, axis=1, keepdims=True)
    )
    old_exp = jnp.exp2((old_scores - peak) * EXP2_SCALE)
    new_exp = jnp.exp2((new_scores - peak) * EXP2_SCALE)
    total = jnp.sum(old_exp, axis=1, keepdims=True) + jnp.sum(new_exp, axis=1, keepdims=True)
    lse_col[...] = jnp.broadcast_to(peak * SCALE + jnp.log(total), lse_col.shape)
    lsc[...] = old_exp
    new_out = dot(new_exp.astype(BF16), new_latent)
    inverse = 1.0 / total
    for s, (top, bottom) in enumerate(spans):
        probs = jnp.concatenate([lsc[top, :], lsc[bottom, :]], axis=0).astype(BF16)
        own_out = dot(probs, slat[s])
        fill(lof, (new_out[top] + own_out[:16]) * inverse[top], top)
        fill(lof, (new_out[bottom] + own_out[16:]) * inverse[bottom], bottom)
    load_wuv.wait()
    for g in range(2):
        for h in range(half):
            rows = take(lof, g * side + h, pairs, 8).astype(BF16)
            lvf[pl.ds(g * side + h, pairs, stride=8), :] = dot(rows, wuv[g * half + h])
        for h in range(half, 8):
            lvf[pl.ds(g * side + h, pairs, stride=8), :] = jnp.zeros((pairs, VDIM), F32)
            rvf[g, pl.ds(h, spots, stride=8), :] = jnp.zeros((spots, VDIM), F32)

    def back_copy(g, k):
        to_z, to_y = behind(k)
        return pltpu.make_async_remote_copy(
            src_ref=back.at[g, k],
            dst_ref=(rr0, rr1)[g].at[here],
            send_sem=b_send.at[g, k],
            recv_sem=b_recv.at[g, k],
            device_id={"prompt": to_z, "sample": to_y},
            device_id_type=MESH,
        )

    load_plat.wait()
    load_prope.wait()
    for k in range(1, slots):
        query_copy(k).wait_recv()
    xf[...] = rb[...].astype(F32).reshape(xf.shape)
    flags = pltpu.roll(xf[pl.ds(heads, spots, stride=wide), :], ROPE, 1)
    down, across = iota((spots, spots), 0), iota((spots, spots), 1)
    before = jnp.where(((across & 1) == 0) & ((across >> 1) < (down >> 1)), 1.0, 0.0)
    rank_down = dot(before.astype(BF16), flags.astype(BF16))[:, :used]
    down, across = iota((spots, used), 0), iota((spots, used), 1)
    unpick = jnp.where(
        (flags[:, :used] > 0.5)
        & (rank_down == (across >> 1).astype(F32))
        & ((across & 1) == (down & 1)),
        1.0,
        0.0,
    ).astype(BF16)
    down, across = iota((spots, spots), 0), iota((spots, spots), 1)
    after = ((down & 1) == 0) & ((down >> 1) < (across >> 1))
    square = flags[:, :spots]
    ones = jnp.ones((used, spots), BF16)
    rank_across = dot(ones, jnp.where(after, square, 0.0).astype(BF16))
    flag_across = dot(ones, jnp.where(down == across, square, 0.0).astype(BF16))
    down, across = iota((used, spots), 0), iota((used, spots), 1)
    pick = jnp.where(
        (flag_across > 0.5)
        & (rank_across == (down >> 1).astype(F32))
        & ((across & 1) == (down & 1)),
        1.0,
        0.0,
    ).astype(BF16)
    rows_all = used * half
    down, across = iota((used, rows_all), 0) * half, iota((used, rows_all), 1)
    gather_rows = jnp.where((across >= down) & (across < down + half), 1.0, 0.0).astype(BF16)
    stat_pick = dot(unpick, gather_rows).astype(BF16)
    length = plat.shape[0]
    tile = min(512, length)
    for g in range(2):
        for h in range(half):
            at = g * half + h
            both = jnp.concatenate(
                [
                    xf[pl.ds(at, spots, stride=wide), :],
                    xf[pl.ds(heads + at, spots, stride=wide), :],
                ],
                axis=1,
            ).astype(BF16)
            both = dot(pick, both)
            put(plf.at[g], h, used, half, dot(both[:, :NOPE].astype(BF16), wuk[at]))
            prf[g, pl.ds(h, used, stride=half), :] = both[:, NOPE:]
        lat_rows = whole(plf.at[g]).astype(BF16)
        rope_rows = prf[g].astype(BF16)[:, :ROPE]
        top = None
        for at in range(0, length, tile):
            scores = dot_nt(lat_rows, plat[at : at + tile, :]) + dot(
                rope_rows, prope[:, at : at + tile]
            )
            sc[g, :, at : at + tile] = scores
            for lanes in range(0, tile, 128):
                piece = scores[:, lanes : lanes + 128]
                top = piece if top is None else jnp.maximum(top, piece)
        peak = jnp.max(top, axis=1, keepdims=True)
        sums_of = jnp.zeros((rows_all, 128), F32)
        for at in range(0, length, tile):
            probs = jnp.exp2((sc[g, :, at : at + tile] - peak) * EXP2_SCALE)
            for lanes in range(0, tile, 128):
                sums_of = sums_of + probs[:, lanes : lanes + 128]
            pb[g, :, at : at + tile] = probs.astype(BF16)
        total = jnp.sum(sums_of, axis=1, keepdims=True)
        fill(pof.at[g], dot(pb[g], plat[...]) * (1.0 / total))
        for h in range(half):
            rows = take(pof.at[g], h, used, half).astype(BF16)
            head_values = dot(rows, wuv[g * half + h]).astype(BF16)
            rvf[g, pl.ds(h, spots, stride=8), :] = dot(unpick, head_values)
        lse = peak * SCALE + jnp.log(total)
        first = lse.astype(BF16).astype(F32)
        second = (lse - first).astype(BF16).astype(F32)
        third = lse - first - second
        row, lane = iota((rows_all, 128), 0), iota((rows_all, 128), 1)
        place = row - half * ((row * 43691) >> 18)
        spread = (
            jnp.where(lane == place, first, 0.0)
            + jnp.where(lane == place + 16, second, 0.0)
            + jnp.where(lane == place + 32, third, 0.0)
        ).astype(BF16)
        rvf[g, pl.ds(half, spots, stride=8), :] = dot(stat_pick, spread)
        back[g] = rvf[g].reshape(slots, 16, VDIM).astype(BF16)
        for k in range(1, slots):
            back_copy(g, k).start()
        (rr0, rr1)[g][here] = back[g, 0]

    def value_copy(g, d):
        return pltpu.make_async_remote_copy(
            src_ref=vg.at[g, y],
            dst_ref=vg.at[g, y],
            send_sem=v_send.at[g, d],
            recv_sem=v_recv.at[g, d],
            device_id={"sample": y_at[d]},
            device_id_type=MESH,
        )

    third_of = half // 2
    row, lane = iota((8, 128), 0), iota((8, 128), 1)
    mine = (lane == row) | (lane == row + 16) | (lane == row + 32)
    for g in range(2):
        for k in range(1, slots):
            back_copy(g, k).wait_recv()
        for s in range(samples):
            cf[16 * s : 16 * s + 16, :] = (rr0, rr1)[g][names[s]].astype(F32)
        for pair in range(pairs):
            rows = slice(8 * pair, 8 * pair + 8)
            local_rows = slice(g * side + 8 * pair, g * side + 8 * pair + 8)
            stat = jnp.broadcast_to(cf[8 * pair + half : 8 * pair + half + 1, :], (8, 128))
            lse_prompt = jnp.sum(jnp.where(mine, stat, 0.0), axis=1, keepdims=True)
            lse_local = lse_col[local_rows, :]
            top = jnp.maximum(lse_prompt, lse_local)
            weight_prompt = jnp.exp(lse_prompt - top)
            weight_local = jnp.exp(lse_local - top)
            lvf[local_rows, :] = (
                weight_prompt * cf[rows, :] + weight_local * lvf[local_rows, :]
            ) / (weight_prompt + weight_local)
        columns = [
            jnp.concatenate(
                [
                    lvf[pl.ds(g * side + h, pairs, stride=8), :],
                    lvf[pl.ds(g * side + h + third_of, pairs, stride=8), :],
                ],
                axis=0,
            )
            for h in range(third_of)
        ]
        vg[g, y] = jnp.concatenate(columns, axis=1).astype(BF16)
        for d in range(1, ny):
            value_copy(g, d).start()

    def sum_copy(j):
        return pltpu.make_async_remote_copy(
            src_ref=blocks.at[j],
            dst_ref=sums.at[head],
            send_sem=o_send.at[j],
            recv_sem=o_recv.at[head],
            device_id={"head": j},
            device_id_type=MESH,
        )

    for k in range(1, slots):
        query_copy(k).wait_send()
    load_wout.wait()
    columns_all = wout.shape[1]
    width = columns_all // nh
    inner = half * VDIM
    done = 0
    tile = 256
    for g in range(2):
        for d in range(1, ny):
            value_copy(g, d).wait_recv()
        for d in range(ny):
            gathered = vg[g, d].astype(F32)
            lhs[pairs * d : pairs * (d + 1), : inner // 2] = gathered[:pairs]
            lhs[pairs * d : pairs * (d + 1), inner // 2 :] = gathered[pairs:]
        left = lhs[...].astype(BF16)
        for at in range(0, columns_all, tile):
            stop = min(at + tile, columns_all)
            product = dot(left, wout[g * inner : (g + 1) * inner, at:stop])
            if g == 0:
                part[:, at:stop] = product
                continue
            part[:, at:stop] = part[:, at:stop] + product
            while done < nh and (done + 1) * width <= stop:
                start = done * width
                floor = start // 128 * 128
                ceil = min(-(-(start + width) // 128) * 128, columns_all)
                block = part[:, floor:ceil]
                if start > floor:
                    block = pltpu.roll(block, ceil - start, 1)
                blocks[done] = block[:, :width].astype(BF16)

                @pl.when(head != done)
                def _(j=done):
                    sum_copy(j).start()

                done += 1

    for g in range(2):
        for k in range(1, slots):
            back_copy(g, k).wait_send()
        for d in range(1, ny):
            value_copy(g, d).wait_send()
    result = blocks[head].astype(F32)
    for d in range(1, nh):
        source = head_at[d]
        pltpu.make_async_remote_copy(
            src_ref=blocks.at[source],
            dst_ref=sums.at[source],
            send_sem=o_send.at[source],
            recv_sem=o_recv.at[source],
            device_id={"head": source},
            device_id_type=MESH,
        ).wait_recv()
        result = result + sums[source].astype(F32)
    final[...] = result
    for row in range(ny * samples):
        out_ref[row] = final[2 * row : 2 * row + 2, :].astype(BF16)
    for d in range(1, nh):
        sum_copy(head_at[d]).wait_send()


def shards(
    q_nope,
    q_rope,
    new_latent,
    new_rope,
    prompt_latent,
    prompt_rope,
    suffix_latent,
    suffix_rope,
    sample_prompt,
    suffix_len,
    w_uk,
    w_uv,
    w_out,
):
    nz, ny, nh = (lax.axis_size(name) for name in ("prompt", "sample", "head"))
    slots = nz * ny
    samples = q_nope.shape[0]
    pairs = 2 * samples
    heads = w_uk.shape[0]
    length = prompt_latent.shape[1]
    width = w_out.shape[1] // nh
    half = heads // 2
    used = 2 * min(MOST, slots)
    rows_all = used * half
    count = 16 * pairs
    vmem = pltpu.VMEM
    dma = pltpu.SemaphoreType.DMA
    in_vmem = pl.BlockSpec(memory_space=pltpu.VMEM)
    in_smem = pl.BlockSpec(memory_space=pltpu.SMEM)
    in_hbm = pl.BlockSpec(memory_space=pl.ANY)
    return pl.pallas_call(
        functools.partial(kernel, (nz, ny, nh)),
        out_shape=jax.ShapeDtypeStruct((samples * ny, 2, width), BF16),
        in_specs=[in_smem] * 2 + [in_vmem] * 4 + [in_hbm] * 7,
        out_specs=in_vmem,
        scratch_shapes=[
            vmem(prompt_latent.shape[1:], BF16),
            vmem(prompt_rope.shape[1:], BF16),
            vmem(suffix_latent.shape, BF16),
            vmem(suffix_rope.shape, BF16),
            vmem(w_uk.shape, BF16),
            vmem(w_uv.shape, BF16),
            vmem(w_out.shape, BF16),
            vmem((pairs, heads * NOPE), F32),
            vmem((pairs, LAT + NOPE), F32),
            vmem((pairs * 2 * heads, NOPE), F32),
            vmem((samples + 1, 4 * heads, NOPE), BF16),
            vmem((slots, 4 * heads, NOPE), BF16),
            vmem((slots, 4 * heads, NOPE), BF16),
            vmem((slots * 4 * heads, NOPE), F32),
            vmem((LAT // 128, count, 128), F32),
            vmem((count, NOPE), F32),
            vmem((count, suffix_latent.shape[1]), F32),
            vmem((LAT // 128, count, 128), F32),
            vmem((count, VDIM), F32),
            vmem((count, VDIM), F32),
            vmem((2, LAT // 128, rows_all, 128), F32),
            vmem((2, rows_all, NOPE), F32),
            vmem((2, rows_all, length), F32),
            vmem((2, rows_all, length), BF16),
            vmem((2, LAT // 128, rows_all, 128), F32),
            vmem((2, 16 * slots, VDIM), F32),
            vmem((2, slots, 16, VDIM), BF16),
            vmem((slots, 16, VDIM), BF16),
            vmem((slots, 16, VDIM), BF16),
            vmem((8 * pairs, VDIM), F32),
            vmem((2, ny, 2 * pairs, half * VDIM // 2), BF16),
            vmem((ny * pairs, half * VDIM), F32),
            vmem((ny * pairs, w_out.shape[1]), F32),
            vmem((nh, ny * pairs, width), BF16),
            vmem((nh, ny * pairs, width), BF16),
            vmem((ny * pairs, width), F32),
            dma((7,)),
            dma((slots,)),
            dma((slots,)),
            dma((2, slots)),
            dma((2, slots)),
            dma((2, ny)),
            dma((2, ny)),
            dma((nh,)),
            dma((nh,)),
        ],
        compiler_params=pltpu.CompilerParams(
            collective_id=0, has_side_effects=True, vmem_limit_bytes=56 * 1024 * 1024
        ),
        cost_estimate=pl.CostEstimate(
            flops=5 * 10**9, bytes_accessed=13 * 10**6, transcendentals=2 * 10**6
        ),
    )(
        sample_prompt,
        suffix_len,
        q_nope,
        q_rope,
        new_latent,
        new_rope,
        prompt_latent,
        prompt_rope,
        suffix_latent,
        suffix_rope,
        w_uk,
        w_uv,
        w_out,
    )


def solution(mesh):
    placed = (
        P(("prompt", "sample"), None, "head"),
        P(("prompt", "sample"), None, "head"),
        P(("prompt", "sample"), None, None),
        P(("prompt", "sample"), None, None),
        P(("prompt", "sample"), None, None),
        P(("prompt", "sample"), None, None),
        P(("prompt", "sample"), None, None),
        P(("prompt", "sample"), None, None),
        P(("prompt", "sample")),
        P(("prompt", "sample")),
        P("head", None, None),
        P("head", None, None),
        P("head", "sample"),
    )
    return jax.shard_map(
        shards,
        mesh=mesh,
        in_specs=placed,
        out_specs=P("prompt", None, ("sample", "head")),
        check_vma=False,
    )
```

```python
import functools
import math

import jax
import jax.numpy as jnp
from jax import lax
from jax.experimental import pallas as pl
from jax.experimental.pallas import tpu as pltpu
from jax.sharding import PartitionSpec as P

NOPE = 128
ROPE = 64
LAT = 512
VDIM = 128
F32 = jnp.float32
BF16 = jnp.bfloat16
MESH = pl.DeviceIdType.MESH
FLOOR = -1e30
SCALE = 1.0 / math.sqrt(NOPE + ROPE)
EXP2_SCALE = SCALE * math.log2(math.e)
MOST = 16
NT = (((1,), (1,)), ((), ()))


def dot(left, right):
    return jnp.dot(left, right, preferred_element_type=F32)


def dot_nt(left, right):
    return lax.dot_general(left, right, NT, preferred_element_type=F32)


def put(ref, first, count, stride, value):
    for tile in range(ref.shape[0]):
        ref[tile, pl.ds(first, count, stride=stride), :] = value[:, 128 * tile : 128 * (tile + 1)]


def take(ref, first, count, stride):
    tiles = [ref[tile, pl.ds(first, count, stride=stride), :] for tile in range(ref.shape[0])]
    return jnp.concatenate(tiles, axis=1)


def whole(ref, rows=slice(None)):
    return jnp.concatenate([ref[tile, rows, :] for tile in range(ref.shape[0])], axis=1)


def fill(ref, value, rows=slice(None)):
    for tile in range(ref.shape[0]):
        ref[tile, rows, :] = value[:, 128 * tile : 128 * (tile + 1)]


def iota(shape, axis):
    return lax.broadcasted_iota(jnp.int32, shape, axis)


def exchange_kernel(
    sizes,
    sp_ref,
    len_ref,
    q_ref,
    r_ref,
    nl_ref,
    nr_ref,
    slat_hbm,
    srope_hbm,
    wuk_hbm,
    wuv_hbm,
    rb,
    lvf,
    lse_col,
    slat,
    srope,
    wuk,
    wuv,
    tok,
    ntok,
    qf,
    qb,
    sb,
    lqf,
    lrf,
    lsc,
    lof,
    load_sem,
    q_send,
    q_recv,
):
    nz, ny, nh = sizes
    slots = nz * ny
    z = lax.axis_index("prompt")
    y = lax.axis_index("sample")
    head = lax.axis_index("head")
    here = z * ny + y
    z_at = [lax.rem(z + d, nz) for d in range(nz)]
    y_at = [lax.rem(y + d, ny) for d in range(ny)]
    head_at = [lax.rem(head + d, nh) for d in range(nh)]

    samples = q_ref.shape[0]
    pairs = 2 * samples
    heads = wuk.shape[0]
    half = heads // 2
    wide = 2 * heads

    def ahead(k):
        step = k // ny
        away = (step + 1) // 2
        return z_at[away if step % 2 == 1 else (nz - away) % nz], y_at[k % ny]

    barrier = pltpu.get_barrier_semaphore()
    for k in range(1, slots):
        to_z, to_y = ahead(k)
        pl.semaphore_signal(
            barrier, inc=1, device_id={"prompt": to_z, "sample": to_y}, device_id_type=MESH
        )
    loads = [
        pltpu.make_async_copy(source, target, load_sem.at[index])
        for index, (source, target) in enumerate(
            (
                (wuk_hbm, wuk),
                (slat_hbm, slat),
                (srope_hbm, srope),
                (wuv_hbm, wuv),
            )
        )
    ]
    for load in loads:
        load.start()
    load_wuk, load_slat, load_srope, load_wuv = loads

    for s in range(samples):
        tok[2 * s : 2 * s + 2, :] = q_ref[s].astype(F32)
    for h in range(heads):
        qf[pl.ds(h, pairs, stride=wide), :] = tok[:, h * NOPE : (h + 1) * NOPE]
    for s in range(samples):
        tok[2 * s : 2 * s + 2, : heads * ROPE] = r_ref[s].astype(F32)
    low = iota((pairs, NOPE), 1) < ROPE
    for h in range(heads):
        both = tok[:, h // 2 * NOPE : (h // 2 + 1) * NOPE]
        if h % 2 == 1:
            both = pltpu.roll(both, ROPE, 1)
        qf[pl.ds(heads + h, pairs, stride=wide), :] = jnp.where(low, both, 1.0)
    for s in range(samples):
        qb[s] = qf[2 * wide * s : 2 * wide * (s + 1), :].astype(BF16)
    qb[samples] = jnp.zeros(qb.shape[1:], BF16)

    pl.semaphore_wait(barrier, slots - 1)

    def query_copy(k):
        to_z, to_y = ahead(k)
        return pltpu.make_async_remote_copy(
            src_ref=sb.at[k],
            dst_ref=rb.at[k],
            send_sem=q_send.at[k],
            recv_sem=q_recv.at[k],
            device_id={"prompt": to_z, "sample": to_y},
            device_id_type=MESH,
        )

    names = [sp_ref[s] for s in range(samples)]

    def sample_for(owner):
        found = samples
        for s in range(samples):
            found = jnp.where(names[s] == owner, s, found)
        return found

    for k in range(1, slots):
        to_z, to_y = ahead(k)
        sb[k] = qb[sample_for(to_z * ny + to_y)]
        query_copy(k).start()
    rb[0] = qb[sample_for(here)]

    side = 8 * pairs
    for s in range(samples):
        ntok[2 * s : 2 * s + 2, :LAT] = nl_ref[s].astype(F32)
        ntok[2 * s : 2 * s + 2, LAT:] = jnp.zeros((2, NOPE), F32)
        ntok[2 * s : 2 * s + 2, LAT : LAT + ROPE] = nr_ref[s].astype(F32)
    for g in range(2):
        for h in range(half, 8):
            lrf[pl.ds(g * side + h, pairs, stride=8), :] = jnp.zeros((pairs, NOPE), F32)
            put(lqf, g * side + h, pairs, 8, jnp.zeros((pairs, LAT), F32))
    load_wuk.wait()
    for g in range(2):
        for h in range(half):
            rows = qf[pl.ds(g * half + h, pairs, stride=wide), :].astype(BF16)
            put(lqf, g * side + h, pairs, 8, dot(rows, wuk[g * half + h]))
            rope_rows = qf[pl.ds(heads + g * half + h, pairs, stride=wide), :]
            lrf[pl.ds(g * side + h, pairs, stride=8), :] = jnp.where(low, rope_rows, 0.0)
    load_slat.wait()
    load_srope.wait()
    lane = iota((32, 128), 1)
    spans = [(slice(16 * s, 16 * s + 16), slice(side + 16 * s, side + 16 * s + 16)) for s in range(samples)]
    for s, (top, bottom) in enumerate(spans):
        lat_rows = jnp.concatenate([whole(lqf, top), whole(lqf, bottom)], axis=0).astype(BF16)
        rope_rows = jnp.concatenate([lrf[top, :], lrf[bottom, :]], axis=0).astype(BF16)[:, :ROPE]
        scores = dot_nt(lat_rows, slat[s]) + dot(rope_rows, srope[s])
        scores = jnp.where(lane < len_ref[s], scores, FLOOR)
        lsc[top, :] = scores[:16]
        lsc[bottom, :] = scores[16:]
    new_latent = ntok[:, :LAT].astype(BF16)
    new_rope = ntok[:, LAT:].astype(BF16)
    count = 2 * side
    new_scores = dot_nt(whole(lqf).astype(BF16), new_latent) + dot_nt(
        lrf[...].astype(BF16), new_rope
    )
    row, key = iota((count, pairs), 0), iota((count, pairs), 1)
    row = jnp.where(row >= side, row - side, row)
    valid = ((key >> 1) == (row >> 4)) & ((key & 1) <= ((row >> 3) & 1))
    new_scores = jnp.where(valid, new_scores, FLOOR)
    old_scores = lsc[...]
    peak = jnp.maximum(
        jnp.max(old_scores, axis=1, keepdims=True), jnp.max(new_scores, axis=1, keepdims=True)
    )
    old_exp = jnp.exp2((old_scores - peak) * EXP2_SCALE)
    new_exp = jnp.exp2((new_scores - peak) * EXP2_SCALE)
    total = jnp.sum(old_exp, axis=1, keepdims=True) + jnp.sum(new_exp, axis=1, keepdims=True)
    lse_col[...] = jnp.broadcast_to(peak * SCALE + jnp.log(total), lse_col.shape)
    lsc[...] = old_exp
    new_out = dot(new_exp.astype(BF16), new_latent)
    inverse = 1.0 / total
    for s, (top, bottom) in enumerate(spans):
        probs = jnp.concatenate([lsc[top, :], lsc[bottom, :]], axis=0).astype(BF16)
        own_out = dot(probs, slat[s])
        fill(lof, (new_out[top] + own_out[:16]) * inverse[top], top)
        fill(lof, (new_out[bottom] + own_out[16:]) * inverse[bottom], bottom)
    load_wuv.wait()
    for g in range(2):
        for h in range(half):
            rows = take(lof, g * side + h, pairs, 8).astype(BF16)
            lvf[pl.ds(g * side + h, pairs, stride=8), :] = dot(rows, wuv[g * half + h])
        for h in range(half, 8):
            lvf[pl.ds(g * side + h, pairs, stride=8), :] = jnp.zeros((pairs, VDIM), F32)

    for k in range(1, slots):
        query_copy(k).wait_recv()
    for k in range(1, slots):
        query_copy(k).wait_send()


def prompt_kernel(
    most,
    rb,
    plat_hbm,
    prope_hbm,
    wuk_hbm,
    wuv_hbm,
    back,
    plat,
    prope,
    wuk,
    wuv,
    xf,
    plf,
    prf,
    sc,
    pb,
    pof,
    rvf,
    load_sem,
):
    slots = rb.shape[0]
    spots = 2 * slots
    used = 2 * most
    heads = wuk.shape[0]
    half = heads // 2
    wide = 2 * heads
    loads = [
        pltpu.make_async_copy(source, target, load_sem.at[index])
        for index, (source, target) in enumerate(
            (
                (wuk_hbm, wuk),
                (plat_hbm.at[0], plat),
                (prope_hbm.at[0], prope),
                (wuv_hbm, wuv),
            )
        )
    ]
    for load in loads:
        load.start()
    load_wuk, load_plat, load_prope, load_wuv = loads

    for g in range(2):
        for h in range(half, 8):
            rvf[g, pl.ds(h, spots, stride=8), :] = jnp.zeros((spots, VDIM), F32)
    xf[...] = rb[...].astype(F32).reshape(xf.shape)
    flags = pltpu.roll(xf[pl.ds(heads, spots, stride=wide), :], ROPE, 1)
    down, across = iota((spots, spots), 0), iota((spots, spots), 1)
    before = jnp.where(((across & 1) == 0) & ((across >> 1) < (down >> 1)), 1.0, 0.0)
    rank_down = dot(before.astype(BF16), flags.astype(BF16))[:, :used]
    down, across = iota((spots, used), 0), iota((spots, used), 1)
    unpick = jnp.where(
        (flags[:, :used] > 0.5)
        & (rank_down == (across >> 1).astype(F32))
        & ((across & 1) == (down & 1)),
        1.0,
        0.0,
    ).astype(BF16)
    down, across = iota((spots, spots), 0), iota((spots, spots), 1)
    after = ((down & 1) == 0) & ((down >> 1) < (across >> 1))
    square = flags[:, :spots]
    ones = jnp.ones((used, spots), BF16)
    rank_across = dot(ones, jnp.where(after, square, 0.0).astype(BF16))
    flag_across = dot(ones, jnp.where(down == across, square, 0.0).astype(BF16))
    down, across = iota((used, spots), 0), iota((used, spots), 1)
    pick = jnp.where(
        (flag_across > 0.5)
        & (rank_across == (down >> 1).astype(F32))
        & ((across & 1) == (down & 1)),
        1.0,
        0.0,
    ).astype(BF16)
    rows_all = used * half
    down, across = iota((used, rows_all), 0) * half, iota((used, rows_all), 1)
    gather_rows = jnp.where((across >= down) & (across < down + half), 1.0, 0.0).astype(BF16)
    stat_pick = dot(unpick, gather_rows).astype(BF16)
    length = plat.shape[0]
    tile = min(512, length)
    for load in loads:
        load.wait()
    for g in range(2):
        for h in range(half):
            at = g * half + h
            both = jnp.concatenate(
                [
                    xf[pl.ds(at, spots, stride=wide), :],
                    xf[pl.ds(heads + at, spots, stride=wide), :],
                ],
                axis=1,
            ).astype(BF16)
            both = dot(pick, both)
            put(plf.at[g], h, used, half, dot(both[:, :NOPE].astype(BF16), wuk[at]))
            prf[g, pl.ds(h, used, stride=half), :] = both[:, NOPE:]
        lat_rows = whole(plf.at[g]).astype(BF16)
        rope_rows = prf[g].astype(BF16)[:, :ROPE]
        top = None
        for at in range(0, length, tile):
            scores = dot_nt(lat_rows, plat[at : at + tile, :]) + dot(
                rope_rows, prope[:, at : at + tile]
            )
            sc[g, :, at : at + tile] = scores
            for lanes in range(0, tile, 128):
                piece = scores[:, lanes : lanes + 128]
                top = piece if top is None else jnp.maximum(top, piece)
        peak = jnp.max(top, axis=1, keepdims=True)
        sums_of = jnp.zeros((rows_all, 128), F32)
        for at in range(0, length, tile):
            probs = jnp.exp2((sc[g, :, at : at + tile] - peak) * EXP2_SCALE)
            for lanes in range(0, tile, 128):
                sums_of = sums_of + probs[:, lanes : lanes + 128]
            pb[g, :, at : at + tile] = probs.astype(BF16)
        total = jnp.sum(sums_of, axis=1, keepdims=True)
        fill(pof.at[g], dot(pb[g], plat[...]) * (1.0 / total))
        for h in range(half):
            rows = take(pof.at[g], h, used, half).astype(BF16)
            head_values = dot(rows, wuv[g * half + h]).astype(BF16)
            rvf[g, pl.ds(h, spots, stride=8), :] = dot(unpick, head_values)
        lse = peak * SCALE + jnp.log(total)
        first = lse.astype(BF16).astype(F32)
        second = (lse - first).astype(BF16).astype(F32)
        third = lse - first - second
        row, lane = iota((rows_all, 128), 0), iota((rows_all, 128), 1)
        place = row - half * ((row * 43691) >> 18)
        spread = (
            jnp.where(lane == place, first, 0.0)
            + jnp.where(lane == place + 16, second, 0.0)
            + jnp.where(lane == place + 32, third, 0.0)
        ).astype(BF16)
        rvf[g, pl.ds(half, spots, stride=8), :] = dot(stat_pick, spread)
        back[g] = rvf[g].reshape(slots, 16, VDIM).astype(BF16)


def return_kernel(
    sizes,
    sp_ref,
    back,
    lvf_in,
    lse_col,
    vg,
    lvf,
    rr0,
    rr1,
    cf,
    b_send,
    b_recv,
    v_send,
    v_recv,
):
    nz, ny, nh = sizes
    slots = nz * ny
    z = lax.axis_index("prompt")
    y = lax.axis_index("sample")
    head = lax.axis_index("head")
    here = z * ny + y
    z_at = [lax.rem(z + d, nz) for d in range(nz)]
    y_at = [lax.rem(y + d, ny) for d in range(ny)]
    head_at = [lax.rem(head + d, nh) for d in range(nh)]

    samples = sp_ref.shape[0]
    pairs = 2 * samples
    half = vg.shape[3] * 2 // VDIM
    side = 8 * pairs

    def ahead(k):
        step = k // ny
        away = (step + 1) // 2
        return z_at[away if step % 2 == 1 else (nz - away) % nz], y_at[k % ny]

    def behind(k):
        step = k // ny
        away = (step + 1) // 2
        return z_at[(nz - away) % nz if step % 2 == 1 else away], y_at[(ny - k % ny) % ny]

    barrier = pltpu.get_barrier_semaphore()
    for k in range(1, slots):
        to_z, to_y = ahead(k)
        pl.semaphore_signal(
            barrier, inc=1, device_id={"prompt": to_z, "sample": to_y}, device_id_type=MESH
        )
    names = [sp_ref[s] for s in range(samples)]
    lvf[...] = lvf_in[...]
    pl.semaphore_wait(barrier, slots - 1)

    def back_copy(g, k):
        to_z, to_y = behind(k)
        return pltpu.make_async_remote_copy(
            src_ref=back.at[g, k],
            dst_ref=(rr0, rr1)[g].at[here],
            send_sem=b_send.at[g, k],
            recv_sem=b_recv.at[g, k],
            device_id={"prompt": to_z, "sample": to_y},
            device_id_type=MESH,
        )

    for g in range(2):
        for k in range(1, slots):
            back_copy(g, k).start()
        (rr0, rr1)[g][here] = back[g, 0]

    def value_copy(g, d):
        return pltpu.make_async_remote_copy(
            src_ref=vg.at[g, y],
            dst_ref=vg.at[g, y],
            send_sem=v_send.at[g, d],
            recv_sem=v_recv.at[g, d],
            device_id={"sample": y_at[d]},
            device_id_type=MESH,
        )

    third_of = half // 2
    row, lane = iota((8, 128), 0), iota((8, 128), 1)
    mine = (lane == row) | (lane == row + 16) | (lane == row + 32)
    for g in range(2):
        for k in range(1, slots):
            back_copy(g, k).wait_recv()
        for s in range(samples):
            cf[16 * s : 16 * s + 16, :] = (rr0, rr1)[g][names[s]].astype(F32)
        for pair in range(pairs):
            rows = slice(8 * pair, 8 * pair + 8)
            local_rows = slice(g * side + 8 * pair, g * side + 8 * pair + 8)
            stat = jnp.broadcast_to(cf[8 * pair + half : 8 * pair + half + 1, :], (8, 128))
            lse_prompt = jnp.sum(jnp.where(mine, stat, 0.0), axis=1, keepdims=True)
            lse_local = lse_col[local_rows, :]
            top = jnp.maximum(lse_prompt, lse_local)
            weight_prompt = jnp.exp(lse_prompt - top)
            weight_local = jnp.exp(lse_local - top)
            lvf[local_rows, :] = (
                weight_prompt * cf[rows, :] + weight_local * lvf[local_rows, :]
            ) / (weight_prompt + weight_local)
        columns = [
            jnp.concatenate(
                [
                    lvf[pl.ds(g * side + h, pairs, stride=8), :],
                    lvf[pl.ds(g * side + h + third_of, pairs, stride=8), :],
                ],
                axis=0,
            )
            for h in range(third_of)
        ]
        vg[g, y] = jnp.concatenate(columns, axis=1).astype(BF16)
        for d in range(1, ny):
            value_copy(g, d).start()

    for g in range(2):
        for d in range(1, ny):
            value_copy(g, d).wait_recv()
        for k in range(1, slots):
            back_copy(g, k).wait_send()
        for d in range(1, ny):
            value_copy(g, d).wait_send()


def sum_kernel(
    sizes,
    vg,
    wout_hbm,
    out_ref,
    wout,
    lhs,
    part,
    blocks,
    sums,
    final,
    load_sem,
    o_send,
    o_recv,
):
    nz, ny, nh = sizes
    slots = nz * ny
    z = lax.axis_index("prompt")
    y = lax.axis_index("sample")
    head = lax.axis_index("head")
    here = z * ny + y
    z_at = [lax.rem(z + d, nz) for d in range(nz)]
    y_at = [lax.rem(y + d, ny) for d in range(ny)]
    head_at = [lax.rem(head + d, nh) for d in range(nh)]

    pairs = lhs.shape[0] // ny
    samples = pairs // 2
    half = lhs.shape[1] // VDIM
    barrier = pltpu.get_barrier_semaphore()
    for d in range(1, nh):
        pl.semaphore_signal(
            barrier, inc=1, device_id={"head": head_at[d]}, device_id_type=MESH
        )
    loads = [
        pltpu.make_async_copy(source, target, load_sem.at[index])
        for index, (source, target) in enumerate(
            (
                (wout_hbm, wout),
            )
        )
    ]
    for load in loads:
        load.start()
    load_wout, = loads

    def sum_copy(j):
        return pltpu.make_async_remote_copy(
            src_ref=blocks.at[j],
            dst_ref=sums.at[head],
            send_sem=o_send.at[j],
            recv_sem=o_recv.at[head],
            device_id={"head": j},
            device_id_type=MESH,
        )

    pl.semaphore_wait(barrier, nh - 1)
    load_wout.wait()
    columns_all = wout.shape[1]
    width = columns_all // nh
    inner = half * VDIM
    done = 0
    tile = 256
    for g in range(2):
        for d in range(ny):
            gathered = vg[g, d].astype(F32)
            lhs[pairs * d : pairs * (d + 1), : inner // 2] = gathered[:pairs]
            lhs[pairs * d : pairs * (d + 1), inner // 2 :] = gathered[pairs:]
        left = lhs[...].astype(BF16)
        for at in range(0, columns_all, tile):
            stop = min(at + tile, columns_all)
            product = dot(left, wout[g * inner : (g + 1) * inner, at:stop])
            if g == 0:
                part[:, at:stop] = product
                continue
            part[:, at:stop] = part[:, at:stop] + product
            while done < nh and (done + 1) * width <= stop:
                start = done * width
                floor = start // 128 * 128
                ceil = min(-(-(start + width) // 128) * 128, columns_all)
                block = part[:, floor:ceil]
                if start > floor:
                    block = pltpu.roll(block, ceil - start, 1)
                blocks[done] = block[:, :width].astype(BF16)

                @pl.when(head != done)
                def _(j=done):
                    sum_copy(j).start()

                done += 1

    result = blocks[head].astype(F32)
    for d in range(1, nh):
        source = head_at[d]
        pltpu.make_async_remote_copy(
            src_ref=blocks.at[source],
            dst_ref=sums.at[source],
            send_sem=o_send.at[source],
            recv_sem=o_recv.at[source],
            device_id={"head": source},
            device_id_type=MESH,
        ).wait_recv()
        result = result + sums[source].astype(F32)
    final[...] = result
    for row in range(ny * samples):
        out_ref[row] = final[2 * row : 2 * row + 2, :].astype(BF16)
    for d in range(1, nh):
        sum_copy(head_at[d]).wait_send()


def shards(
    q_nope,
    q_rope,
    new_latent,
    new_rope,
    prompt_latent,
    prompt_rope,
    suffix_latent,
    suffix_rope,
    sample_prompt,
    suffix_len,
    w_uk,
    w_uv,
    w_out,
):
    sizes = nz, ny, nh = tuple(lax.axis_size(name) for name in ("prompt", "sample", "head"))
    slots = nz * ny
    samples = q_nope.shape[0]
    pairs = 2 * samples
    heads = w_uk.shape[0]
    length = prompt_latent.shape[1]
    width = w_out.shape[1] // nh
    half = heads // 2
    most = min(MOST, slots)
    rows_all = 2 * most * half
    count = 16 * pairs
    vmem = pltpu.VMEM
    dma = pltpu.SemaphoreType.DMA
    in_vmem = pl.BlockSpec(memory_space=pltpu.VMEM)
    in_smem = pl.BlockSpec(memory_space=pltpu.SMEM)
    in_hbm = pl.BlockSpec(memory_space=pl.ANY)
    shape = jax.ShapeDtypeStruct

    def params(number, mebibytes):
        return pltpu.CompilerParams(
            collective_id=number, has_side_effects=True, vmem_limit_bytes=mebibytes * 1024 * 1024
        )

    queries, own_values, own_lse = pl.pallas_call(
        functools.partial(exchange_kernel, sizes),
        out_shape=[
            shape((slots, 4 * heads, NOPE), BF16),
            shape((count, VDIM), F32),
            shape((count, VDIM), F32),
        ],
        in_specs=[in_smem] * 2 + [in_vmem] * 4 + [in_hbm] * 4,
        out_specs=[in_vmem] * 3,
        scratch_shapes=[
            vmem(suffix_latent.shape, BF16),
            vmem(suffix_rope.shape, BF16),
            vmem(w_uk.shape, BF16),
            vmem(w_uv.shape, BF16),
            vmem((pairs, heads * NOPE), F32),
            vmem((pairs, LAT + NOPE), F32),
            vmem((pairs * 2 * heads, NOPE), F32),
            vmem((samples + 1, 4 * heads, NOPE), BF16),
            vmem((slots, 4 * heads, NOPE), BF16),
            vmem((LAT // 128, count, 128), F32),
            vmem((count, NOPE), F32),
            vmem((count, suffix_latent.shape[1]), F32),
            vmem((LAT // 128, count, 128), F32),
            dma((4,)),
            dma((slots,)),
            dma((slots,)),
        ],
        compiler_params=params(0, 24),
        cost_estimate=pl.CostEstimate(
            flops=4 * 10**8, bytes_accessed=6 * 10**6, transcendentals=10**5
        ),
    )(
        sample_prompt,
        suffix_len,
        q_nope,
        q_rope,
        new_latent,
        new_rope,
        suffix_latent,
        suffix_rope,
        w_uk,
        w_uv,
    )
    back = pl.pallas_call(
        functools.partial(prompt_kernel, most),
        out_shape=shape((2, slots, 16, VDIM), BF16),
        in_specs=[in_vmem] + [in_hbm] * 4,
        out_specs=in_vmem,
        scratch_shapes=[
            vmem(prompt_latent.shape[1:], BF16),
            vmem(prompt_rope.shape[1:], BF16),
            vmem(w_uk.shape, BF16),
            vmem(w_uv.shape, BF16),
            vmem((slots * 4 * heads, NOPE), F32),
            vmem((2, LAT // 128, rows_all, 128), F32),
            vmem((2, rows_all, NOPE), F32),
            vmem((2, rows_all, length), F32),
            vmem((2, rows_all, length), BF16),
            vmem((2, LAT // 128, rows_all, 128), F32),
            vmem((2, 16 * slots, VDIM), F32),
            dma((4,)),
        ],
        compiler_params=pltpu.CompilerParams(vmem_limit_bytes=32 * 1024 * 1024),
        cost_estimate=pl.CostEstimate(
            flops=3 * 10**9, bytes_accessed=6 * 10**6, transcendentals=10**6
        ),
    )(queries, prompt_latent, prompt_rope, w_uk, w_uv)
    gathered = pl.pallas_call(
        functools.partial(return_kernel, sizes),
        out_shape=shape((2, ny, 2 * pairs, half * VDIM // 2), BF16),
        in_specs=[in_smem] + [in_vmem] * 3,
        out_specs=in_vmem,
        scratch_shapes=[
            vmem((count, VDIM), F32),
            vmem((slots, 16, VDIM), BF16),
            vmem((slots, 16, VDIM), BF16),
            vmem((8 * pairs, VDIM), F32),
            dma((2, slots)),
            dma((2, slots)),
            dma((2, ny)),
            dma((2, ny)),
        ],
        compiler_params=params(1, 8),
        cost_estimate=pl.CostEstimate(flops=10**6, bytes_accessed=10**6, transcendentals=10**4),
    )(sample_prompt, back, own_values, own_lse)
    return pl.pallas_call(
        functools.partial(sum_kernel, sizes),
        out_shape=shape((samples * ny, 2, width), BF16),
        in_specs=[in_vmem, in_hbm],
        out_specs=in_vmem,
        scratch_shapes=[
            vmem(w_out.shape, BF16),
            vmem((ny * pairs, half * VDIM), F32),
            vmem((ny * pairs, w_out.shape[1]), F32),
            vmem((nh, ny * pairs, width), BF16),
            vmem((nh, ny * pairs, width), BF16),
            vmem((ny * pairs, width), F32),
            dma((1,)),
            dma((nh,)),
            dma((nh,)),
        ],
        compiler_params=params(2, 16),
        cost_estimate=pl.CostEstimate(flops=6 * 10**8, bytes_accessed=6 * 10**6, transcendentals=0),
    )(gathered, w_out)


def solution(mesh):
    placed = (
        P(("prompt", "sample"), None, "head"),
        P(("prompt", "sample"), None, "head"),
        P(("prompt", "sample"), None, None),
        P(("prompt", "sample"), None, None),
        P(("prompt", "sample"), None, None),
        P(("prompt", "sample"), None, None),
        P(("prompt", "sample"), None, None),
        P(("prompt", "sample"), None, None),
        P(("prompt", "sample")),
        P(("prompt", "sample")),
        P("head", None, None),
        P("head", None, None),
        P("head", "sample"),
    )
    return jax.shard_map(
        shards,
        mesh=mesh,
        in_specs=placed,
        out_specs=P("prompt", None, ("sample", "head")),
        check_vma=False,
    )
```

```python
import functools
import math

import jax
import jax.numpy as jnp
from jax import lax
from jax.experimental import pallas as pl
from jax.experimental.pallas import tpu as pltpu
from jax.sharding import PartitionSpec as P

NOPE = 128
ROPE = 64
LAT = 512
VDIM = 128
F32 = jnp.float32
BF16 = jnp.bfloat16
MESH = pl.DeviceIdType.MESH
FLOOR = -1e30
SCALE = 1.0 / math.sqrt(NOPE + ROPE)
EXP2_SCALE = SCALE * math.log2(math.e)
MOST = 16
NT = (((1,), (1,)), ((), ()))


def dot(left, right):
    return jnp.dot(left, right, preferred_element_type=F32)


def dot_nt(left, right):
    return lax.dot_general(left, right, NT, preferred_element_type=F32)


def put(ref, first, count, stride, value):
    for tile in range(ref.shape[0]):
        ref[tile, pl.ds(first, count, stride=stride), :] = value[:, 128 * tile : 128 * (tile + 1)]


def take(ref, first, count, stride):
    tiles = [ref[tile, pl.ds(first, count, stride=stride), :] for tile in range(ref.shape[0])]
    return jnp.concatenate(tiles, axis=1)


def whole(ref, rows=slice(None)):
    return jnp.concatenate([ref[tile, rows, :] for tile in range(ref.shape[0])], axis=1)


def fill(ref, value, rows=slice(None)):
    for tile in range(ref.shape[0]):
        ref[tile, rows, :] = value[:, 128 * tile : 128 * (tile + 1)]


def iota(shape, axis):
    return lax.broadcasted_iota(jnp.int32, shape, axis)


def kernel(
    sizes,
    sp_ref,
    len_ref,
    q_hbm,
    r_hbm,
    nl_hbm,
    nr_hbm,
    plat_hbm,
    prope_hbm,
    slat_hbm,
    srope_hbm,
    wuk_hbm,
    wuv_hbm,
    wout_hbm,
    out_ref,
    q_ref,
    r_ref,
    nl_ref,
    nr_ref,
    plat,
    prope,
    slat,
    srope,
    wuk,
    wuv,
    wout,
    tok,
    ntok,
    qf,
    qb,
    sb,
    rb,
    xf,
    lqf,
    lrf,
    lsc,
    lnew,
    linv,
    lof,
    lvf,
    lse_col,
    plf,
    prf,
    sc,
    pb,
    pof,
    rvf,
    back,
    rr,
    cf,
    vg,
    lhs,
    part,
    keep,
    blocks,
    pair_in,
    chip_sum,
    sums,
    final,
    load_sem,
    ready,
    q_send,
    q_recv,
    b_send,
    b_recv,
    v_send,
    v_recv,
    p_send,
    p_recv,
    o_send,
    o_recv,
):
    nz, ny, nh = sizes
    nx = nh // 2
    slots = nz * ny
    samples = q_ref.shape[0]
    pairs = 2 * samples
    heads = wuk.shape[0]
    wide = 2 * heads
    spots = 2 * slots
    used = 2 * min(MOST, slots)
    z = lax.axis_index("prompt")
    y = lax.axis_index("sample")
    head = lax.axis_index("head")
    core = lax.rem(head, 2)
    x = head // 2
    here = z * ny + y
    z_at = [lax.rem(z + d, nz) for d in range(nz)]
    y_at = [lax.rem(y + d, ny) for d in range(ny)]
    x_at = [lax.rem(x + d, nx) for d in range(nx)]
    mate = head + 1 - 2 * core

    def ahead(k):
        step = k // ny
        away = (step + 1) // 2
        return z_at[away if step % 2 == 1 else (nz - away) % nz], y_at[k % ny]

    def behind(k):
        step = k // ny
        away = (step + 1) // 2
        return z_at[(nz - away) % nz if step % 2 == 1 else away], y_at[(ny - k % ny) % ny]

    barrier = pltpu.get_barrier_semaphore()
    near = (
        [{"prompt": z_at[d]} for d in range(1, nz)]
        + [{"sample": y_at[d]} for d in range(1, ny)]
        + [{"head": mate}]
        + [{"head": 2 * x_at[d] + core} for d in range(1, nx)]
    )
    for device in near:
        pl.semaphore_signal(barrier, inc=1, device_id=device, device_id_type=MESH)

    loads = [
        pltpu.make_async_copy(source, target, load_sem.at[index])
        for index, (source, target) in enumerate(
            (
                (q_hbm, q_ref),
                (r_hbm, r_ref),
                (nl_hbm, nl_ref),
                (nr_hbm, nr_ref),
                (wuk_hbm, wuk),
                (slat_hbm, slat),
                (srope_hbm, srope),
                (plat_hbm.at[0], plat),
                (prope_hbm.at[0], prope),
                (wuv_hbm, wuv),
                (wout_hbm, wout),
            )
        )
    ]
    for load in loads:
        load.start()

    loads[0].wait()
    for s in range(samples):
        tok[2 * s : 2 * s + 2, :] = q_ref[s].astype(F32)
    for h in range(heads):
        qf[pl.ds(h, pairs, stride=wide), :] = tok[:, h * NOPE : (h + 1) * NOPE]
    loads[1].wait()
    for s in range(samples):
        tok[2 * s : 2 * s + 2, : heads * ROPE] = r_ref[s].astype(F32)
    low = iota((pairs, NOPE), 1) < ROPE
    for h in range(heads):
        both = tok[:, h // 2 * NOPE : (h // 2 + 1) * NOPE]
        if h % 2 == 1:
            both = pltpu.roll(both, ROPE, 1)
        qf[pl.ds(heads + h, pairs, stride=wide), :] = jnp.where(low, both, 1.0)
    for s in range(samples):
        qb[s] = qf[2 * wide * s : 2 * wide * (s + 1), :].astype(BF16)
    qb[samples] = jnp.zeros(qb.shape[1:], BF16)

    pl.semaphore_wait(barrier, len(near))
    for d in range(1, ny):
        pl.semaphore_signal(ready, inc=1, device_id={"sample": y_at[d]}, device_id_type=MESH)
    pl.semaphore_wait(ready, ny - 1)

    def query_copy(k):
        to_z, to_y = ahead(k)
        return pltpu.make_async_remote_copy(
            src_ref=sb.at[k],
            dst_ref=rb.at[k],
            send_sem=q_send.at[k],
            recv_sem=q_recv.at[k],
            device_id={"prompt": to_z, "sample": to_y},
            device_id_type=MESH,
        )

    names = [sp_ref[s] for s in range(samples)]

    def sample_for(owner):
        found = samples
        for s in range(samples):
            found = jnp.where(names[s] == owner, s, found)
        return found

    for k in range(1, slots):
        to_z, to_y = ahead(k)
        sb[k] = qb[sample_for(to_z * ny + to_y)]
        query_copy(k).start()
    rb[0] = qb[sample_for(here)]

    loads[2].wait()
    loads[3].wait()
    for s in range(samples):
        ntok[2 * s : 2 * s + 2, :LAT] = nl_ref[s].astype(F32)
        ntok[2 * s : 2 * s + 2, LAT:] = jnp.zeros((2, NOPE), F32)
        ntok[2 * s : 2 * s + 2, LAT : LAT + ROPE] = nr_ref[s].astype(F32)
    for h in range(heads, 16):
        lrf[pl.ds(h, pairs, stride=16), :] = jnp.zeros((pairs, NOPE), F32)
        put(lqf, h, pairs, 16, jnp.zeros((pairs, LAT), F32))
    loads[4].wait()
    for h in range(heads):
        rows = qf[pl.ds(h, pairs, stride=wide), :].astype(BF16)
        put(lqf, h, pairs, 16, dot(rows, wuk[h]))
        rope_rows = qf[pl.ds(heads + h, pairs, stride=wide), :]
        lrf[pl.ds(h, pairs, stride=16), :] = jnp.where(low, rope_rows, 0.0)
    loads[5].wait()
    loads[6].wait()
    lane = iota((32, 128), 1)
    for s in range(samples):
        rows = slice(32 * s, 32 * s + 32)
        scores = dot_nt(whole(lqf, rows).astype(BF16), slat[s]) + dot(
            lrf[rows, :].astype(BF16)[:, :ROPE], srope[s]
        )
        lsc[rows, :] = jnp.where(lane < len_ref[s], scores, FLOOR)
    new_latent = ntok[:, :LAT].astype(BF16)
    new_rope = ntok[:, LAT:].astype(BF16)
    count = 16 * pairs
    new_scores = dot_nt(whole(lqf).astype(BF16), new_latent) + dot_nt(
        lrf[...].astype(BF16), new_rope
    )
    row, key = iota((count, pairs), 0), iota((count, pairs), 1)
    valid = ((key >> 1) == (row >> 5)) & ((key & 1) <= ((row >> 4) & 1))
    new_scores = jnp.where(valid, new_scores, FLOOR)
    old_scores = lsc[...]
    peak = jnp.maximum(
        jnp.max(old_scores, axis=1, keepdims=True), jnp.max(new_scores, axis=1, keepdims=True)
    )
    old_exp = jnp.exp2((old_scores - peak) * EXP2_SCALE)
    new_exp = jnp.exp2((new_scores - peak) * EXP2_SCALE)
    total = jnp.sum(old_exp, axis=1, keepdims=True) + jnp.sum(new_exp, axis=1, keepdims=True)
    lse_col[...] = jnp.broadcast_to(peak * SCALE + jnp.log(total), lse_col.shape)
    linv[...] = jnp.broadcast_to(1.0 / total, linv.shape)
    lsc[...] = old_exp
    lnew[...] = new_exp

    def back_copy(k):
        to_z, to_y = behind(k)
        return pltpu.make_async_remote_copy(
            src_ref=back.at[k],
            dst_ref=rr.at[here],
            send_sem=b_send.at[k],
            recv_sem=b_recv.at[k],
            device_id={"prompt": to_z, "sample": to_y},
            device_id_type=MESH,
        )

    for h in range(heads, 16):
        rvf[pl.ds(h, spots, stride=16), :] = jnp.zeros((spots, VDIM), F32)
    for load in loads[7:10]:
        load.wait()
    for k in range(1, slots):
        query_copy(k).wait_recv()
    xf[...] = rb[...].astype(F32).reshape(xf.shape)
    flags = pltpu.roll(xf[pl.ds(heads, spots, stride=wide), :], ROPE, 1)
    down, across = iota((spots, spots), 0), iota((spots, spots), 1)
    before = jnp.where(((across & 1) == 0) & ((across >> 1) < (down >> 1)), 1.0, 0.0)
    rank_down = dot(before.astype(BF16), flags.astype(BF16))[:, :used]
    down, across = iota((spots, used), 0), iota((spots, used), 1)
    unpick = jnp.where(
        (flags[:, :used] > 0.5)
        & (rank_down == (across >> 1).astype(F32))
        & ((across & 1) == (down & 1)),
        1.0,
        0.0,
    ).astype(BF16)
    down, across = iota((spots, spots), 0), iota((spots, spots), 1)
    after = ((down & 1) == 0) & ((down >> 1) < (across >> 1))
    square = flags[:, :spots]
    ones = jnp.ones((used, spots), BF16)
    rank_across = dot(ones, jnp.where(after, square, 0.0).astype(BF16))
    flag_across = dot(ones, jnp.where(down == across, square, 0.0).astype(BF16))
    down, across = iota((used, spots), 0), iota((used, spots), 1)
    pick = jnp.where(
        (flag_across > 0.5)
        & (rank_across == (down >> 1).astype(F32))
        & ((across & 1) == (down & 1)),
        1.0,
        0.0,
    ).astype(BF16)
    rows_all = used * heads
    down, across = iota((used, rows_all), 0) * heads, iota((used, rows_all), 1)
    gather_rows = jnp.where((across >= down) & (across < down + heads), 1.0, 0.0).astype(BF16)
    stat_pick = dot(unpick, gather_rows).astype(BF16)
    length = plat.shape[0]
    tile = min(512, length)
    for h in range(heads):
        both = jnp.concatenate(
            [xf[pl.ds(h, spots, stride=wide), :], xf[pl.ds(heads + h, spots, stride=wide), :]],
            axis=1,
        ).astype(BF16)
        both = dot(pick, both)
        put(plf, h, used, heads, dot(both[:, :NOPE].astype(BF16), wuk[h]))
        prf[pl.ds(h, used, stride=heads), :] = both[:, NOPE:]
    lat_rows = whole(plf).astype(BF16)
    rope_rows = prf[...].astype(BF16)[:, :ROPE]
    top = None
    for at in range(0, length, tile):
        scores = dot_nt(lat_rows, plat[at : at + tile, :]) + dot(
            rope_rows, prope[:, at : at + tile]
        )
        sc[:, at : at + tile] = scores
        for lanes in range(0, tile, 128):
            piece = scores[:, lanes : lanes + 128]
            top = piece if top is None else jnp.maximum(top, piece)
    peak = jnp.max(top, axis=1, keepdims=True)
    sums_of = jnp.zeros((rows_all, 128), F32)
    for at in range(0, length, tile):
        probs = jnp.exp2((sc[:, at : at + tile] - peak) * EXP2_SCALE)
        for lanes in range(0, tile, 128):
            sums_of = sums_of + probs[:, lanes : lanes + 128]
        pb[:, at : at + tile] = probs.astype(BF16)
    total = jnp.sum(sums_of, axis=1, keepdims=True)
    fill(pof, dot(pb[...], plat[...]) * (1.0 / total))
    for h in range(heads):
        head_values = dot(take(pof, h, used, heads).astype(BF16), wuv[h]).astype(BF16)
        rvf[pl.ds(h, spots, stride=16), :] = dot(unpick, head_values)
    lse = peak * SCALE + jnp.log(total)
    first = lse.astype(BF16).astype(F32)
    second = (lse - first).astype(BF16).astype(F32)
    third = lse - first - second
    row, lane = iota((rows_all, 128), 0), iota((rows_all, 128), 1)
    place = row - heads * ((row * 43691) >> 19)
    spread = (
        jnp.where(lane == place, first, 0.0)
        + jnp.where(lane == place + 16, second, 0.0)
        + jnp.where(lane == place + 32, third, 0.0)
    ).astype(BF16)
    rvf[pl.ds(heads, spots, stride=16), :] = dot(stat_pick, spread)
    back[...] = rvf[...].reshape(slots, 32, VDIM).astype(BF16)
    for k in range(1, slots):
        back_copy(k).start()
    rr[here] = back[0]

    new_out = dot(lnew[...].astype(BF16), ntok[:, :LAT].astype(BF16))
    for s in range(samples):
        rows = slice(32 * s, 32 * s + 32)
        own_out = new_out[rows] + dot(lsc[rows, :].astype(BF16), slat[s])
        fill(lof, own_out * linv[rows, :1], rows)
    for h in range(heads):
        lvf[pl.ds(h, pairs, stride=16), :] = dot(take(lof, h, pairs, 16).astype(BF16), wuv[h])
    for h in range(heads, 16):
        lvf[pl.ds(h, pairs, stride=16), :] = jnp.zeros((pairs, VDIM), F32)
    for k in range(1, slots):
        query_copy(k).wait_send()
    loads[10].wait()
    for k in range(1, slots):
        back_copy(k).wait_recv()

    for s in range(samples):
        cf[32 * s : 32 * s + 32, :] = rr[names[s]].astype(F32)
    row, lane = iota((16, 128), 0), iota((16, 128), 1)
    mine = (lane == row) | (lane == row + 16) | (lane == row + 32)
    for pair in range(pairs):
        rows = slice(16 * pair, 16 * pair + 16)
        stat = jnp.broadcast_to(cf[16 * pair + heads : 16 * pair + heads + 1, :], (16, 128))
        lse_prompt = jnp.sum(jnp.where(mine, stat, 0.0), axis=1, keepdims=True)
        lse_local = lse_col[rows, :]
        top = jnp.maximum(lse_prompt, lse_local)
        weight_prompt = jnp.exp(lse_prompt - top)
        weight_local = jnp.exp(lse_local - top)
        lvf[rows, :] = (weight_prompt * cf[rows, :] + weight_local * lvf[rows, :]) / (
            weight_prompt + weight_local
        )
    half = heads // 2
    columns = [
        jnp.concatenate(
            [lvf[pl.ds(h, pairs, stride=16), :], lvf[pl.ds(h + half, pairs, stride=16), :]], axis=0
        )
        for h in range(half)
    ]
    vg[y] = jnp.concatenate(columns, axis=1).astype(BF16)

    def value_copy(d):
        return pltpu.make_async_remote_copy(
            src_ref=vg.at[y],
            dst_ref=vg.at[y],
            send_sem=v_send.at[d],
            recv_sem=v_recv.at[d],
            device_id={"sample": y_at[d]},
            device_id_type=MESH,
        )

    for d in range(1, ny):
        value_copy(d).start()
    for k in range(1, slots):
        back_copy(k).wait_send()
    for d in range(1, ny):
        value_copy(d).wait_recv()

    for d in range(ny):
        gathered = vg[d].astype(F32)
        lhs[pairs * d : pairs * (d + 1), : half * VDIM] = gathered[:pairs]
        lhs[pairs * d : pairs * (d + 1), half * VDIM :] = gathered[pairs:]
    left = lhs[...].astype(BF16)
    columns_all = wout.shape[1]
    width = columns_all // nh

    def mate_copy(chip, block):
        return pltpu.make_async_remote_copy(
            src_ref=blocks.at[block],
            dst_ref=pair_in.at[chip],
            send_sem=p_send.at[chip],
            recv_sem=p_recv.at[chip],
            device_id={"head": mate},
            device_id_type=MESH,
        )

    def chip_copy(chip, source):
        return pltpu.make_async_remote_copy(
            src_ref=chip_sum.at[chip],
            dst_ref=sums.at[source],
            send_sem=o_send.at[chip],
            recv_sem=o_recv.at[source],
            device_id={"head": 2 * chip + core},
            device_id_type=MESH,
        )

    def add_mate(chip):
        mate_copy(chip, 2 * chip).wait_recv()
        both = keep[2 * chip + core] + pair_in[chip].astype(F32)
        chip_sum[chip] = both.astype(BF16)

        @pl.when(x != chip)
        def _():
            chip_copy(chip, x).start()

        @pl.when(x == chip)
        def _():
            final[...] = both

    done = 0
    tile = 256
    for at in range(0, columns_all, tile):
        stop = min(at + tile, columns_all)
        part[:, at:stop] = dot(left, wout[:, at:stop])
        while done < nh and (done + 1) * width <= stop:
            start = done * width
            floor = start // 128 * 128
            ceil = min(-(-(start + width) // 128) * 128, columns_all)
            block = part[:, floor:ceil]
            if start > floor:
                block = pltpu.roll(block, ceil - start, 1)
            keep[done] = block[:, :width]
            blocks[done] = block[:, :width].astype(BF16)

            @pl.when(core != done % 2)
            def _(j=done):
                mate_copy(j // 2, j).start()

            if done % 2 == 1 and done > 1:
                add_mate(done // 2 - 1)
            done += 1
    add_mate(nx - 1)
    for d in range(1, ny):
        value_copy(d).wait_send()
    for chip in range(nx):
        mate_copy(chip, 2 * chip).wait_send()
    result = final[...]
    for d in range(1, nx):
        chip_copy(x_at[d], x_at[d]).wait_recv()
        result = result + sums[x_at[d]].astype(F32)
    final[...] = result
    for row in range(ny * samples):
        out_ref[row] = final[2 * row : 2 * row + 2, :]
    for d in range(1, nx):
        chip_copy(x_at[d], x).wait_send()


def shards(
    q_nope,
    q_rope,
    new_latent,
    new_rope,
    prompt_latent,
    prompt_rope,
    suffix_latent,
    suffix_rope,
    sample_prompt,
    suffix_len,
    w_uk,
    w_uv,
    w_out,
):
    nz, ny, nh = (lax.axis_size(name) for name in ("prompt", "sample", "head"))
    slots = nz * ny
    samples = q_nope.shape[0]
    pairs = 2 * samples
    heads = w_uk.shape[0]
    length = prompt_latent.shape[1]
    width = w_out.shape[1] // nh
    used = 2 * min(MOST, slots)
    rows_all = used * heads
    count = 16 * pairs
    vmem = pltpu.VMEM
    dma = pltpu.SemaphoreType.DMA
    in_vmem = pl.BlockSpec(memory_space=pltpu.VMEM)
    in_smem = pl.BlockSpec(memory_space=pltpu.SMEM)
    in_hbm = pl.BlockSpec(memory_space=pltpu.HBM)
    arrays = (
        q_nope,
        q_rope,
        new_latent,
        new_rope,
        prompt_latent,
        prompt_rope,
        suffix_latent,
        suffix_rope,
        w_uk,
        w_uv,
        w_out,
    )
    return pl.pallas_call(
        functools.partial(kernel, (nz, ny, nh)),
        out_shape=jax.ShapeDtypeStruct((samples * ny, 2, width), F32),
        in_specs=[in_smem] * 2 + [in_hbm] * 11,
        out_specs=in_vmem,
        scratch_shapes=[
            vmem(q_nope.shape, BF16),
            vmem(q_rope.shape, BF16),
            vmem(new_latent.shape, BF16),
            vmem(new_rope.shape, BF16),
            vmem(prompt_latent.shape[1:], BF16),
            vmem(prompt_rope.shape[1:], BF16),
            vmem(suffix_latent.shape, BF16),
            vmem(suffix_rope.shape, BF16),
            vmem(w_uk.shape, BF16),
            vmem(w_uv.shape, BF16),
            vmem(w_out.shape, BF16),
            vmem((pairs, heads * NOPE), F32),
            vmem((pairs, LAT + NOPE), F32),
            vmem((pairs * 2 * heads, NOPE), F32),
            vmem((samples + 1, 4 * heads, NOPE), BF16),
            vmem((slots, 4 * heads, NOPE), BF16),
            vmem((slots, 4 * heads, NOPE), BF16),
            vmem((slots * 4 * heads, NOPE), F32),
            vmem((LAT // 128, count, 128), F32),
            vmem((count, NOPE), F32),
            vmem((count, suffix_latent.shape[1]), F32),
            vmem((count, pairs), F32),
            vmem((count, VDIM), F32),
            vmem((LAT // 128, count, 128), F32),
            vmem((count, VDIM), F32),
            vmem((count, VDIM), F32),
            vmem((LAT // 128, rows_all, 128), F32),
            vmem((rows_all, NOPE), F32),
            vmem((rows_all, length), F32),
            vmem((rows_all, length), BF16),
            vmem((LAT // 128, rows_all, 128), F32),
            vmem((32 * slots, VDIM), F32),
            vmem((slots, 32, VDIM), BF16),
            vmem((slots, 32, VDIM), BF16),
            vmem((count, VDIM), F32),
            vmem((ny, 2 * pairs, heads * VDIM // 2), BF16),
            vmem((ny * pairs, heads * VDIM), F32),
            vmem((ny * pairs, w_out.shape[1]), F32),
            vmem((nh, ny * pairs, width), F32),
            vmem((nh, ny * pairs, width), BF16),
            vmem((nh // 2, ny * pairs, width), BF16),
            vmem((nh // 2, ny * pairs, width), BF16),
            vmem((nh // 2, ny * pairs, width), BF16),
            vmem((ny * pairs, width), F32),
            dma((len(arrays),)),
            pltpu.SemaphoreType.REGULAR,
            dma((slots,)),
            dma((slots,)),
            dma((slots,)),
            dma((slots,)),
            dma((ny,)),
            dma((ny,)),
            dma((nh // 2,)),
            dma((nh // 2,)),
            dma((nh // 2,)),
            dma((nh // 2,)),
        ],
        compiler_params=pltpu.CompilerParams(
            collective_id=0, has_side_effects=True, vmem_limit_bytes=56 * 1024 * 1024
        ),
        cost_estimate=pl.CostEstimate(
            flops=4 * 10**9, bytes_accessed=13 * 10**6, transcendentals=10**6
        ),
    )(sample_prompt, suffix_len, *arrays).astype(BF16)


def solution(mesh):
    placed = (
        P(("prompt", "sample"), None, "head"),
        P(("prompt", "sample"), None, "head"),
        P(("prompt", "sample"), None, None),
        P(("prompt", "sample"), None, None),
        P(("prompt", "sample"), None, None),
        P(("prompt", "sample"), None, None),
        P(("prompt", "sample"), None, None),
        P(("prompt", "sample"), None, None),
        P(("prompt", "sample")),
        P(("prompt", "sample")),
        P("head", None, None),
        P("head", None, None),
        P("head", "sample"),
    )
    return jax.shard_map(
        shards,
        mesh=mesh,
        in_specs=placed,
        out_specs=P("prompt", None, ("sample", "head")),
        check_vma=False,
    )
```

```python
import functools
import math

import jax
import jax.numpy as jnp
from jax import lax
from jax.experimental import pallas as pl
from jax.experimental.pallas import tpu as pltpu
from jax.sharding import PartitionSpec as P

NOPE = 128
ROPE = 64
LAT = 512
VDIM = 128
F32 = jnp.float32
BF16 = jnp.bfloat16
MESH = pl.DeviceIdType.MESH
FLOOR = -1e30
SCALE = 1.0 / math.sqrt(NOPE + ROPE)
EXP2_SCALE = SCALE * math.log2(math.e)
CHUNKS = 2
NT = (((1,), (1,)), ((), ()))


def dot(left, right):
    return jnp.dot(left, right, preferred_element_type=F32)


def dot_nt(left, right):
    return lax.dot_general(left, right, NT, preferred_element_type=F32)


def put(ref, first, count, stride, value):
    for tile in range(ref.shape[0]):
        ref[tile, pl.ds(first, count, stride=stride), :] = value[:, 128 * tile : 128 * (tile + 1)]


def take(ref, first, count, stride):
    tiles = [ref[tile, pl.ds(first, count, stride=stride), :] for tile in range(ref.shape[0])]
    return jnp.concatenate(tiles, axis=1)


def whole(ref, rows=slice(None)):
    return jnp.concatenate([ref[tile, rows, :] for tile in range(ref.shape[0])], axis=1)


def fill(ref, value, rows=slice(None)):
    for tile in range(ref.shape[0]):
        ref[tile, rows, :] = value[:, 128 * tile : 128 * (tile + 1)]


def iota(shape, axis):
    return lax.broadcasted_iota(jnp.int32, shape, axis)


def kernel(
    sizes,
    sp_ref,
    len_ref,
    q_hbm,
    r_hbm,
    nl_hbm,
    nr_hbm,
    plat_hbm,
    prope_hbm,
    slat_hbm,
    srope_hbm,
    wuk_hbm,
    wuv_hbm,
    wout_hbm,
    out_ref,
    q_ref,
    r_ref,
    nl_ref,
    nr_ref,
    plat,
    prope,
    slat,
    srope,
    wuk,
    wuv,
    wout,
    tok,
    ntok,
    qf,
    qb,
    sb,
    rb,
    xf,
    lqf,
    lrf,
    lsc,
    lnew,
    linv,
    lof,
    lvf,
    lse_col,
    plf,
    prf,
    sc,
    pb,
    pof,
    rvf,
    back,
    rr,
    cf,
    vg0,
    vg1,
    lhs0,
    lhs1,
    part,
    keep0,
    keep1,
    blocks0,
    blocks1,
    pair_in0,
    pair_in1,
    chip_sum0,
    chip_sum1,
    sums0,
    sums1,
    final0,
    final1,
    load_sem,
    q_send,
    q_recv,
    b_send,
    b_recv,
    v_send,
    v_recv,
    p_send,
    p_recv,
    o_send,
    o_recv,
):
    nz, ny, nh = sizes
    nx = nh // 2
    slots = nz * ny
    samples = q_ref.shape[0]
    pairs = 2 * samples
    heads = wuk.shape[0]
    wide = 2 * heads
    z = lax.axis_index("prompt")
    y = lax.axis_index("sample")
    head = lax.axis_index("head")
    core = lax.rem(head, 2)
    x = head // 2
    here = z * ny + y
    y_at = [lax.rem(y + d, ny) for d in range(ny)]
    x_at = [lax.rem(x + d, nx) for d in range(nx)]
    mate = head + 1 - 2 * core

    def ahead(k):
        step = k // ny
        half = (step + 1) // 2
        shift = jnp.where(step % 2 == 1, half, nz - half)
        return lax.rem(z + shift, nz), lax.rem(y + k % ny, ny)

    def behind(k):
        step = k // ny
        half = (step + 1) // 2
        shift = jnp.where(step % 2 == 1, nz - half, half)
        return lax.rem(z + shift, nz), lax.rem(y + ny - k % ny, ny)

    barrier = pltpu.get_barrier_semaphore()

    @pl.loop(1, slots)
    def _(k):
        to_z, to_y = ahead(k)
        pl.semaphore_signal(
            barrier, inc=1, device_id={"prompt": to_z, "sample": to_y}, device_id_type=MESH
        )

    near = [mate] + [2 * x_at[d] + core for d in range(1, nx)]
    for peer in near:
        pl.semaphore_signal(barrier, inc=1, device_id={"head": peer}, device_id_type=MESH)

    loads = [
        pltpu.make_async_copy(source, target, load_sem.at[index])
        for index, (source, target) in enumerate(
            (
                (q_hbm, q_ref),
                (r_hbm, r_ref),
                (nl_hbm, nl_ref),
                (nr_hbm, nr_ref),
                (wuk_hbm, wuk),
                (slat_hbm, slat),
                (srope_hbm, srope),
                (plat_hbm.at[0], plat),
                (prope_hbm.at[0], prope),
                (wuv_hbm, wuv),
                (wout_hbm, wout),
            )
        )
    ]
    for load in loads:
        load.start()

    loads[0].wait()
    for s in range(samples):
        tok[2 * s : 2 * s + 2, :] = q_ref[s].astype(F32)
    for h in range(heads):
        qf[pl.ds(h, pairs, stride=wide), :] = tok[:, h * NOPE : (h + 1) * NOPE]
    loads[1].wait()
    for s in range(samples):
        tok[2 * s : 2 * s + 2, : heads * ROPE] = r_ref[s].astype(F32)
    low = iota((pairs, NOPE), 1) < ROPE
    for h in range(heads):
        both = tok[:, h // 2 * NOPE : (h // 2 + 1) * NOPE]
        if h % 2 == 1:
            both = pltpu.roll(both, ROPE, 1)
        qf[pl.ds(heads + h, pairs, stride=wide), :] = jnp.where(low, both, 0.0)
    for s in range(samples):
        qb[s] = qf[2 * wide * s : 2 * wide * (s + 1), :].astype(BF16)

    pl.semaphore_wait(barrier, slots - 1 + len(near))

    def query_copy(k):
        to_z, to_y = ahead(k)
        return pltpu.make_async_remote_copy(
            src_ref=sb.at[k],
            dst_ref=rb.at[k],
            send_sem=q_send.at[k],
            recv_sem=q_recv.at[k],
            device_id={"prompt": to_z, "sample": to_y},
            device_id_type=MESH,
        )

    names = [sp_ref[s] for s in range(samples)]

    def sample_for(owner):
        found = 0
        for s in range(samples):
            found = jnp.where(names[s] == owner, s, found)
        return found

    @pl.loop(1, slots)
    def _(k):
        to_z, to_y = ahead(k)
        sb[k] = qb[sample_for(to_z * ny + to_y)]
        query_copy(k).start()

    rb[0] = qb[sample_for(here)]

    loads[2].wait()
    loads[3].wait()
    for s in range(samples):
        ntok[2 * s : 2 * s + 2, :LAT] = nl_ref[s].astype(F32)
        ntok[2 * s : 2 * s + 2, LAT:] = jnp.zeros((2, NOPE), F32)
        ntok[2 * s : 2 * s + 2, LAT : LAT + ROPE] = nr_ref[s].astype(F32)
    for h in range(heads, 16):
        lrf[pl.ds(h, pairs, stride=16), :] = jnp.zeros((pairs, NOPE), F32)
        put(lqf, h, pairs, 16, jnp.zeros((pairs, LAT), F32))
    loads[4].wait()
    for h in range(heads):
        rows = qf[pl.ds(h, pairs, stride=wide), :].astype(BF16)
        put(lqf, h, pairs, 16, dot(rows, wuk[h]))
        lrf[pl.ds(h, pairs, stride=16), :] = qf[pl.ds(heads + h, pairs, stride=wide), :]
    loads[5].wait()
    loads[6].wait()
    lane = iota((32, 128), 1)
    for s in range(samples):
        rows = slice(32 * s, 32 * s + 32)
        scores = dot_nt(whole(lqf, rows).astype(BF16), slat[s]) + dot(
            lrf[rows, :].astype(BF16)[:, :ROPE], srope[s]
        )
        lsc[rows, :] = jnp.where(lane < len_ref[s], scores, FLOOR)
    new_latent = ntok[:, :LAT].astype(BF16)
    new_rope = ntok[:, LAT:].astype(BF16)
    count = 16 * pairs
    new_scores = dot_nt(whole(lqf).astype(BF16), new_latent) + dot_nt(
        lrf[...].astype(BF16), new_rope
    )
    row, key = iota((count, pairs), 0), iota((count, pairs), 1)
    valid = ((key >> 1) == (row >> 5)) & ((key & 1) <= ((row >> 4) & 1))
    new_scores = jnp.where(valid, new_scores, FLOOR)
    old_scores = lsc[...]
    peak = jnp.maximum(
        jnp.max(old_scores, axis=1, keepdims=True), jnp.max(new_scores, axis=1, keepdims=True)
    )
    old_exp = jnp.exp2((old_scores - peak) * EXP2_SCALE)
    new_exp = jnp.exp2((new_scores - peak) * EXP2_SCALE)
    total = jnp.sum(old_exp, axis=1, keepdims=True) + jnp.sum(new_exp, axis=1, keepdims=True)
    lse_col[...] = jnp.broadcast_to(peak * SCALE + jnp.log(total), lse_col.shape)
    linv[...] = jnp.broadcast_to(1.0 / total, linv.shape)
    lsc[...] = old_exp
    lnew[...] = new_exp

    for load in loads[7:10]:
        load.wait()
    size = slots // CHUNKS
    duo = 2 * size
    rows_all = wide * size
    for h in range(heads, 16):
        rvf[pl.ds(h, duo, stride=16), :] = jnp.zeros((duo, VDIM), F32)

    def back_copy(k):
        to_z, to_y = behind(k)
        return pltpu.make_async_remote_copy(
            src_ref=back.at[k],
            dst_ref=rr.at[here],
            send_sem=b_send.at[k],
            recv_sem=b_recv.at[k],
            device_id={"prompt": to_z, "sample": to_y},
            device_id_type=MESH,
        )

    @pl.loop(0, CHUNKS)
    def _(chunk):
        base = chunk * size

        @pl.loop(0, size)
        def _(i):
            @pl.when(base + i > 0)
            def _():
                query_copy(base + i).wait_recv()

        xf[...] = rb[pl.ds(base, size)].astype(F32).reshape(xf.shape)
        for h in range(heads):
            rows = xf[pl.ds(h, duo, stride=wide), :].astype(BF16)
            put(plf, h, duo, heads, dot(rows, wuk[h]))
            prf[pl.ds(h, duo, stride=heads), :] = xf[pl.ds(heads + h, duo, stride=wide), :]
        lat_rows = whole(plf).astype(BF16)
        rope_rows = prf[...].astype(BF16)[:, :ROPE]
        length = plat.shape[0]
        tile = min(512, length)
        top = None
        for at in range(0, length, tile):
            scores = dot_nt(lat_rows, plat[at : at + tile, :]) + dot(
                rope_rows, prope[:, at : at + tile]
            )
            sc[:, at : at + tile] = scores
            for lanes in range(0, tile, 128):
                piece = scores[:, lanes : lanes + 128]
                top = piece if top is None else jnp.maximum(top, piece)
        peak = jnp.max(top, axis=1, keepdims=True)
        sums_of = jnp.zeros((rows_all, 128), F32)
        for at in range(0, length, tile):
            probs = jnp.exp2((sc[:, at : at + tile] - peak) * EXP2_SCALE)
            for lanes in range(0, tile, 128):
                sums_of = sums_of + probs[:, lanes : lanes + 128]
            pb[:, at : at + tile] = probs.astype(BF16)
        total = jnp.sum(sums_of, axis=1, keepdims=True)
        fill(pof, dot(pb[...], plat[...]) * (1.0 / total))
        for h in range(heads):
            rows = take(pof, h, duo, heads).astype(BF16)
            rvf[pl.ds(h, duo, stride=16), :] = dot(rows, wuv[h])
        lse = peak * SCALE + jnp.log(total)
        first = lse.astype(BF16).astype(F32)
        second = (lse - first).astype(BF16).astype(F32)
        third = lse - first - second
        row, lane = iota((rows_all, 128), 0), iota((rows_all, 128), 1)
        place = row - heads * ((row * 43691) >> 19)
        spread = (
            jnp.where(lane == place, first, 0.0)
            + jnp.where(lane == place + 16, second, 0.0)
            + jnp.where(lane == place + 32, third, 0.0)
        ).astype(BF16)
        at, of = iota((duo, rows_all), 0) * heads, iota((duo, rows_all), 1)
        pick = jnp.where((of >= at) & (of < at + heads), 1.0, 0.0).astype(BF16)
        rvf[pl.ds(heads, duo, stride=16), :] = dot(pick, spread)
        back[pl.ds(base, size)] = rvf[...].reshape(size, 32, VDIM).astype(BF16)

        @pl.loop(0, size)
        def _(i):
            @pl.when(base + i > 0)
            def _():
                back_copy(base + i).start()

    rr[here] = back[0]

    new_out = dot(lnew[...].astype(BF16), ntok[:, :LAT].astype(BF16))
    for s in range(samples):
        rows = slice(32 * s, 32 * s + 32)
        own_out = new_out[rows] + dot(lsc[rows, :].astype(BF16), slat[s])
        fill(lof, own_out * linv[rows, :1], rows)
    for h in range(heads):
        lvf[pl.ds(h, pairs, stride=16), :] = dot(take(lof, h, pairs, 16).astype(BF16), wuv[h])
    for h in range(heads, 16):
        lvf[pl.ds(h, pairs, stride=16), :] = jnp.zeros((pairs, VDIM), F32)
    @pl.loop(1, slots)
    def _(k):
        query_copy(k).wait_send()

    loads[10].wait()

    @pl.loop(1, slots)
    def _(k):
        back_copy(k).wait_recv()

    cuts = (0, 2 * pairs // 3, pairs)
    vgs = (vg0, vg1)
    lhss = (lhs0, lhs1)
    keeps = (keep0, keep1)
    blockss = (blocks0, blocks1)
    pair_ins = (pair_in0, pair_in1)
    chip_sums = (chip_sum0, chip_sum1)
    sumss = (sums0, sums1)
    finals = (final0, final1)

    def value_copy(g, d):
        return pltpu.make_async_remote_copy(
            src_ref=vgs[g].at[y],
            dst_ref=vgs[g].at[y],
            send_sem=v_send.at[g, d],
            recv_sem=v_recv.at[g, d],
            device_id={"sample": y_at[d]},
            device_id_type=MESH,
        )

    for s in range(samples):
        cf[32 * s : 32 * s + 32, :] = rr[names[s]].astype(F32)
    row, lane = iota((16, 128), 0), iota((16, 128), 1)
    mine = (lane == row) | (lane == row + 16) | (lane == row + 32)
    for g in range(2):
        for pair in range(cuts[g], cuts[g + 1]):
            rows = slice(16 * pair, 16 * pair + 16)
            stat = jnp.broadcast_to(cf[16 * pair + heads : 16 * pair + heads + 1, :], (16, 128))
            lse_prompt = jnp.sum(jnp.where(mine, stat, 0.0), axis=1, keepdims=True)
            lse_local = lse_col[rows, :]
            top = jnp.maximum(lse_prompt, lse_local)
            weight_prompt = jnp.exp(lse_prompt - top)
            weight_local = jnp.exp(lse_local - top)
            lvf[rows, :] = (weight_prompt * cf[rows, :] + weight_local * lvf[rows, :]) / (
                weight_prompt + weight_local
            )
        rows_of = cuts[g + 1] - cuts[g]
        columns = [
            lvf[pl.ds(16 * cuts[g] + h, rows_of, stride=16), :] for h in range(heads)
        ]
        folds = 16 // rows_of if rows_of < 16 else 1
        per = heads // folds
        vgs[g][y] = jnp.concatenate(
            [
                jnp.concatenate(columns[fold * per : (fold + 1) * per], axis=1)
                for fold in range(folds)
            ],
            axis=0,
        ).astype(BF16)
        for d in range(1, ny):
            value_copy(g, d).start()

    @pl.loop(1, slots)
    def _(k):
        back_copy(k).wait_send()

    columns_all = wout.shape[1]
    width = columns_all // nh

    def mate_copy(g, chip, block):
        return pltpu.make_async_remote_copy(
            src_ref=blockss[g].at[block],
            dst_ref=pair_ins[g].at[chip],
            send_sem=p_send.at[g, chip],
            recv_sem=p_recv.at[g, chip],
            device_id={"head": mate},
            device_id_type=MESH,
        )

    def chip_copy(g, chip, source):
        return pltpu.make_async_remote_copy(
            src_ref=chip_sums[g].at[chip],
            dst_ref=sumss[g].at[source],
            send_sem=o_send.at[g, chip],
            recv_sem=o_recv.at[g, source],
            device_id={"head": 2 * chip + core},
            device_id_type=MESH,
        )

    def add_mate(g, chip):
        mate_copy(g, chip, 2 * chip).wait_recv()
        both = keeps[g][2 * chip + core] + pair_ins[g][chip].astype(F32)
        chip_sums[g][chip] = both.astype(BF16)

        @pl.when(x != chip)
        def _():
            chip_copy(g, chip, x).start()

        @pl.when(x == chip)
        def _():
            finals[g][...] = both

    for g in range(2):
        rows_of = cuts[g + 1] - cuts[g]
        folds = 16 // rows_of if rows_of < 16 else 1
        inner = heads * VDIM // folds
        for d in range(1, ny):
            value_copy(g, d).wait_recv()
        for d in range(ny):
            gathered = vgs[g][d].astype(F32)
            for fold in range(folds):
                lhss[g][rows_of * d : rows_of * (d + 1), fold * inner : (fold + 1) * inner] = gathered[
                    fold * rows_of : (fold + 1) * rows_of
                ]
        left = lhss[g][...].astype(BF16)
        rows_here = slice(ny * cuts[g], ny * cuts[g + 1])
        done = 0
        tile = 256
        for at in range(0, columns_all, tile):
            stop = min(at + tile, columns_all)
            part[rows_here, at:stop] = dot(left, wout[:, at:stop])
            while done < nh and (done + 1) * width <= stop:
                start = done * width
                floor = start // 128 * 128
                ceil = min(-(-(start + width) // 128) * 128, columns_all)
                block = part[rows_here, floor:ceil]
                if start > floor:
                    block = pltpu.roll(block, ceil - start, 1)
                keeps[g][done] = block[:, :width]
                blockss[g][done] = block[:, :width].astype(BF16)

                @pl.when(core != done % 2)
                def _(j=done):
                    mate_copy(g, j // 2, j).start()

                if done % 2 == 1 and done > 1:
                    add_mate(g, done // 2 - 1)
                done += 1
        add_mate(g, nx - 1)

    for g in range(2):
        for d in range(1, ny):
            value_copy(g, d).wait_send()
        for chip in range(nx):
            mate_copy(g, chip, 2 * chip).wait_send()
    for g in range(2):
        result = finals[g][...]
        for d in range(1, nx):
            chip_copy(g, x_at[d], x_at[d]).wait_recv()
            result = result + sumss[g][x_at[d]].astype(F32)
        finals[g][...] = result
        rows_of = cuts[g + 1] - cuts[g]
        for d in range(ny):
            for s in range(rows_of // 2):
                out_ref[d * samples + cuts[g] // 2 + s] = finals[g][
                    rows_of * d + 2 * s : rows_of * d + 2 * s + 2, :
                ].astype(BF16)
    for g in range(2):
        for d in range(1, nx):
            chip_copy(g, x_at[d], x).wait_send()


def shards(
    q_nope,
    q_rope,
    new_latent,
    new_rope,
    prompt_latent,
    prompt_rope,
    suffix_latent,
    suffix_rope,
    sample_prompt,
    suffix_len,
    w_uk,
    w_uv,
    w_out,
):
    nz, ny, nh = (lax.axis_size(name) for name in ("prompt", "sample", "head"))
    slots = nz * ny
    samples = q_nope.shape[0]
    pairs = 2 * samples
    heads = w_uk.shape[0]
    length = prompt_latent.shape[1]
    width = w_out.shape[1] // nh
    size = slots // CHUNKS
    duo = 2 * size
    rows_all = duo * heads
    big = 2 * pairs // 3
    small = pairs - big
    fold = max(1, 16 // small)
    fold_big = max(1, 16 // big)
    count = 16 * pairs
    vmem = pltpu.VMEM
    dma = pltpu.SemaphoreType.DMA
    in_vmem = pl.BlockSpec(memory_space=pltpu.VMEM)
    in_smem = pl.BlockSpec(memory_space=pltpu.SMEM)
    in_hbm = pl.BlockSpec(memory_space=pltpu.HBM)
    arrays = (
        q_nope,
        q_rope,
        new_latent,
        new_rope,
        prompt_latent,
        prompt_rope,
        suffix_latent,
        suffix_rope,
        w_uk,
        w_uv,
        w_out,
    )
    return pl.pallas_call(
        functools.partial(kernel, (nz, ny, nh)),
        out_shape=jax.ShapeDtypeStruct((samples * ny, 2, width), BF16),
        in_specs=[in_smem] * 2 + [in_hbm] * 11,
        out_specs=in_vmem,
        scratch_shapes=[
            vmem(q_nope.shape, BF16),
            vmem(q_rope.shape, BF16),
            vmem(new_latent.shape, BF16),
            vmem(new_rope.shape, BF16),
            vmem(prompt_latent.shape[1:], BF16),
            vmem(prompt_rope.shape[1:], BF16),
            vmem(suffix_latent.shape, BF16),
            vmem(suffix_rope.shape, BF16),
            vmem(w_uk.shape, BF16),
            vmem(w_uv.shape, BF16),
            vmem(w_out.shape, BF16),
            vmem((pairs, heads * NOPE), F32),
            vmem((pairs, LAT + NOPE), F32),
            vmem((pairs * 2 * heads, NOPE), F32),
            vmem((samples, 4 * heads, NOPE), BF16),
            vmem((slots, 4 * heads, NOPE), BF16),
            vmem((slots, 4 * heads, NOPE), BF16),
            vmem((size * 4 * heads, NOPE), F32),
            vmem((LAT // 128, count, 128), F32),
            vmem((count, NOPE), F32),
            vmem((count, suffix_latent.shape[1]), F32),
            vmem((count, pairs), F32),
            vmem((count, VDIM), F32),
            vmem((LAT // 128, count, 128), F32),
            vmem((count, VDIM), F32),
            vmem((count, VDIM), F32),
            vmem((LAT // 128, rows_all, 128), F32),
            vmem((rows_all, NOPE), F32),
            vmem((rows_all, length), F32),
            vmem((rows_all, length), BF16),
            vmem((LAT // 128, rows_all, 128), F32),
            vmem((32 * size, VDIM), F32),
            vmem((slots, 32, VDIM), BF16),
            vmem((slots, 32, VDIM), BF16),
            vmem((count, VDIM), F32),
            vmem((ny, big * fold_big, heads * VDIM // fold_big), BF16),
            vmem((ny, small * fold, heads * VDIM // fold), BF16),
            vmem((ny * big, heads * VDIM), F32),
            vmem((ny * small, heads * VDIM), F32),
            vmem((ny * pairs, w_out.shape[1]), F32),
            vmem((nh, ny * big, width), F32),
            vmem((nh, ny * small, width), F32),
            vmem((nh, ny * big, width), BF16),
            vmem((nh, ny * small, width), BF16),
            vmem((nh // 2, ny * big, width), BF16),
            vmem((nh // 2, ny * small, width), BF16),
            vmem((nh // 2, ny * big, width), BF16),
            vmem((nh // 2, ny * small, width), BF16),
            vmem((nh // 2, ny * big, width), BF16),
            vmem((nh // 2, ny * small, width), BF16),
            vmem((ny * big, width), F32),
            vmem((ny * small, width), F32),
            dma((len(arrays),)),
            dma((slots,)),
            dma((slots,)),
            dma((slots,)),
            dma((slots,)),
            dma((2, ny)),
            dma((2, ny)),
            dma((2, nh // 2)),
            dma((2, nh // 2)),
            dma((2, nh // 2)),
            dma((2, nh // 2)),
        ],
        compiler_params=pltpu.CompilerParams(
            collective_id=0, has_side_effects=True, vmem_limit_bytes=56 * 1024 * 1024
        ),
        cost_estimate=pl.CostEstimate(
            flops=4 * 10**9, bytes_accessed=13 * 10**6, transcendentals=10**6
        ),
    )(sample_prompt, suffix_len, *arrays)


def solution(mesh):
    placed = (
        P(("prompt", "sample"), None, "head"),
        P(("prompt", "sample"), None, "head"),
        P(("prompt", "sample"), None, None),
        P(("prompt", "sample"), None, None),
        P(("prompt", "sample"), None, None),
        P(("prompt", "sample"), None, None),
        P(("prompt", "sample"), None, None),
        P(("prompt", "sample"), None, None),
        P(("prompt", "sample")),
        P(("prompt", "sample")),
        P("head", None, None),
        P("head", None, None),
        P("head", "sample"),
    )
    return jax.shard_map(
        shards,
        mesh=mesh,
        in_specs=placed,
        out_specs=P("prompt", None, ("sample", "head")),
        check_vma=False,
    )
```

```python
import functools
import math

import jax
import jax.numpy as jnp
from jax import lax
from jax.experimental import pallas as pl
from jax.experimental.pallas import tpu as pltpu
from jax.sharding import PartitionSpec as P

NOPE = 128
ROPE = 64
LAT = 512
VDIM = 128
F32 = jnp.float32
BF16 = jnp.bfloat16
MESH = pl.DeviceIdType.MESH
FLOOR = -1e30
SCALE = 1.0 / math.sqrt(NOPE + ROPE)
EXP2_SCALE = SCALE * math.log2(math.e)
CHUNKS = 2
NT = (((1,), (1,)), ((), ()))


def dot(left, right):
    return jnp.dot(left, right, preferred_element_type=F32)


def dot_nt(left, right):
    return lax.dot_general(left, right, NT, preferred_element_type=F32)


def put(ref, first, count, stride, value):
    for tile in range(ref.shape[0]):
        ref[tile, pl.ds(first, count, stride=stride), :] = value[:, 128 * tile : 128 * (tile + 1)]


def take(ref, first, count, stride):
    tiles = [ref[tile, pl.ds(first, count, stride=stride), :] for tile in range(ref.shape[0])]
    return jnp.concatenate(tiles, axis=1)


def whole(ref, rows=slice(None)):
    return jnp.concatenate([ref[tile, rows, :] for tile in range(ref.shape[0])], axis=1)


def fill(ref, value, rows=slice(None)):
    for tile in range(ref.shape[0]):
        ref[tile, rows, :] = value[:, 128 * tile : 128 * (tile + 1)]


def iota(shape, axis):
    return lax.broadcasted_iota(jnp.int32, shape, axis)


def kernel(
    sizes,
    sp_ref,
    len_ref,
    q_hbm,
    r_hbm,
    nl_hbm,
    nr_hbm,
    plat_hbm,
    prope_hbm,
    slat_hbm,
    srope_hbm,
    wuk_hbm,
    wuv_hbm,
    wout_hbm,
    out_ref,
    q_ref,
    r_ref,
    nl_ref,
    nr_ref,
    plat,
    prope,
    slat,
    srope,
    wuk,
    wuv,
    wout,
    tok,
    ntok,
    qf,
    qb,
    sb,
    rb,
    xf,
    lqf,
    lrf,
    lsc,
    lnew,
    linv,
    lof,
    lvf,
    lse_col,
    plf,
    prf,
    sc,
    pb,
    pof,
    rvf,
    back,
    rr,
    cf,
    vg,
    lhs,
    part,
    blocks,
    sums,
    load_sem,
    q_send,
    q_recv,
    b_send,
    b_recv,
    v_send,
    v_recv,
    o_send,
    o_recv,
):
    nz, ny, nh = sizes
    slots = nz * ny
    samples = q_ref.shape[0]
    pairs = 2 * samples
    heads = wuk.shape[0]
    wide = 2 * heads
    z = lax.axis_index("prompt")
    y = lax.axis_index("sample")
    head = lax.axis_index("head")
    here = z * ny + y

    def ahead(k):
        step = k // ny
        half = (step + 1) // 2
        shift = jnp.where(step % 2 == 1, half, nz - half)
        return lax.rem(z + shift, nz), lax.rem(y + k % ny, ny)

    def behind(k):
        step = k // ny
        half = (step + 1) // 2
        shift = jnp.where(step % 2 == 1, nz - half, half)
        return lax.rem(z + shift, nz), lax.rem(y + ny - k % ny, ny)

    loads = [
        pltpu.make_async_copy(source, target, load_sem.at[index])
        for index, (source, target) in enumerate(
            (
                (q_hbm, q_ref),
                (r_hbm, r_ref),
                (nl_hbm, nl_ref),
                (nr_hbm, nr_ref),
                (wuk_hbm, wuk),
                (slat_hbm, slat),
                (srope_hbm, srope),
                (plat_hbm.at[0], plat),
                (prope_hbm.at[0], prope),
                (wuv_hbm, wuv),
                (wout_hbm, wout),
            )
        )
    ]
    for load in loads[:2]:
        load.start()
    barrier = pltpu.get_barrier_semaphore()

    @pl.loop(1, slots)
    def _(k):
        to_z, to_y = ahead(k)
        pl.semaphore_signal(
            barrier, inc=1, device_id={"prompt": to_z, "sample": to_y}, device_id_type=MESH
        )

    @pl.loop(1, nh)
    def _(d):
        pl.semaphore_signal(
            barrier, inc=1, device_id={"head": lax.rem(head + d, nh)}, device_id_type=MESH
        )

    for load in loads[2:]:
        load.start()

    loads[0].wait()
    for s in range(samples):
        tok[2 * s : 2 * s + 2, :] = q_ref[s].astype(F32)
    for h in range(heads):
        qf[pl.ds(h, pairs, stride=wide), :] = tok[:, h * NOPE : (h + 1) * NOPE]
    loads[1].wait()
    for s in range(samples):
        tok[2 * s : 2 * s + 2, : heads * ROPE] = r_ref[s].astype(F32)
    low = iota((pairs, NOPE), 1) < ROPE
    for h in range(heads):
        both = tok[:, h // 2 * NOPE : (h // 2 + 1) * NOPE]
        if h % 2 == 1:
            both = pltpu.roll(both, ROPE, 1)
        qf[pl.ds(heads + h, pairs, stride=wide), :] = jnp.where(low, both, 0.0)
    for s in range(samples):
        qb[s] = qf[2 * wide * s : 2 * wide * (s + 1), :].astype(BF16)

    pl.semaphore_wait(barrier, slots - 1 + nh - 1)

    def query_copy(k):
        to_z, to_y = ahead(k)
        return pltpu.make_async_remote_copy(
            src_ref=sb.at[k],
            dst_ref=rb.at[k],
            send_sem=q_send.at[k],
            recv_sem=q_recv.at[k],
            device_id={"prompt": to_z, "sample": to_y},
            device_id_type=MESH,
        )

    names = [sp_ref[s] for s in range(samples)]

    def sample_for(owner):
        found = 0
        for s in range(samples):
            found = jnp.where(names[s] == owner, s, found)
        return found

    @pl.loop(1, slots)
    def _(k):
        to_z, to_y = ahead(k)
        sb[k] = qb[sample_for(to_z * ny + to_y)]
        query_copy(k).start()

    rb[0] = qb[sample_for(here)]

    loads[2].wait()
    loads[3].wait()
    for s in range(samples):
        ntok[2 * s : 2 * s + 2, :LAT] = nl_ref[s].astype(F32)
        ntok[2 * s : 2 * s + 2, LAT:] = jnp.zeros((2, NOPE), F32)
        ntok[2 * s : 2 * s + 2, LAT : LAT + ROPE] = nr_ref[s].astype(F32)
    for h in range(heads, 16):
        lrf[pl.ds(h, pairs, stride=16), :] = jnp.zeros((pairs, NOPE), F32)
        put(lqf, h, pairs, 16, jnp.zeros((pairs, LAT), F32))
    loads[4].wait()
    for h in range(heads):
        rows = qf[pl.ds(h, pairs, stride=wide), :].astype(BF16)
        put(lqf, h, pairs, 16, dot(rows, wuk[h]))
        lrf[pl.ds(h, pairs, stride=16), :] = qf[pl.ds(heads + h, pairs, stride=wide), :]
    loads[5].wait()
    loads[6].wait()
    lane = iota((32, 128), 1)
    for s in range(samples):
        rows = slice(32 * s, 32 * s + 32)
        scores = dot_nt(whole(lqf, rows).astype(BF16), slat[s]) + dot(
            lrf[rows, :].astype(BF16)[:, :ROPE], srope[s]
        )
        lsc[rows, :] = jnp.where(lane < len_ref[s], scores, FLOOR)
    new_latent = ntok[:, :LAT].astype(BF16)
    new_rope = ntok[:, LAT:].astype(BF16)
    count = 16 * pairs
    new_scores = dot_nt(whole(lqf).astype(BF16), new_latent) + dot_nt(
        lrf[...].astype(BF16), new_rope
    )
    row, key = iota((count, pairs), 0), iota((count, pairs), 1)
    valid = ((key >> 1) == (row >> 5)) & ((key & 1) <= ((row >> 4) & 1))
    new_scores = jnp.where(valid, new_scores, FLOOR)
    old_scores = lsc[...]
    peak = jnp.maximum(
        jnp.max(old_scores, axis=1, keepdims=True), jnp.max(new_scores, axis=1, keepdims=True)
    )
    old_exp = jnp.exp2((old_scores - peak) * EXP2_SCALE)
    new_exp = jnp.exp2((new_scores - peak) * EXP2_SCALE)
    total = jnp.sum(old_exp, axis=1, keepdims=True) + jnp.sum(new_exp, axis=1, keepdims=True)
    lse_col[...] = jnp.broadcast_to(peak * SCALE + jnp.log(total), lse_col.shape)
    linv[...] = jnp.broadcast_to(1.0 / total, linv.shape)
    lsc[...] = old_exp
    lnew[...] = new_exp

    for load in loads[7:10]:
        load.wait()
    size = slots // CHUNKS
    duo = 2 * size
    rows_all = wide * size
    for h in range(heads, 16):
        rvf[pl.ds(h, duo, stride=16), :] = jnp.zeros((duo, VDIM), F32)

    def back_copy(k):
        to_z, to_y = behind(k)
        return pltpu.make_async_remote_copy(
            src_ref=back.at[k],
            dst_ref=rr.at[here],
            send_sem=b_send.at[k],
            recv_sem=b_recv.at[k],
            device_id={"prompt": to_z, "sample": to_y},
            device_id_type=MESH,
        )

    @pl.loop(0, CHUNKS)
    def _(chunk):
        base = chunk * size

        @pl.loop(0, size)
        def _(i):
            @pl.when(base + i > 0)
            def _():
                query_copy(base + i).wait_recv()

        xf[...] = rb[pl.ds(base, size)].astype(F32).reshape(xf.shape)
        for h in range(heads):
            rows = xf[pl.ds(h, duo, stride=wide), :].astype(BF16)
            put(plf, h, duo, heads, dot(rows, wuk[h]))
            prf[pl.ds(h, duo, stride=heads), :] = xf[pl.ds(heads + h, duo, stride=wide), :]
        lat_rows = whole(plf).astype(BF16)
        rope_rows = prf[...].astype(BF16)[:, :ROPE]
        length = plat.shape[0]
        tile = min(512, length)
        top = None
        for at in range(0, length, tile):
            scores = dot_nt(lat_rows, plat[at : at + tile, :]) + dot(
                rope_rows, prope[:, at : at + tile]
            )
            sc[:, at : at + tile] = scores
            for lanes in range(0, tile, 128):
                piece = scores[:, lanes : lanes + 128]
                top = piece if top is None else jnp.maximum(top, piece)
        peak = jnp.max(top, axis=1, keepdims=True)
        sums_of = jnp.zeros((rows_all, 128), F32)
        for at in range(0, length, tile):
            probs = jnp.exp2((sc[:, at : at + tile] - peak) * EXP2_SCALE)
            for lanes in range(0, tile, 128):
                sums_of = sums_of + probs[:, lanes : lanes + 128]
            pb[:, at : at + tile] = probs.astype(BF16)
        total = jnp.sum(sums_of, axis=1, keepdims=True)
        fill(pof, dot(pb[...], plat[...]) * (1.0 / total))
        for h in range(heads):
            rows = take(pof, h, duo, heads).astype(BF16)
            rvf[pl.ds(h, duo, stride=16), :] = dot(rows, wuv[h])
        lse = peak * SCALE + jnp.log(total)
        first = lse.astype(BF16).astype(F32)
        second = (lse - first).astype(BF16).astype(F32)
        third = lse - first - second
        row, lane = iota((rows_all, 128), 0), iota((rows_all, 128), 1)
        place = row - heads * ((row * 43691) >> 19)
        spread = (
            jnp.where(lane == place, first, 0.0)
            + jnp.where(lane == place + 16, second, 0.0)
            + jnp.where(lane == place + 32, third, 0.0)
        ).astype(BF16)
        at, of = iota((duo, rows_all), 0) * heads, iota((duo, rows_all), 1)
        pick = jnp.where((of >= at) & (of < at + heads), 1.0, 0.0).astype(BF16)
        rvf[pl.ds(heads, duo, stride=16), :] = dot(pick, spread)
        back[pl.ds(base, size)] = rvf[...].reshape(size, 32, VDIM).astype(BF16)

        @pl.loop(0, size)
        def _(i):
            @pl.when(base + i > 0)
            def _():
                back_copy(base + i).start()

    rr[here] = back[0]

    new_out = dot(lnew[...].astype(BF16), ntok[:, :LAT].astype(BF16))
    for s in range(samples):
        rows = slice(32 * s, 32 * s + 32)
        own_out = new_out[rows] + dot(lsc[rows, :].astype(BF16), slat[s])
        fill(lof, own_out * linv[rows, :1], rows)
    for h in range(heads):
        lvf[pl.ds(h, pairs, stride=16), :] = dot(take(lof, h, pairs, 16).astype(BF16), wuv[h])
    for h in range(heads, 16):
        lvf[pl.ds(h, pairs, stride=16), :] = jnp.zeros((pairs, VDIM), F32)
    @pl.loop(1, slots)
    def _(k):
        query_copy(k).wait_send()

    loads[10].wait()

    @pl.loop(1, slots)
    def _(k):
        back_copy(k).wait_recv()

    for s in range(samples):
        cf[32 * s : 32 * s + 32, :] = rr[sp_ref[s]].astype(F32)
    row, lane = iota((16, 128), 0), iota((16, 128), 1)
    mine = (lane == row) | (lane == row + 16) | (lane == row + 32)
    for pair in range(pairs):
        rows = slice(16 * pair, 16 * pair + 16)
        stat = jnp.broadcast_to(cf[16 * pair + heads : 16 * pair + heads + 1, :], (16, 128))
        lse_prompt = jnp.sum(jnp.where(mine, stat, 0.0), axis=1, keepdims=True)
        lse_local = lse_col[rows, :]
        top = jnp.maximum(lse_prompt, lse_local)
        weight_prompt = jnp.exp(lse_prompt - top)
        weight_local = jnp.exp(lse_local - top)
        lvf[rows, :] = (weight_prompt * cf[rows, :] + weight_local * lvf[rows, :]) / (
            weight_prompt + weight_local
        )
    half = heads // 2
    columns = [
        jnp.concatenate(
            [lvf[pl.ds(h, pairs, stride=16), :], lvf[pl.ds(h + half, pairs, stride=16), :]], axis=0
        )
        for h in range(half)
    ]
    vg[y] = jnp.concatenate(columns, axis=1).astype(BF16)

    def value_copy(d):
        return pltpu.make_async_remote_copy(
            src_ref=vg.at[y],
            dst_ref=vg.at[y],
            send_sem=v_send.at[d],
            recv_sem=v_recv.at[d],
            device_id={"sample": lax.rem(y + d, ny)},
            device_id_type=MESH,
        )

    for d in range(1, ny):
        value_copy(d).start()
    for d in range(1, ny):
        value_copy(d).wait_recv()

    for d in range(ny):
        gathered = vg[d].astype(F32)
        lhs[pairs * d : pairs * (d + 1), : half * VDIM] = gathered[:pairs]
        lhs[pairs * d : pairs * (d + 1), half * VDIM :] = gathered[pairs:]
    left = lhs[...].astype(BF16)
    columns_all = wout.shape[1]
    width = columns_all // nh

    def sum_copy(j):
        return pltpu.make_async_remote_copy(
            src_ref=blocks.at[j],
            dst_ref=sums.at[head],
            send_sem=o_send.at[j],
            recv_sem=o_recv.at[head],
            device_id={"head": j},
            device_id_type=MESH,
        )

    done = 0
    tile = 256
    for at in range(0, columns_all, tile):
        stop = min(at + tile, columns_all)
        part[:, at:stop] = dot(left, wout[:, at:stop])
        while done < nh and (done + 1) * width <= stop:
            start = done * width
            floor = start // 128 * 128
            ceil = min(-(-(start + width) // 128) * 128, columns_all)
            block = part[:, floor:ceil]
            if start > floor:
                block = pltpu.roll(block, ceil - start, 1)
            blocks[done] = block[:, :width].astype(BF16)

            @pl.when(head != done)
            def _(j=done):
                sum_copy(j).start()

            done += 1
    @pl.loop(1, slots)
    def _(k):
        back_copy(k).wait_send()

    for d in range(1, ny):
        value_copy(d).wait_send()
    result = blocks[head].astype(F32)
    for d in range(1, nh):
        source = lax.rem(head + d, nh)
        pltpu.make_async_remote_copy(
            src_ref=blocks.at[source],
            dst_ref=sums.at[source],
            send_sem=o_send.at[source],
            recv_sem=o_recv.at[source],
            device_id={"head": source},
            device_id_type=MESH,
        ).wait_recv()
        result = result + sums[source].astype(F32)
    out_ref[...] = result.astype(BF16)


    @pl.loop(1, nh)
    def _(d):
        sum_copy(lax.rem(head + d, nh)).wait_send()


def shards(
    q_nope,
    q_rope,
    new_latent,
    new_rope,
    prompt_latent,
    prompt_rope,
    suffix_latent,
    suffix_rope,
    sample_prompt,
    suffix_len,
    w_uk,
    w_uv,
    w_out,
):
    nz, ny, nh = (lax.axis_size(name) for name in ("prompt", "sample", "head"))
    slots = nz * ny
    samples = q_nope.shape[0]
    pairs = 2 * samples
    heads = w_uk.shape[0]
    length = prompt_latent.shape[1]
    width = w_out.shape[1] // nh
    size = slots // CHUNKS
    duo = 2 * size
    rows_all = duo * heads
    count = 16 * pairs
    vmem = pltpu.VMEM
    dma = pltpu.SemaphoreType.DMA
    in_vmem = pl.BlockSpec(memory_space=pltpu.VMEM)
    in_smem = pl.BlockSpec(memory_space=pltpu.SMEM)
    in_hbm = pl.BlockSpec(memory_space=pltpu.HBM)
    arrays = (
        q_nope,
        q_rope,
        new_latent,
        new_rope,
        prompt_latent,
        prompt_rope,
        suffix_latent,
        suffix_rope,
        w_uk,
        w_uv,
        w_out,
    )
    result = pl.pallas_call(
        functools.partial(kernel, (nz, ny, nh)),
        out_shape=jax.ShapeDtypeStruct((ny * pairs, width), BF16),
        in_specs=[in_smem] * 2 + [in_hbm] * 11,
        out_specs=in_vmem,
        scratch_shapes=[
            vmem(q_nope.shape, BF16),
            vmem(q_rope.shape, BF16),
            vmem(new_latent.shape, BF16),
            vmem(new_rope.shape, BF16),
            vmem(prompt_latent.shape[1:], BF16),
            vmem(prompt_rope.shape[1:], BF16),
            vmem(suffix_latent.shape, BF16),
            vmem(suffix_rope.shape, BF16),
            vmem(w_uk.shape, BF16),
            vmem(w_uv.shape, BF16),
            vmem(w_out.shape, BF16),
            vmem((pairs, heads * NOPE), F32),
            vmem((pairs, LAT + NOPE), F32),
            vmem((pairs * 2 * heads, NOPE), F32),
            vmem((samples, 4 * heads, NOPE), BF16),
            vmem((slots, 4 * heads, NOPE), BF16),
            vmem((slots, 4 * heads, NOPE), BF16),
            vmem((size * 4 * heads, NOPE), F32),
            vmem((LAT // 128, count, 128), F32),
            vmem((count, NOPE), F32),
            vmem((count, suffix_latent.shape[1]), F32),
            vmem((count, pairs), F32),
            vmem((count, VDIM), F32),
            vmem((LAT // 128, count, 128), F32),
            vmem((count, VDIM), F32),
            vmem((count, VDIM), F32),
            vmem((LAT // 128, rows_all, 128), F32),
            vmem((rows_all, NOPE), F32),
            vmem((rows_all, length), F32),
            vmem((rows_all, length), BF16),
            vmem((LAT // 128, rows_all, 128), F32),
            vmem((32 * size, VDIM), F32),
            vmem((slots, 32, VDIM), BF16),
            vmem((slots, 32, VDIM), BF16),
            vmem((count, VDIM), F32),
            vmem((ny, 2 * pairs, heads * VDIM // 2), BF16),
            vmem((ny * pairs, heads * VDIM), F32),
            vmem((ny * pairs, w_out.shape[1]), F32),
            vmem((nh, ny * pairs, width), BF16),
            vmem((nh, ny * pairs, width), BF16),
            dma((len(arrays),)),
            dma((slots,)),
            dma((slots,)),
            dma((slots,)),
            dma((slots,)),
            dma((ny,)),
            dma((ny,)),
            dma((nh,)),
            dma((nh,)),
        ],
        compiler_params=pltpu.CompilerParams(
            collective_id=0, has_side_effects=True, vmem_limit_bytes=56 * 1024 * 1024
        ),
        cost_estimate=pl.CostEstimate(
            flops=4 * 10**9, bytes_accessed=13 * 10**6, transcendentals=10**6
        ),
    )(sample_prompt, suffix_len, *arrays)
    return result.reshape(ny * samples, 2, width)


def solution(mesh):
    placed = (
        P(("prompt", "sample"), None, "head"),
        P(("prompt", "sample"), None, "head"),
        P(("prompt", "sample"), None, None),
        P(("prompt", "sample"), None, None),
        P(("prompt", "sample"), None, None),
        P(("prompt", "sample"), None, None),
        P(("prompt", "sample"), None, None),
        P(("prompt", "sample"), None, None),
        P(("prompt", "sample")),
        P(("prompt", "sample")),
        P("head", None, None),
        P("head", None, None),
        P("head", "sample"),
    )
    return jax.shard_map(
        shards,
        mesh=mesh,
        in_specs=placed,
        out_specs=P("prompt", None, ("sample", "head")),
        check_vma=False,
    )
```

```python
import functools
import math

import jax
import jax.numpy as jnp
from jax import lax
from jax.experimental import pallas as pl
from jax.experimental.pallas import tpu as pltpu
from jax.sharding import PartitionSpec as P

NOPE = 128
ROPE = 64
LAT = 512
VDIM = 128
F32 = jnp.float32
BF16 = jnp.bfloat16
MESH = pl.DeviceIdType.MESH
FLOOR = -1e30
SCALE = 1.0 / math.sqrt(NOPE + ROPE)
EXP2_SCALE = SCALE * math.log2(math.e)
CHUNKS = 2
NT = (((1,), (1,)), ((), ()))


def dot(left, right):
    return jnp.dot(left, right, preferred_element_type=F32)


def dot_nt(left, right):
    return lax.dot_general(left, right, NT, preferred_element_type=F32)


def put(ref, first, count, stride, value):
    for tile in range(ref.shape[0]):
        ref[tile, pl.ds(first, count, stride=stride), :] = value[:, 128 * tile : 128 * (tile + 1)]


def take(ref, first, count, stride):
    tiles = [ref[tile, pl.ds(first, count, stride=stride), :] for tile in range(ref.shape[0])]
    return jnp.concatenate(tiles, axis=1)


def whole(ref, rows=slice(None)):
    return jnp.concatenate([ref[tile, rows, :] for tile in range(ref.shape[0])], axis=1)


def fill(ref, value, rows=slice(None)):
    for tile in range(ref.shape[0]):
        ref[tile, rows, :] = value[:, 128 * tile : 128 * (tile + 1)]


def iota(shape, axis):
    return lax.broadcasted_iota(jnp.int32, shape, axis)


def kernel(
    sizes,
    sp_ref,
    len_ref,
    q_hbm,
    r_hbm,
    nl_hbm,
    nr_hbm,
    plat_hbm,
    prope_hbm,
    slat_hbm,
    srope_hbm,
    wuk_hbm,
    wuv_hbm,
    wout_hbm,
    out_ref,
    q_ref,
    r_ref,
    nl_ref,
    nr_ref,
    plat,
    prope,
    slat,
    srope,
    wuk,
    wuv,
    wout,
    tok,
    ntok,
    qf,
    qb,
    sb,
    rb,
    xf,
    lqf,
    lrf,
    lsc,
    lnew,
    linv,
    lof,
    lvf,
    lse_col,
    plf,
    prf,
    sc,
    pb,
    pof,
    rvf,
    back,
    rr,
    cf,
    vg0,
    vg1,
    lhs0,
    lhs1,
    part,
    blocks0,
    blocks1,
    sums0,
    sums1,
    load_sem,
    q_send,
    q_recv,
    b_send,
    b_recv,
    v_send,
    v_recv,
    o_send,
    o_recv,
):
    nz, ny, nh = sizes
    slots = nz * ny
    samples = q_ref.shape[0]
    pairs = 2 * samples
    heads = wuk.shape[0]
    wide = 2 * heads
    z = lax.axis_index("prompt")
    y = lax.axis_index("sample")
    head = lax.axis_index("head")
    here = z * ny + y
    y_at = [lax.rem(y + d, ny) for d in range(ny)]
    own = slots - ny

    def other(i):
        return jnp.where(i <= own, i - 1, i)

    def ahead(k):
        step = nz - 1 - k // ny
        half = (step + 1) // 2
        shift = jnp.where(step % 2 == 1, half, nz - half)
        return lax.rem(z + shift, nz), lax.rem(y + k % ny, ny)

    def behind(k):
        step = nz - 1 - k // ny
        half = (step + 1) // 2
        shift = jnp.where(step % 2 == 1, nz - half, half)
        return lax.rem(z + shift, nz), lax.rem(y + ny - k % ny, ny)

    loads = [
        pltpu.make_async_copy(source, target, load_sem.at[index])
        for index, (source, target) in enumerate(
            (
                (q_hbm, q_ref),
                (r_hbm, r_ref),
                (nl_hbm, nl_ref),
                (nr_hbm, nr_ref),
                (wuk_hbm, wuk),
                (slat_hbm, slat),
                (srope_hbm, srope),
                (plat_hbm.at[0], plat),
                (prope_hbm.at[0], prope),
                (wuv_hbm, wuv),
                (wout_hbm, wout),
            )
        )
    ]
    for load in loads[:2]:
        load.start()
    barrier = pltpu.get_barrier_semaphore()

    @pl.loop(1, slots)
    def _(i):
        to_z, to_y = ahead(other(i))
        pl.semaphore_signal(
            barrier, inc=1, device_id={"prompt": to_z, "sample": to_y}, device_id_type=MESH
        )

    @pl.loop(1, nh)
    def _(d):
        pl.semaphore_signal(
            barrier, inc=1, device_id={"head": lax.rem(head + d, nh)}, device_id_type=MESH
        )

    for load in loads[2:]:
        load.start()

    loads[0].wait()
    for s in range(samples):
        tok[2 * s : 2 * s + 2, :] = q_ref[s].astype(F32)
    for h in range(heads):
        qf[pl.ds(h, pairs, stride=wide), :] = tok[:, h * NOPE : (h + 1) * NOPE]
    loads[1].wait()
    for s in range(samples):
        tok[2 * s : 2 * s + 2, : heads * ROPE] = r_ref[s].astype(F32)
    low = iota((pairs, NOPE), 1) < ROPE
    for h in range(heads):
        both = tok[:, h // 2 * NOPE : (h // 2 + 1) * NOPE]
        if h % 2 == 1:
            both = pltpu.roll(both, ROPE, 1)
        qf[pl.ds(heads + h, pairs, stride=wide), :] = jnp.where(low, both, 0.0)
    for s in range(samples):
        qb[s] = qf[2 * wide * s : 2 * wide * (s + 1), :].astype(BF16)

    pl.semaphore_wait(barrier, slots - 1 + nh - 1)

    def query_copy(k):
        to_z, to_y = ahead(k)
        return pltpu.make_async_remote_copy(
            src_ref=sb.at[k],
            dst_ref=rb.at[k],
            send_sem=q_send.at[k],
            recv_sem=q_recv.at[k],
            device_id={"prompt": to_z, "sample": to_y},
            device_id_type=MESH,
        )

    names = [sp_ref[s] for s in range(samples)]

    def sample_for(owner):
        found = 0
        for s in range(samples):
            found = jnp.where(names[s] == owner, s, found)
        return found

    @pl.loop(1, slots)
    def _(i):
        k = other(i)
        to_z, to_y = ahead(k)
        sb[k] = qb[sample_for(to_z * ny + to_y)]
        query_copy(k).start()

    rb[own] = qb[sample_for(here)]

    loads[2].wait()
    loads[3].wait()
    for s in range(samples):
        ntok[2 * s : 2 * s + 2, :LAT] = nl_ref[s].astype(F32)
        ntok[2 * s : 2 * s + 2, LAT:] = jnp.zeros((2, NOPE), F32)
        ntok[2 * s : 2 * s + 2, LAT : LAT + ROPE] = nr_ref[s].astype(F32)
    for h in range(heads, 16):
        lrf[pl.ds(h, pairs, stride=16), :] = jnp.zeros((pairs, NOPE), F32)
        put(lqf, h, pairs, 16, jnp.zeros((pairs, LAT), F32))
    loads[4].wait()
    for h in range(heads):
        rows = qf[pl.ds(h, pairs, stride=wide), :].astype(BF16)
        put(lqf, h, pairs, 16, dot(rows, wuk[h]))
        lrf[pl.ds(h, pairs, stride=16), :] = qf[pl.ds(heads + h, pairs, stride=wide), :]
    loads[5].wait()
    loads[6].wait()
    lane = iota((32, 128), 1)
    for s in range(samples):
        rows = slice(32 * s, 32 * s + 32)
        scores = dot_nt(whole(lqf, rows).astype(BF16), slat[s]) + dot(
            lrf[rows, :].astype(BF16)[:, :ROPE], srope[s]
        )
        lsc[rows, :] = jnp.where(lane < len_ref[s], scores, FLOOR)
    new_latent = ntok[:, :LAT].astype(BF16)
    new_rope = ntok[:, LAT:].astype(BF16)
    count = 16 * pairs
    new_scores = dot_nt(whole(lqf).astype(BF16), new_latent) + dot_nt(
        lrf[...].astype(BF16), new_rope
    )
    row, key = iota((count, pairs), 0), iota((count, pairs), 1)
    valid = ((key >> 1) == (row >> 5)) & ((key & 1) <= ((row >> 4) & 1))
    new_scores = jnp.where(valid, new_scores, FLOOR)
    old_scores = lsc[...]
    peak = jnp.maximum(
        jnp.max(old_scores, axis=1, keepdims=True), jnp.max(new_scores, axis=1, keepdims=True)
    )
    old_exp = jnp.exp2((old_scores - peak) * EXP2_SCALE)
    new_exp = jnp.exp2((new_scores - peak) * EXP2_SCALE)
    total = jnp.sum(old_exp, axis=1, keepdims=True) + jnp.sum(new_exp, axis=1, keepdims=True)
    lse_col[...] = jnp.broadcast_to(peak * SCALE + jnp.log(total), lse_col.shape)
    linv[...] = jnp.broadcast_to(1.0 / total, linv.shape)
    lsc[...] = old_exp
    lnew[...] = new_exp

    for load in loads[7:10]:
        load.wait()
    size = slots // CHUNKS
    duo = 2 * size
    rows_all = wide * size
    for h in range(heads, 16):
        rvf[pl.ds(h, duo, stride=16), :] = jnp.zeros((duo, VDIM), F32)

    def back_copy(k):
        to_z, to_y = behind(k)
        return pltpu.make_async_remote_copy(
            src_ref=back.at[k],
            dst_ref=rr.at[here],
            send_sem=b_send.at[k],
            recv_sem=b_recv.at[k],
            device_id={"prompt": to_z, "sample": to_y},
            device_id_type=MESH,
        )

    @pl.loop(0, CHUNKS)
    def _(chunk):
        base = chunk * size

        @pl.loop(0, size)
        def _(i):
            @pl.when(base + i != own)
            def _():
                query_copy(base + i).wait_recv()

        xf[...] = rb[pl.ds(base, size)].astype(F32).reshape(xf.shape)
        for h in range(heads):
            rows = xf[pl.ds(h, duo, stride=wide), :].astype(BF16)
            put(plf, h, duo, heads, dot(rows, wuk[h]))
            prf[pl.ds(h, duo, stride=heads), :] = xf[pl.ds(heads + h, duo, stride=wide), :]
        lat_rows = whole(plf).astype(BF16)
        rope_rows = prf[...].astype(BF16)[:, :ROPE]
        length = plat.shape[0]
        tile = min(512, length)
        top = None
        for at in range(0, length, tile):
            scores = dot_nt(lat_rows, plat[at : at + tile, :]) + dot(
                rope_rows, prope[:, at : at + tile]
            )
            sc[:, at : at + tile] = scores
            for lanes in range(0, tile, 128):
                piece = scores[:, lanes : lanes + 128]
                top = piece if top is None else jnp.maximum(top, piece)
        peak = jnp.max(top, axis=1, keepdims=True)
        sums_of = jnp.zeros((rows_all, 128), F32)
        for at in range(0, length, tile):
            probs = jnp.exp2((sc[:, at : at + tile] - peak) * EXP2_SCALE)
            for lanes in range(0, tile, 128):
                sums_of = sums_of + probs[:, lanes : lanes + 128]
            pb[:, at : at + tile] = probs.astype(BF16)
        total = jnp.sum(sums_of, axis=1, keepdims=True)
        fill(pof, dot(pb[...], plat[...]) * (1.0 / total))
        for h in range(heads):
            rows = take(pof, h, duo, heads).astype(BF16)
            rvf[pl.ds(h, duo, stride=16), :] = dot(rows, wuv[h])
        lse = peak * SCALE + jnp.log(total)
        first = lse.astype(BF16).astype(F32)
        second = (lse - first).astype(BF16).astype(F32)
        third = lse - first - second
        row, lane = iota((rows_all, 128), 0), iota((rows_all, 128), 1)
        place = row - heads * ((row * 43691) >> 19)
        spread = (
            jnp.where(lane == place, first, 0.0)
            + jnp.where(lane == place + 16, second, 0.0)
            + jnp.where(lane == place + 32, third, 0.0)
        ).astype(BF16)
        at, of = iota((duo, rows_all), 0) * heads, iota((duo, rows_all), 1)
        pick = jnp.where((of >= at) & (of < at + heads), 1.0, 0.0).astype(BF16)
        rvf[pl.ds(heads, duo, stride=16), :] = dot(pick, spread)
        back[pl.ds(base, size)] = rvf[...].reshape(size, 32, VDIM).astype(BF16)

        @pl.loop(0, size)
        def _(i):
            @pl.when(base + i != own)
            def _():
                back_copy(base + i).start()

    rr[here] = back[own]

    new_out = dot(lnew[...].astype(BF16), ntok[:, :LAT].astype(BF16))
    for s in range(samples):
        rows = slice(32 * s, 32 * s + 32)
        own_out = new_out[rows] + dot(lsc[rows, :].astype(BF16), slat[s])
        fill(lof, own_out * linv[rows, :1], rows)
    for h in range(heads):
        lvf[pl.ds(h, pairs, stride=16), :] = dot(take(lof, h, pairs, 16).astype(BF16), wuv[h])
    for h in range(heads, 16):
        lvf[pl.ds(h, pairs, stride=16), :] = jnp.zeros((pairs, VDIM), F32)
    @pl.loop(1, slots)
    def _(i):
        query_copy(other(i)).wait_send()

    loads[10].wait()

    @pl.loop(1, slots)
    def _(i):
        back_copy(other(i)).wait_recv()

    cuts = (0, 2 * pairs // 3, pairs)
    vgs = (vg0, vg1)
    lhss = (lhs0, lhs1)
    blockss = (blocks0, blocks1)
    sumss = (sums0, sums1)

    def value_copy(g, d):
        return pltpu.make_async_remote_copy(
            src_ref=vgs[g].at[y],
            dst_ref=vgs[g].at[y],
            send_sem=v_send.at[g, d],
            recv_sem=v_recv.at[g, d],
            device_id={"sample": y_at[d]},
            device_id_type=MESH,
        )

    for s in range(samples):
        cf[32 * s : 32 * s + 32, :] = rr[names[s]].astype(F32)
    row, lane = iota((16, 128), 0), iota((16, 128), 1)
    mine = (lane == row) | (lane == row + 16) | (lane == row + 32)
    for g in range(2):
        for pair in range(cuts[g], cuts[g + 1]):
            rows = slice(16 * pair, 16 * pair + 16)
            stat = jnp.broadcast_to(cf[16 * pair + heads : 16 * pair + heads + 1, :], (16, 128))
            lse_prompt = jnp.sum(jnp.where(mine, stat, 0.0), axis=1, keepdims=True)
            lse_local = lse_col[rows, :]
            top = jnp.maximum(lse_prompt, lse_local)
            weight_prompt = jnp.exp(lse_prompt - top)
            weight_local = jnp.exp(lse_local - top)
            lvf[rows, :] = (weight_prompt * cf[rows, :] + weight_local * lvf[rows, :]) / (
                weight_prompt + weight_local
            )
        rows_of = cuts[g + 1] - cuts[g]
        columns = [
            lvf[pl.ds(16 * cuts[g] + h, rows_of, stride=16), :] for h in range(heads)
        ]
        folds = 16 // rows_of if rows_of < 16 else 1
        per = heads // folds
        vgs[g][y] = jnp.concatenate(
            [
                jnp.concatenate(columns[fold * per : (fold + 1) * per], axis=1)
                for fold in range(folds)
            ],
            axis=0,
        ).astype(BF16)
        for d in sorted(range(1, ny), key=lambda d: abs(d - ny // 2)):
            value_copy(g, d).start()

    @pl.loop(1, slots)
    def _(i):
        back_copy(other(i)).wait_send()

    columns_all = wout.shape[1]
    width = columns_all // nh

    def sum_copy(g, target, source):
        return pltpu.make_async_remote_copy(
            src_ref=blockss[g].at[target],
            dst_ref=sumss[g].at[source],
            send_sem=o_send.at[g, target],
            recv_sem=o_recv.at[g, source],
            device_id={"head": target},
            device_id_type=MESH,
        )

    for g in range(2):
        rows_of = cuts[g + 1] - cuts[g]
        folds = 16 // rows_of if rows_of < 16 else 1
        inner = heads * VDIM // folds
        for d in range(1, ny):
            value_copy(g, d).wait_recv()
        for d in range(ny):
            gathered = vgs[g][d].astype(F32)
            for fold in range(folds):
                lhss[g][rows_of * d : rows_of * (d + 1), fold * inner : (fold + 1) * inner] = gathered[
                    fold * rows_of : (fold + 1) * rows_of
                ]
        left = lhss[g][...].astype(BF16)
        rows_here = slice(ny * cuts[g], ny * cuts[g + 1])
        done = 0
        tile = 256
        for at in range(0, columns_all, tile):
            stop = min(at + tile, columns_all)
            part[rows_here, at:stop] = dot(left, wout[:, at:stop])
            while done < nh and (done + 1) * width <= stop:
                start = done * width
                floor = start // 128 * 128
                ceil = min(-(-(start + width) // 128) * 128, columns_all)
                block = part[rows_here, floor:ceil]
                if start > floor:
                    block = pltpu.roll(block, ceil - start, 1)
                blockss[g][done] = block[:, :width].astype(BF16)

                @pl.when(head != done)
                def _(j=done):
                    sum_copy(g, j, head).start()

                done += 1

    for g in range(2):
        for d in range(1, ny):
            value_copy(g, d).wait_send()
    for g in range(2):
        rows_of = cuts[g + 1] - cuts[g]
        result = blockss[g][head].astype(F32)
        for d in range(1, nh):
            source = lax.rem(head + d, nh)
            sum_copy(g, source, source).wait_recv()
            result = result + sumss[g][source].astype(F32)
        result = result.astype(BF16)
        for d in range(ny):
            at = pairs * d + cuts[g]
            out_ref[at : at + rows_of, :] = result[rows_of * d : rows_of * (d + 1)]

    @pl.loop(1, nh)
    def _(d):
        for g in range(2):
            sum_copy(g, lax.rem(head + d, nh), head).wait_send()


def shards(
    q_nope,
    q_rope,
    new_latent,
    new_rope,
    prompt_latent,
    prompt_rope,
    suffix_latent,
    suffix_rope,
    sample_prompt,
    suffix_len,
    w_uk,
    w_uv,
    w_out,
):
    nz, ny, nh = (lax.axis_size(name) for name in ("prompt", "sample", "head"))
    slots = nz * ny
    samples = q_nope.shape[0]
    pairs = 2 * samples
    heads = w_uk.shape[0]
    length = prompt_latent.shape[1]
    width = w_out.shape[1] // nh
    size = slots // CHUNKS
    duo = 2 * size
    rows_all = duo * heads
    count = 16 * pairs
    big = 2 * pairs // 3
    small = pairs - big
    fold = max(1, 16 // small)
    fold_big = max(1, 16 // big)
    vmem = pltpu.VMEM
    dma = pltpu.SemaphoreType.DMA
    in_vmem = pl.BlockSpec(memory_space=pltpu.VMEM)
    in_smem = pl.BlockSpec(memory_space=pltpu.SMEM)
    in_hbm = pl.BlockSpec(memory_space=pltpu.HBM)
    arrays = (
        q_nope,
        q_rope,
        new_latent,
        new_rope,
        prompt_latent,
        prompt_rope,
        suffix_latent,
        suffix_rope,
        w_uk,
        w_uv,
        w_out,
    )
    result = pl.pallas_call(
        functools.partial(kernel, (nz, ny, nh)),
        out_shape=jax.ShapeDtypeStruct((ny * pairs, width), BF16),
        in_specs=[in_smem] * 2 + [in_hbm] * 11,
        out_specs=in_vmem,
        scratch_shapes=[
            vmem(q_nope.shape, BF16),
            vmem(q_rope.shape, BF16),
            vmem(new_latent.shape, BF16),
            vmem(new_rope.shape, BF16),
            vmem(prompt_latent.shape[1:], BF16),
            vmem(prompt_rope.shape[1:], BF16),
            vmem(suffix_latent.shape, BF16),
            vmem(suffix_rope.shape, BF16),
            vmem(w_uk.shape, BF16),
            vmem(w_uv.shape, BF16),
            vmem(w_out.shape, BF16),
            vmem((pairs, heads * NOPE), F32),
            vmem((pairs, LAT + NOPE), F32),
            vmem((pairs * 2 * heads, NOPE), F32),
            vmem((samples, 4 * heads, NOPE), BF16),
            vmem((slots, 4 * heads, NOPE), BF16),
            vmem((slots, 4 * heads, NOPE), BF16),
            vmem((size * 4 * heads, NOPE), F32),
            vmem((LAT // 128, count, 128), F32),
            vmem((count, NOPE), F32),
            vmem((count, suffix_latent.shape[1]), F32),
            vmem((count, pairs), F32),
            vmem((count, VDIM), F32),
            vmem((LAT // 128, count, 128), F32),
            vmem((count, VDIM), F32),
            vmem((count, VDIM), F32),
            vmem((LAT // 128, rows_all, 128), F32),
            vmem((rows_all, NOPE), F32),
            vmem((rows_all, length), F32),
            vmem((rows_all, length), BF16),
            vmem((LAT // 128, rows_all, 128), F32),
            vmem((32 * size, VDIM), F32),
            vmem((slots, 32, VDIM), BF16),
            vmem((slots, 32, VDIM), BF16),
            vmem((count, VDIM), F32),
            vmem((ny, big * fold_big, heads * VDIM // fold_big), BF16),
            vmem((ny, small * fold, heads * VDIM // fold), BF16),
            vmem((ny * big, heads * VDIM), F32),
            vmem((ny * small, heads * VDIM), F32),
            vmem((ny * pairs, w_out.shape[1]), F32),
            vmem((nh, ny * big, width), BF16),
            vmem((nh, ny * small, width), BF16),
            vmem((nh, ny * big, width), BF16),
            vmem((nh, ny * small, width), BF16),
            dma((len(arrays),)),
            dma((slots,)),
            dma((slots,)),
            dma((slots,)),
            dma((slots,)),
            dma((2, ny)),
            dma((2, ny)),
            dma((2, nh)),
            dma((2, nh)),
        ],
        compiler_params=pltpu.CompilerParams(
            collective_id=0, has_side_effects=True, vmem_limit_bytes=56 * 1024 * 1024
        ),
        cost_estimate=pl.CostEstimate(
            flops=4 * 10**9, bytes_accessed=13 * 10**6, transcendentals=10**6
        ),
    )(sample_prompt, suffix_len, *arrays)
    return result.reshape(ny * samples, 2, width)


def solution(mesh):
    placed = (
        P(("prompt", "sample"), None, "head"),
        P(("prompt", "sample"), None, "head"),
        P(("prompt", "sample"), None, None),
        P(("prompt", "sample"), None, None),
        P(("prompt", "sample"), None, None),
        P(("prompt", "sample"), None, None),
        P(("prompt", "sample"), None, None),
        P(("prompt", "sample"), None, None),
        P(("prompt", "sample")),
        P(("prompt", "sample")),
        P("head", None, None),
        P("head", None, None),
        P("head", "sample"),
    )
    return jax.shard_map(
        shards,
        mesh=mesh,
        in_specs=placed,
        out_specs=P("prompt", None, ("sample", "head")),
        check_vma=False,
    )
```

```python
import functools
import math

import jax
import jax.numpy as jnp
from jax import lax
from jax.experimental import pallas as pl
from jax.experimental.pallas import tpu as pltpu
from jax.sharding import PartitionSpec as P

NOPE = 128
ROPE = 64
LAT = 512
VDIM = 128
F32 = jnp.float32
BF16 = jnp.bfloat16
MESH = pl.DeviceIdType.MESH
FLOOR = -1e30
SCALE = 1.0 / math.sqrt(NOPE + ROPE)
EXP2_SCALE = SCALE * math.log2(math.e)
CHUNKS = 4
NT = (((1,), (1,)), ((), ()))


def dot(left, right):
    return jnp.dot(left, right, preferred_element_type=F32)


def dot_nt(left, right):
    return lax.dot_general(left, right, NT, preferred_element_type=F32)


def put(ref, first, count, stride, value):
    for tile in range(ref.shape[0]):
        ref[tile, pl.ds(first, count, stride=stride), :] = value[:, 128 * tile : 128 * (tile + 1)]


def take(ref, first, count, stride):
    tiles = [ref[tile, pl.ds(first, count, stride=stride), :] for tile in range(ref.shape[0])]
    return jnp.concatenate(tiles, axis=1)


def whole(ref, rows=slice(None)):
    return jnp.concatenate([ref[tile, rows, :] for tile in range(ref.shape[0])], axis=1)


def fill(ref, value, rows=slice(None)):
    for tile in range(ref.shape[0]):
        ref[tile, rows, :] = value[:, 128 * tile : 128 * (tile + 1)]


def iota(shape, axis):
    return lax.broadcasted_iota(jnp.int32, shape, axis)


def kernel(
    sizes,
    sp_ref,
    len_ref,
    q_hbm,
    r_hbm,
    nl_hbm,
    nr_hbm,
    plat_hbm,
    prope_hbm,
    slat_hbm,
    srope_hbm,
    wuk_hbm,
    wuv_hbm,
    wout_hbm,
    out_ref,
    q_ref,
    r_ref,
    nl_ref,
    nr_ref,
    plat,
    prope,
    slat,
    srope,
    wuk,
    wuv,
    wout,
    tok,
    ntok,
    qf,
    qb,
    sb,
    rb,
    xf,
    lqf,
    lrf,
    lsc,
    lnew,
    linv,
    lof,
    lvf,
    lse_col,
    plf,
    prf,
    sc,
    pb,
    pof,
    rvf,
    back,
    rr,
    cf,
    vg,
    lhs,
    part,
    blocks,
    sums,
    load_sem,
    q_send,
    q_recv,
    b_send,
    b_recv,
    v_send,
    v_recv,
    o_send,
    o_recv,
):
    nz, ny, nh = sizes
    slots = nz * ny
    samples = q_ref.shape[0]
    pairs = 2 * samples
    heads = wuk.shape[0]
    wide = 2 * heads
    z = lax.axis_index("prompt")
    y = lax.axis_index("sample")
    head = lax.axis_index("head")
    here = z * ny + y

    def ahead(k):
        step = k // ny
        half = (step + 1) // 2
        shift = jnp.where(step % 2 == 1, half, nz - half)
        return lax.rem(z + shift, nz), lax.rem(y + k % ny, ny)

    def behind(k):
        step = k // ny
        half = (step + 1) // 2
        shift = jnp.where(step % 2 == 1, nz - half, half)
        return lax.rem(z + shift, nz), lax.rem(y + ny - k % ny, ny)

    loads = [
        pltpu.make_async_copy(source, target, load_sem.at[index])
        for index, (source, target) in enumerate(
            (
                (q_hbm, q_ref),
                (r_hbm, r_ref),
                (nl_hbm, nl_ref),
                (nr_hbm, nr_ref),
                (wuk_hbm, wuk),
                (plat_hbm.at[0], plat),
                (prope_hbm.at[0], prope),
                (wuv_hbm, wuv),
                (slat_hbm, slat),
                (srope_hbm, srope),
                (wout_hbm, wout),
            )
        )
    ]
    for load in loads[:2]:
        load.start()
    barrier = pltpu.get_barrier_semaphore()

    @pl.loop(1, slots)
    def _(k):
        to_z, to_y = ahead(k)
        pl.semaphore_signal(
            barrier, inc=1, device_id={"prompt": to_z, "sample": to_y}, device_id_type=MESH
        )

    @pl.loop(1, nh)
    def _(d):
        pl.semaphore_signal(
            barrier, inc=1, device_id={"head": lax.rem(head + d, nh)}, device_id_type=MESH
        )

    for load in loads[2:]:
        load.start()

    loads[0].wait()
    for s in range(samples):
        tok[2 * s : 2 * s + 2, :] = q_ref[s].astype(F32)
    for h in range(heads):
        qf[pl.ds(h, pairs, stride=wide), :] = tok[:, h * NOPE : (h + 1) * NOPE]
    loads[1].wait()
    for s in range(samples):
        tok[2 * s : 2 * s + 2, : heads * ROPE] = r_ref[s].astype(F32)
    low = iota((pairs, NOPE), 1) < ROPE
    for h in range(heads):
        both = tok[:, h // 2 * NOPE : (h // 2 + 1) * NOPE]
        if h % 2 == 1:
            both = pltpu.roll(both, ROPE, 1)
        qf[pl.ds(heads + h, pairs, stride=wide), :] = jnp.where(low, both, 0.0)
    for s in range(samples):
        qb[s] = qf[2 * wide * s : 2 * wide * (s + 1), :].astype(BF16)

    early = nz // 2

    def local_attention():
        for s in range(samples):
            ntok[2 * s : 2 * s + 2, :LAT] = nl_ref[s].astype(F32)
            ntok[2 * s : 2 * s + 2, LAT:] = jnp.zeros((2, NOPE), F32)
            ntok[2 * s : 2 * s + 2, LAT : LAT + ROPE] = nr_ref[s].astype(F32)
        for h in range(heads, 16):
            lrf[pl.ds(h, pairs, stride=16), :] = jnp.zeros((pairs, NOPE), F32)
            put(lqf, h, pairs, 16, jnp.zeros((pairs, LAT), F32))
        for h in range(heads):
            rows = qf[pl.ds(h, pairs, stride=wide), :].astype(BF16)
            put(lqf, h, pairs, 16, dot(rows, wuk[h]))
            lrf[pl.ds(h, pairs, stride=16), :] = qf[pl.ds(heads + h, pairs, stride=wide), :]
        lane = iota((32, 128), 1)
        for s in range(samples):
            rows = slice(32 * s, 32 * s + 32)
            scores = dot_nt(whole(lqf, rows).astype(BF16), slat[s]) + dot(
                lrf[rows, :].astype(BF16)[:, :ROPE], srope[s]
            )
            lsc[rows, :] = jnp.where(lane < len_ref[s], scores, FLOOR)
        new_latent = ntok[:, :LAT].astype(BF16)
        new_rope = ntok[:, LAT:].astype(BF16)
        count = 16 * pairs
        new_scores = dot_nt(whole(lqf).astype(BF16), new_latent) + dot_nt(
            lrf[...].astype(BF16), new_rope
        )
        row, key = iota((count, pairs), 0), iota((count, pairs), 1)
        valid = ((key >> 1) == (row >> 5)) & ((key & 1) <= ((row >> 4) & 1))
        new_scores = jnp.where(valid, new_scores, FLOOR)
        old_scores = lsc[...]
        peak = jnp.maximum(
            jnp.max(old_scores, axis=1, keepdims=True), jnp.max(new_scores, axis=1, keepdims=True)
        )
        old_exp = jnp.exp2((old_scores - peak) * EXP2_SCALE)
        new_exp = jnp.exp2((new_scores - peak) * EXP2_SCALE)
        total = jnp.sum(old_exp, axis=1, keepdims=True) + jnp.sum(new_exp, axis=1, keepdims=True)
        lse_col[...] = jnp.broadcast_to(peak * SCALE + jnp.log(total), lse_col.shape)
        linv[...] = jnp.broadcast_to(1.0 / total, linv.shape)
        lsc[...] = old_exp
        lnew[...] = new_exp
        new_out = dot(lnew[...].astype(BF16), ntok[:, :LAT].astype(BF16))
        for s in range(samples):
            rows = slice(32 * s, 32 * s + 32)
            own_out = new_out[rows] + dot(lsc[rows, :].astype(BF16), slat[s])
            fill(lof, own_out * linv[rows, :1], rows)
        for h in range(heads):
            lvf[pl.ds(h, pairs, stride=16), :] = dot(take(lof, h, pairs, 16).astype(BF16), wuv[h])
        for h in range(heads, 16):
            lvf[pl.ds(h, pairs, stride=16), :] = jnp.zeros((pairs, VDIM), F32)

    @pl.when(z < early)
    def _():
        for index in (2, 3, 4, 7, 8, 9):
            loads[index].wait()
        local_attention()

    pl.semaphore_wait(barrier, slots - 1 + nh - 1)

    def query_copy(k):
        to_z, to_y = ahead(k)
        return pltpu.make_async_remote_copy(
            src_ref=sb.at[k],
            dst_ref=rb.at[k],
            send_sem=q_send.at[k],
            recv_sem=q_recv.at[k],
            device_id={"prompt": to_z, "sample": to_y},
            device_id_type=MESH,
        )

    names = [sp_ref[s] for s in range(samples)]

    def sample_for(owner):
        found = 0
        for s in range(samples):
            found = jnp.where(names[s] == owner, s, found)
        return found

    @pl.loop(1, slots)
    def _(k):
        to_z, to_y = ahead(k)
        sb[k] = qb[sample_for(to_z * ny + to_y)]
        query_copy(k).start()

    rb[0] = qb[sample_for(here)]

    loads[5].wait()
    loads[6].wait()

    @pl.when(z >= early)
    def _():
        loads[4].wait()
        loads[7].wait()

    size = slots // CHUNKS
    duo = 2 * size
    rows_all = wide * size
    for h in range(heads, 16):
        rvf[pl.ds(h, duo, stride=16), :] = jnp.zeros((duo, VDIM), F32)

    def back_copy(k):
        to_z, to_y = behind(k)
        return pltpu.make_async_remote_copy(
            src_ref=back.at[k],
            dst_ref=rr.at[here],
            send_sem=b_send.at[k],
            recv_sem=b_recv.at[k],
            device_id={"prompt": to_z, "sample": to_y},
            device_id_type=MESH,
        )

    @pl.loop(0, CHUNKS)
    def _(chunk):
        base = chunk * size

        @pl.loop(0, size)
        def _(i):
            @pl.when(base + i > 0)
            def _():
                query_copy(base + i).wait_recv()

        xf[...] = rb[pl.ds(base, size)].astype(F32).reshape(xf.shape)
        for h in range(heads):
            rows = xf[pl.ds(h, duo, stride=wide), :].astype(BF16)
            put(plf, h, duo, heads, dot(rows, wuk[h]))
            prf[pl.ds(h, duo, stride=heads), :] = xf[pl.ds(heads + h, duo, stride=wide), :]
        lat_rows = whole(plf).astype(BF16)
        rope_rows = prf[...].astype(BF16)[:, :ROPE]
        length = plat.shape[0]
        tile = min(512, length)
        top = None
        for at in range(0, length, tile):
            scores = dot_nt(lat_rows, plat[at : at + tile, :]) + dot(
                rope_rows, prope[:, at : at + tile]
            )
            sc[:, at : at + tile] = scores
            for lanes in range(0, tile, 128):
                piece = scores[:, lanes : lanes + 128]
                top = piece if top is None else jnp.maximum(top, piece)
        peak = jnp.max(top, axis=1, keepdims=True)
        sums_of = jnp.zeros((rows_all, 128), F32)
        for at in range(0, length, tile):
            probs = jnp.exp2((sc[:, at : at + tile] - peak) * EXP2_SCALE)
            for lanes in range(0, tile, 128):
                sums_of = sums_of + probs[:, lanes : lanes + 128]
            pb[:, at : at + tile] = probs.astype(BF16)
        total = jnp.sum(sums_of, axis=1, keepdims=True)
        fill(pof, dot(pb[...], plat[...]) * (1.0 / total))
        for h in range(heads):
            rows = take(pof, h, duo, heads).astype(BF16)
            rvf[pl.ds(h, duo, stride=16), :] = dot(rows, wuv[h])
        lse = peak * SCALE + jnp.log(total)
        first = lse.astype(BF16).astype(F32)
        second = (lse - first).astype(BF16).astype(F32)
        third = lse - first - second
        row, lane = iota((rows_all, 128), 0), iota((rows_all, 128), 1)
        place = row - heads * ((row * 43691) >> 19)
        spread = (
            jnp.where(lane == place, first, 0.0)
            + jnp.where(lane == place + 16, second, 0.0)
            + jnp.where(lane == place + 32, third, 0.0)
        ).astype(BF16)
        at, of = iota((duo, rows_all), 0) * heads, iota((duo, rows_all), 1)
        pick = jnp.where((of >= at) & (of < at + heads), 1.0, 0.0).astype(BF16)
        rvf[pl.ds(heads, duo, stride=16), :] = dot(pick, spread)
        back[pl.ds(base, size)] = rvf[...].reshape(size, 32, VDIM).astype(BF16)

        @pl.loop(0, size)
        def _(i):
            @pl.when(base + i > 0)
            def _():
                back_copy(base + i).start()

    rr[here] = back[0]

    @pl.when(z >= early)
    def _():
        for index in (2, 3, 8, 9):
            loads[index].wait()
        local_attention()

    @pl.loop(1, slots)
    def _(k):
        query_copy(k).wait_send()

    loads[10].wait()

    @pl.loop(1, slots)
    def _(k):
        back_copy(k).wait_recv()

    for s in range(samples):
        cf[32 * s : 32 * s + 32, :] = rr[sp_ref[s]].astype(F32)
    row, lane = iota((16, 128), 0), iota((16, 128), 1)
    mine = (lane == row) | (lane == row + 16) | (lane == row + 32)
    for pair in range(pairs):
        rows = slice(16 * pair, 16 * pair + 16)
        stat = jnp.broadcast_to(cf[16 * pair + heads : 16 * pair + heads + 1, :], (16, 128))
        lse_prompt = jnp.sum(jnp.where(mine, stat, 0.0), axis=1, keepdims=True)
        lse_local = lse_col[rows, :]
        top = jnp.maximum(lse_prompt, lse_local)
        weight_prompt = jnp.exp(lse_prompt - top)
        weight_local = jnp.exp(lse_local - top)
        lvf[rows, :] = (weight_prompt * cf[rows, :] + weight_local * lvf[rows, :]) / (
            weight_prompt + weight_local
        )
    half = heads // 2
    columns = [
        jnp.concatenate(
            [lvf[pl.ds(h, pairs, stride=16), :], lvf[pl.ds(h + half, pairs, stride=16), :]], axis=0
        )
        for h in range(half)
    ]
    vg[y] = jnp.concatenate(columns, axis=1).astype(BF16)

    def value_copy(d):
        return pltpu.make_async_remote_copy(
            src_ref=vg.at[y],
            dst_ref=vg.at[y],
            send_sem=v_send.at[d],
            recv_sem=v_recv.at[d],
            device_id={"sample": lax.rem(y + d, ny)},
            device_id_type=MESH,
        )

    for d in range(1, ny):
        value_copy(d).start()
    for d in range(1, ny):
        value_copy(d).wait_recv()

    for d in range(ny):
        gathered = vg[d].astype(F32)
        lhs[pairs * d : pairs * (d + 1), : half * VDIM] = gathered[:pairs]
        lhs[pairs * d : pairs * (d + 1), half * VDIM :] = gathered[pairs:]
    left = lhs[...].astype(BF16)
    columns_all = wout.shape[1]
    width = columns_all // nh

    def sum_copy(j):
        return pltpu.make_async_remote_copy(
            src_ref=blocks.at[j],
            dst_ref=sums.at[head],
            send_sem=o_send.at[j],
            recv_sem=o_recv.at[head],
            device_id={"head": j},
            device_id_type=MESH,
        )

    done = 0
    tile = 256
    for at in range(0, columns_all, tile):
        stop = min(at + tile, columns_all)
        part[:, at:stop] = dot(left, wout[:, at:stop])
        while done < nh and (done + 1) * width <= stop:
            start = done * width
            floor = start // 128 * 128
            ceil = min(-(-(start + width) // 128) * 128, columns_all)
            block = part[:, floor:ceil]
            if start > floor:
                block = pltpu.roll(block, ceil - start, 1)
            blocks[done] = block[:, :width].astype(BF16)

            @pl.when(head != done)
            def _(j=done):
                sum_copy(j).start()

            done += 1
    @pl.loop(1, slots)
    def _(k):
        back_copy(k).wait_send()

    for d in range(1, ny):
        value_copy(d).wait_send()
    result = blocks[head].astype(F32)
    for d in range(1, nh):
        source = lax.rem(head + d, nh)
        pltpu.make_async_remote_copy(
            src_ref=blocks.at[source],
            dst_ref=sums.at[source],
            send_sem=o_send.at[source],
            recv_sem=o_recv.at[source],
            device_id={"head": source},
            device_id_type=MESH,
        ).wait_recv()
        result = result + sums[source].astype(F32)
    out_ref[...] = result.astype(BF16)


    @pl.loop(1, nh)
    def _(d):
        sum_copy(lax.rem(head + d, nh)).wait_send()


def shards(
    q_nope,
    q_rope,
    new_latent,
    new_rope,
    prompt_latent,
    prompt_rope,
    suffix_latent,
    suffix_rope,
    sample_prompt,
    suffix_len,
    w_uk,
    w_uv,
    w_out,
):
    nz, ny, nh = (lax.axis_size(name) for name in ("prompt", "sample", "head"))
    slots = nz * ny
    samples = q_nope.shape[0]
    pairs = 2 * samples
    heads = w_uk.shape[0]
    length = prompt_latent.shape[1]
    width = w_out.shape[1] // nh
    size = slots // CHUNKS
    duo = 2 * size
    rows_all = duo * heads
    count = 16 * pairs
    vmem = pltpu.VMEM
    dma = pltpu.SemaphoreType.DMA
    in_vmem = pl.BlockSpec(memory_space=pltpu.VMEM)
    in_smem = pl.BlockSpec(memory_space=pltpu.SMEM)
    in_hbm = pl.BlockSpec(memory_space=pltpu.HBM)
    arrays = (
        q_nope,
        q_rope,
        new_latent,
        new_rope,
        prompt_latent,
        prompt_rope,
        suffix_latent,
        suffix_rope,
        w_uk,
        w_uv,
        w_out,
    )
    result = pl.pallas_call(
        functools.partial(kernel, (nz, ny, nh)),
        out_shape=jax.ShapeDtypeStruct((ny * pairs, width), BF16),
        in_specs=[in_smem] * 2 + [in_hbm] * 11,
        out_specs=in_vmem,
        scratch_shapes=[
            vmem(q_nope.shape, BF16),
            vmem(q_rope.shape, BF16),
            vmem(new_latent.shape, BF16),
            vmem(new_rope.shape, BF16),
            vmem(prompt_latent.shape[1:], BF16),
            vmem(prompt_rope.shape[1:], BF16),
            vmem(suffix_latent.shape, BF16),
            vmem(suffix_rope.shape, BF16),
            vmem(w_uk.shape, BF16),
            vmem(w_uv.shape, BF16),
            vmem(w_out.shape, BF16),
            vmem((pairs, heads * NOPE), F32),
            vmem((pairs, LAT + NOPE), F32),
            vmem((pairs * 2 * heads, NOPE), F32),
            vmem((samples, 4 * heads, NOPE), BF16),
            vmem((slots, 4 * heads, NOPE), BF16),
            vmem((slots, 4 * heads, NOPE), BF16),
            vmem((size * 4 * heads, NOPE), F32),
            vmem((LAT // 128, count, 128), F32),
            vmem((count, NOPE), F32),
            vmem((count, suffix_latent.shape[1]), F32),
            vmem((count, pairs), F32),
            vmem((count, VDIM), F32),
            vmem((LAT // 128, count, 128), F32),
            vmem((count, VDIM), F32),
            vmem((count, VDIM), F32),
            vmem((LAT // 128, rows_all, 128), F32),
            vmem((rows_all, NOPE), F32),
            vmem((rows_all, length), F32),
            vmem((rows_all, length), BF16),
            vmem((LAT // 128, rows_all, 128), F32),
            vmem((32 * size, VDIM), F32),
            vmem((slots, 32, VDIM), BF16),
            vmem((slots, 32, VDIM), BF16),
            vmem((count, VDIM), F32),
            vmem((ny, 2 * pairs, heads * VDIM // 2), BF16),
            vmem((ny * pairs, heads * VDIM), F32),
            vmem((ny * pairs, w_out.shape[1]), F32),
            vmem((nh, ny * pairs, width), BF16),
            vmem((nh, ny * pairs, width), BF16),
            dma((len(arrays),)),
            dma((slots,)),
            dma((slots,)),
            dma((slots,)),
            dma((slots,)),
            dma((ny,)),
            dma((ny,)),
            dma((nh,)),
            dma((nh,)),
        ],
        compiler_params=pltpu.CompilerParams(
            collective_id=0, has_side_effects=True, vmem_limit_bytes=56 * 1024 * 1024
        ),
        cost_estimate=pl.CostEstimate(
            flops=4 * 10**9, bytes_accessed=13 * 10**6, transcendentals=10**6
        ),
    )(sample_prompt, suffix_len, *arrays)
    return result.reshape(ny * samples, 2, width)


def solution(mesh):
    placed = (
        P(("prompt", "sample"), None, "head"),
        P(("prompt", "sample"), None, "head"),
        P(("prompt", "sample"), None, None),
        P(("prompt", "sample"), None, None),
        P(("prompt", "sample"), None, None),
        P(("prompt", "sample"), None, None),
        P(("prompt", "sample"), None, None),
        P(("prompt", "sample"), None, None),
        P(("prompt", "sample")),
        P(("prompt", "sample")),
        P("head", None, None),
        P("head", None, None),
        P("head", "sample"),
    )
    return jax.shard_map(
        shards,
        mesh=mesh,
        in_specs=placed,
        out_specs=P("prompt", None, ("sample", "head")),
        check_vma=False,
    )
```

```python
import functools
import math

import jax
import jax.numpy as jnp
from jax import lax
from jax.experimental import pallas as pl
from jax.experimental.pallas import tpu as pltpu
from jax.sharding import PartitionSpec as P

NOPE = 128
ROPE = 64
LAT = 512
VDIM = 128
F32 = jnp.float32
BF16 = jnp.bfloat16
MESH = pl.DeviceIdType.MESH
FLOOR = -1e30
SCALE = 1.0 / math.sqrt(NOPE + ROPE)
EXP2_SCALE = SCALE * math.log2(math.e)
CHUNKS = 4
NT = (((1,), (1,)), ((), ()))


def dot(left, right):
    return jnp.dot(left, right, preferred_element_type=F32)


def dot_nt(left, right):
    return lax.dot_general(left, right, NT, preferred_element_type=F32)


def put(ref, first, count, stride, value):
    for tile in range(ref.shape[0]):
        ref[tile, pl.ds(first, count, stride=stride), :] = value[:, 128 * tile : 128 * (tile + 1)]


def take(ref, first, count, stride):
    tiles = [ref[tile, pl.ds(first, count, stride=stride), :] for tile in range(ref.shape[0])]
    return jnp.concatenate(tiles, axis=1)


def whole(ref, rows=slice(None)):
    return jnp.concatenate([ref[tile, rows, :] for tile in range(ref.shape[0])], axis=1)


def fill(ref, value, rows=slice(None)):
    for tile in range(ref.shape[0]):
        ref[tile, rows, :] = value[:, 128 * tile : 128 * (tile + 1)]


def iota(shape, axis):
    return lax.broadcasted_iota(jnp.int32, shape, axis)


def kernel(
    sizes,
    sp_ref,
    len_ref,
    q_hbm,
    r_hbm,
    nl_hbm,
    nr_hbm,
    plat_hbm,
    prope_hbm,
    slat_hbm,
    srope_hbm,
    wuk_hbm,
    wuv_hbm,
    wout_hbm,
    out_ref,
    q_ref,
    r_ref,
    nl_ref,
    nr_ref,
    plat,
    prope,
    slat,
    srope,
    wuk,
    wuv,
    wout,
    tok,
    ntok,
    qf,
    qb,
    sb,
    rb,
    xf,
    rest,
    rest_of,
    rest_out,
    rest_in,
    rest_all,
    xr,
    lqf,
    lrf,
    lsc,
    lnew,
    linv,
    lof,
    lvf,
    lse_col,
    plf,
    prf,
    sc,
    pb,
    pof,
    rvf,
    back,
    rr,
    cf,
    vg,
    lhs,
    part,
    blocks,
    sums,
    load_sem,
    m_send,
    m_recv,
    f_send,
    f_recv,
    q_send,
    q_recv,
    b_send,
    b_recv,
    v_send,
    v_recv,
    o_send,
    o_recv,
):
    nz, ny, nh = sizes
    slots = nz * ny
    samples = q_ref.shape[0]
    pairs = 2 * samples
    heads = wuk.shape[0]
    kept = 16 - heads
    duos = heads // 2
    z = lax.axis_index("prompt")
    y = lax.axis_index("sample")
    head = lax.axis_index("head")
    here = z * ny + y

    def ahead(k):
        step = k // ny
        half = (step + 1) // 2
        shift = jnp.where(step % 2 == 1, half, nz - half)
        return lax.rem(z + shift, nz), lax.rem(y + k % ny, ny)

    def behind(k):
        step = k // ny
        half = (step + 1) // 2
        shift = jnp.where(step % 2 == 1, nz - half, half)
        return lax.rem(z + shift, nz), lax.rem(y + ny - k % ny, ny)

    loads = [
        pltpu.make_async_copy(source, target, load_sem.at[index])
        for index, (source, target) in enumerate(
            (
                (q_hbm, q_ref),
                (r_hbm, r_ref),
                (nl_hbm, nl_ref),
                (nr_hbm, nr_ref),
                (wuk_hbm, wuk),
                (plat_hbm.at[0], plat),
                (prope_hbm.at[0], prope),
                (wuv_hbm, wuv),
                (slat_hbm, slat),
                (srope_hbm, srope),
                (wout_hbm, wout),
            )
        )
    ]
    for load in loads[:2]:
        load.start()
    barrier = pltpu.get_barrier_semaphore()

    @pl.loop(1, slots)
    def _(k):
        to_z, to_y = ahead(k)
        pl.semaphore_signal(
            barrier, inc=1, device_id={"prompt": to_z, "sample": to_y}, device_id_type=MESH
        )

    @pl.loop(1, nh)
    def _(d):
        pl.semaphore_signal(
            barrier, inc=1, device_id={"head": lax.rem(head + d, nh)}, device_id_type=MESH
        )

    for load in loads[2:]:
        load.start()

    loads[0].wait()
    for s in range(samples):
        tok[2 * s : 2 * s + 2, :] = q_ref[s].astype(F32)
    for h in range(heads):
        qf[pl.ds(h, pairs, stride=16), :] = tok[:, h * NOPE : (h + 1) * NOPE]
    loads[1].wait()
    for s in range(samples):
        tok[2 * s : 2 * s + 2, : heads * ROPE] = r_ref[s].astype(F32)
    for p in range(duos):
        duo_rows = tok[:, p * NOPE : (p + 1) * NOPE]
        if p < kept:
            qf[pl.ds(heads + p, pairs, stride=16), :] = duo_rows
        else:
            rest[pl.ds(p - kept, pairs, stride=2), :] = duo_rows
    for s in range(samples):
        qb[s] = qf[32 * s : 32 * (s + 1), :].astype(BF16)
        rest_of[s, :4, :] = rest[4 * s : 4 * s + 4, :]

    early = nz // 2

    def local_attention():
        for s in range(samples):
            ntok[2 * s : 2 * s + 2, :LAT] = nl_ref[s].astype(F32)
            ntok[2 * s : 2 * s + 2, LAT:] = jnp.zeros((2, NOPE), F32)
            ntok[2 * s : 2 * s + 2, LAT : LAT + ROPE] = nr_ref[s].astype(F32)
        for h in range(heads, 16):
            lrf[pl.ds(h, pairs, stride=16), :] = jnp.zeros((pairs, NOPE), F32)
            put(lqf, h, pairs, 16, jnp.zeros((pairs, LAT), F32))
        for h in range(heads):
            rows = qf[pl.ds(h, pairs, stride=16), :].astype(BF16)
            put(lqf, h, pairs, 16, dot(rows, wuk[h]))
            if h % 2 == 0:
                p = h // 2
                if p < kept:
                    both = qf[pl.ds(heads + p, pairs, stride=16), :]
                else:
                    both = rest[pl.ds(p - kept, pairs, stride=2), :]
                lrf[pl.ds(h, pairs, stride=16), :] = both
                lrf[pl.ds(h + 1, pairs, stride=16), :] = pltpu.roll(both, ROPE, 1)
        lane = iota((32, 128), 1)
        for s in range(samples):
            rows = slice(32 * s, 32 * s + 32)
            scores = dot_nt(whole(lqf, rows).astype(BF16), slat[s]) + dot(
                lrf[rows, :].astype(BF16)[:, :ROPE], srope[s]
            )
            lsc[rows, :] = jnp.where(lane < len_ref[s], scores, FLOOR)
        new_latent = ntok[:, :LAT].astype(BF16)
        new_rope = ntok[:, LAT:].astype(BF16)
        count = 16 * pairs
        new_scores = dot_nt(whole(lqf).astype(BF16), new_latent) + dot_nt(
            lrf[...].astype(BF16), new_rope
        )
        row, key = iota((count, pairs), 0), iota((count, pairs), 1)
        valid = ((key >> 1) == (row >> 5)) & ((key & 1) <= ((row >> 4) & 1))
        new_scores = jnp.where(valid, new_scores, FLOOR)
        old_scores = lsc[...]
        peak = jnp.maximum(
            jnp.max(old_scores, axis=1, keepdims=True), jnp.max(new_scores, axis=1, keepdims=True)
        )
        old_exp = jnp.exp2((old_scores - peak) * EXP2_SCALE)
        new_exp = jnp.exp2((new_scores - peak) * EXP2_SCALE)
        total = jnp.sum(old_exp, axis=1, keepdims=True) + jnp.sum(new_exp, axis=1, keepdims=True)
        lse_col[...] = jnp.broadcast_to(peak * SCALE + jnp.log(total), lse_col.shape)
        linv[...] = jnp.broadcast_to(1.0 / total, linv.shape)
        lsc[...] = old_exp
        lnew[...] = new_exp
        new_out = dot(lnew[...].astype(BF16), ntok[:, :LAT].astype(BF16))
        for s in range(samples):
            rows = slice(32 * s, 32 * s + 32)
            own_out = new_out[rows] + dot(lsc[rows, :].astype(BF16), slat[s])
            fill(lof, own_out * linv[rows, :1], rows)
        for h in range(heads):
            lvf[pl.ds(h, pairs, stride=16), :] = dot(take(lof, h, pairs, 16).astype(BF16), wuv[h])
        for h in range(heads, 16):
            lvf[pl.ds(h, pairs, stride=16), :] = jnp.zeros((pairs, VDIM), F32)

    @pl.when(z < early)
    def _():
        for index in (2, 3, 4, 7, 8, 9):
            loads[index].wait()
        local_attention()

    pl.semaphore_wait(barrier, slots - 1 + nh - 1)

    def query_copy(k):
        to_z, to_y = ahead(k)
        return pltpu.make_async_remote_copy(
            src_ref=sb.at[k],
            dst_ref=rb.at[k],
            send_sem=q_send.at[k],
            recv_sem=q_recv.at[k],
            device_id={"prompt": to_z, "sample": to_y},
            device_id_type=MESH,
        )

    names = [sp_ref[s] for s in range(samples)]

    def sample_for(owner):
        found = 0
        for s in range(samples):
            found = jnp.where(names[s] == owner, s, found)
        return found

    def rest_copy(step):
        to_z, _ = ahead(step * ny)
        return pltpu.make_async_remote_copy(
            src_ref=rest_out.at[step],
            dst_ref=rest_in.at[step],
            send_sem=m_send.at[step],
            recv_sem=m_recv.at[step],
            device_id={"prompt": to_z},
            device_id_type=MESH,
        )

    def pass_copy(d):
        return pltpu.make_async_remote_copy(
            src_ref=rest_in,
            dst_ref=rest_all.at[d],
            send_sem=f_send.at[d],
            recv_sem=f_recv.at[d],
            device_id={"sample": lax.rem(y + d, ny)},
            device_id_type=MESH,
        )

    def rest_tile(step):
        pieces = []
        for d in range(ny):
            to_z, to_y = ahead(step * ny + d)
            pieces.append(rest_of[sample_for(to_z * ny + to_y)][:4])
        return jnp.concatenate(pieces, axis=0)

    @pl.loop(1, nz)
    def _(step):
        rest_out[step] = rest_tile(step).astype(BF16)
        rest_copy(step).start()

    rest_in[0] = rest_tile(0).astype(BF16)

    @pl.loop(1, slots)
    def _(k):
        to_z, to_y = ahead(k)
        sb[k] = qb[sample_for(to_z * ny + to_y)]
        query_copy(k).start()

    rb[0] = qb[sample_for(here)]
    for step in range(1, nz):
        rest_copy(step).wait_recv()
    for d in range(1, ny):
        pass_copy(d).start()
    rest_all[0] = rest_in[...]

    loads[5].wait()
    loads[6].wait()

    @pl.when(z >= early)
    def _():
        loads[4].wait()
        loads[7].wait()

    size = slots // CHUNKS
    duo = 2 * size
    rows_all = 2 * heads * size
    for h in range(heads, 16):
        rvf[pl.ds(h, duo, stride=16), :] = jnp.zeros((duo, VDIM), F32)

    def back_copy(k):
        to_z, to_y = behind(k)
        return pltpu.make_async_remote_copy(
            src_ref=back.at[k],
            dst_ref=rr.at[here],
            send_sem=b_send.at[k],
            recv_sem=b_recv.at[k],
            device_id={"prompt": to_z, "sample": to_y},
            device_id_type=MESH,
        )

    @pl.loop(0, CHUNKS)
    def _(chunk):
        base = chunk * size

        @pl.loop(0, size)
        def _(i):
            @pl.when(base + i > 0)
            def _():
                query_copy(base + i).wait_recv()

        @pl.when(chunk == 0)
        def _():
            for d in range(1, ny):
                pass_copy(d).wait_recv()

        xf[...] = rb[pl.ds(base, size)].astype(F32).reshape(xf.shape)
        for i in range(size):
            d = i % ny
            tile_rows = rest_all[d, chunk * (size // ny) + i // ny].astype(F32)
            xr[4 * i : 4 * i + 4, :] = tile_rows[4 * d : 4 * d + 4]
        for h in range(heads):
            rows = xf[pl.ds(h, duo, stride=16), :].astype(BF16)
            put(plf, h, duo, heads, dot(rows, wuk[h]))
        for p in range(duos):
            if p < kept:
                both = xf[pl.ds(heads + p, duo, stride=16), :]
            else:
                both = xr[pl.ds(p - kept, duo, stride=2), :]
            prf[pl.ds(2 * p, duo, stride=heads), :] = both
            prf[pl.ds(2 * p + 1, duo, stride=heads), :] = pltpu.roll(both, ROPE, 1)
        lat_rows = whole(plf).astype(BF16)
        rope_rows = prf[...].astype(BF16)[:, :ROPE]
        length = plat.shape[0]
        tile = min(512, length)
        top = None
        for at in range(0, length, tile):
            scores = dot_nt(lat_rows, plat[at : at + tile, :]) + dot(
                rope_rows, prope[:, at : at + tile]
            )
            sc[:, at : at + tile] = scores
            for lanes in range(0, tile, 128):
                piece = scores[:, lanes : lanes + 128]
                top = piece if top is None else jnp.maximum(top, piece)
        peak = jnp.max(top, axis=1, keepdims=True)
        sums_of = jnp.zeros((rows_all, 128), F32)
        for at in range(0, length, tile):
            probs = jnp.exp2((sc[:, at : at + tile] - peak) * EXP2_SCALE)
            for lanes in range(0, tile, 128):
                sums_of = sums_of + probs[:, lanes : lanes + 128]
            pb[:, at : at + tile] = probs.astype(BF16)
        total = jnp.sum(sums_of, axis=1, keepdims=True)
        fill(pof, dot(pb[...], plat[...]) * (1.0 / total))
        for h in range(heads):
            rows = take(pof, h, duo, heads).astype(BF16)
            rvf[pl.ds(h, duo, stride=16), :] = dot(rows, wuv[h])
        lse = peak * SCALE + jnp.log(total)
        first = lse.astype(BF16).astype(F32)
        second = (lse - first).astype(BF16).astype(F32)
        third = lse - first - second
        row, lane = iota((rows_all, 128), 0), iota((rows_all, 128), 1)
        place = row - heads * ((row * 43691) >> 19)
        spread = (
            jnp.where(lane == place, first, 0.0)
            + jnp.where(lane == place + 16, second, 0.0)
            + jnp.where(lane == place + 32, third, 0.0)
        ).astype(BF16)
        at, of = iota((duo, rows_all), 0) * heads, iota((duo, rows_all), 1)
        pick = jnp.where((of >= at) & (of < at + heads), 1.0, 0.0).astype(BF16)
        rvf[pl.ds(heads, duo, stride=16), :] = dot(pick, spread)
        back[pl.ds(base, size)] = rvf[...].reshape(size, 32, VDIM).astype(BF16)

        @pl.loop(0, size)
        def _(i):
            @pl.when(base + i > 0)
            def _():
                back_copy(base + i).start()

    rr[here] = back[0]

    @pl.when(z >= early)
    def _():
        for index in (2, 3, 8, 9):
            loads[index].wait()
        local_attention()

    @pl.loop(1, slots)
    def _(k):
        query_copy(k).wait_send()

    for step in range(1, nz):
        rest_copy(step).wait_send()
    for d in range(1, ny):
        pass_copy(d).wait_send()

    loads[10].wait()

    @pl.loop(1, slots)
    def _(k):
        back_copy(k).wait_recv()

    for s in range(samples):
        cf[32 * s : 32 * s + 32, :] = rr[sp_ref[s]].astype(F32)
    row, lane = iota((16, 128), 0), iota((16, 128), 1)
    mine = (lane == row) | (lane == row + 16) | (lane == row + 32)
    for pair in range(pairs):
        rows = slice(16 * pair, 16 * pair + 16)
        stat = jnp.broadcast_to(cf[16 * pair + heads : 16 * pair + heads + 1, :], (16, 128))
        lse_prompt = jnp.sum(jnp.where(mine, stat, 0.0), axis=1, keepdims=True)
        lse_local = lse_col[rows, :]
        top = jnp.maximum(lse_prompt, lse_local)
        weight_prompt = jnp.exp(lse_prompt - top)
        weight_local = jnp.exp(lse_local - top)
        lvf[rows, :] = (weight_prompt * cf[rows, :] + weight_local * lvf[rows, :]) / (
            weight_prompt + weight_local
        )
    half = heads // 2
    columns = [
        jnp.concatenate(
            [lvf[pl.ds(h, pairs, stride=16), :], lvf[pl.ds(h + half, pairs, stride=16), :]], axis=0
        )
        for h in range(half)
    ]
    vg[y] = jnp.concatenate(columns, axis=1).astype(BF16)

    def value_copy(d):
        return pltpu.make_async_remote_copy(
            src_ref=vg.at[y],
            dst_ref=vg.at[y],
            send_sem=v_send.at[d],
            recv_sem=v_recv.at[d],
            device_id={"sample": lax.rem(y + d, ny)},
            device_id_type=MESH,
        )

    for d in range(1, ny):
        value_copy(d).start()
    for d in range(1, ny):
        value_copy(d).wait_recv()

    for d in range(ny):
        gathered = vg[d].astype(F32)
        lhs[pairs * d : pairs * (d + 1), : half * VDIM] = gathered[:pairs]
        lhs[pairs * d : pairs * (d + 1), half * VDIM :] = gathered[pairs:]
    left = lhs[...].astype(BF16)
    columns_all = wout.shape[1]
    width = columns_all // nh

    def sum_copy(j):
        return pltpu.make_async_remote_copy(
            src_ref=blocks.at[j],
            dst_ref=sums.at[head],
            send_sem=o_send.at[j],
            recv_sem=o_recv.at[head],
            device_id={"head": j},
            device_id_type=MESH,
        )

    done = 0
    tile = 256
    for at in range(0, columns_all, tile):
        stop = min(at + tile, columns_all)
        part[:, at:stop] = dot(left, wout[:, at:stop])
        while done < nh and (done + 1) * width <= stop:
            start = done * width
            floor = start // 128 * 128
            ceil = min(-(-(start + width) // 128) * 128, columns_all)
            block = part[:, floor:ceil]
            if start > floor:
                block = pltpu.roll(block, ceil - start, 1)
            blocks[done] = block[:, :width].astype(BF16)

            @pl.when(head != done)
            def _(j=done):
                sum_copy(j).start()

            done += 1
    @pl.loop(1, slots)
    def _(k):
        back_copy(k).wait_send()

    for d in range(1, ny):
        value_copy(d).wait_send()
    result = blocks[head].astype(F32)
    for d in range(1, nh):
        source = lax.rem(head + d, nh)
        pltpu.make_async_remote_copy(
            src_ref=blocks.at[source],
            dst_ref=sums.at[source],
            send_sem=o_send.at[source],
            recv_sem=o_recv.at[source],
            device_id={"head": source},
            device_id_type=MESH,
        ).wait_recv()
        result = result + sums[source].astype(F32)
    out_ref[...] = result.astype(BF16)


    @pl.loop(1, nh)
    def _(d):
        sum_copy(lax.rem(head + d, nh)).wait_send()


def shards(
    q_nope,
    q_rope,
    new_latent,
    new_rope,
    prompt_latent,
    prompt_rope,
    suffix_latent,
    suffix_rope,
    sample_prompt,
    suffix_len,
    w_uk,
    w_uv,
    w_out,
):
    nz, ny, nh = (lax.axis_size(name) for name in ("prompt", "sample", "head"))
    slots = nz * ny
    samples = q_nope.shape[0]
    pairs = 2 * samples
    heads = w_uk.shape[0]
    length = prompt_latent.shape[1]
    width = w_out.shape[1] // nh
    size = slots // CHUNKS
    duo = 2 * size
    rows_all = duo * heads
    count = 16 * pairs
    vmem = pltpu.VMEM
    dma = pltpu.SemaphoreType.DMA
    in_vmem = pl.BlockSpec(memory_space=pltpu.VMEM)
    in_smem = pl.BlockSpec(memory_space=pltpu.SMEM)
    in_hbm = pl.BlockSpec(memory_space=pltpu.HBM)
    arrays = (
        q_nope,
        q_rope,
        new_latent,
        new_rope,
        prompt_latent,
        prompt_rope,
        suffix_latent,
        suffix_rope,
        w_uk,
        w_uv,
        w_out,
    )
    result = pl.pallas_call(
        functools.partial(kernel, (nz, ny, nh)),
        out_shape=jax.ShapeDtypeStruct((ny * pairs, width), BF16),
        in_specs=[in_smem] * 2 + [in_hbm] * 11,
        out_specs=in_vmem,
        scratch_shapes=[
            vmem(q_nope.shape, BF16),
            vmem(q_rope.shape, BF16),
            vmem(new_latent.shape, BF16),
            vmem(new_rope.shape, BF16),
            vmem(prompt_latent.shape[1:], BF16),
            vmem(prompt_rope.shape[1:], BF16),
            vmem(suffix_latent.shape, BF16),
            vmem(suffix_rope.shape, BF16),
            vmem(w_uk.shape, BF16),
            vmem(w_uv.shape, BF16),
            vmem(w_out.shape, BF16),
            vmem((pairs, heads * NOPE), F32),
            vmem((pairs, LAT + NOPE), F32),
            vmem((16 * pairs, NOPE), F32),
            vmem((samples, 32, NOPE), BF16),
            vmem((slots, 32, NOPE), BF16),
            vmem((slots, 32, NOPE), BF16),
            vmem((size * 32, NOPE), F32),
            vmem((2 * pairs, NOPE), F32),
            vmem((samples, 8, NOPE), F32),
            vmem((nz, 16, NOPE), BF16),
            vmem((nz, 16, NOPE), BF16),
            vmem((ny, nz, 16, NOPE), BF16),
            vmem((size * 4, NOPE), F32),
            vmem((LAT // 128, count, 128), F32),
            vmem((count, NOPE), F32),
            vmem((count, suffix_latent.shape[1]), F32),
            vmem((count, pairs), F32),
            vmem((count, VDIM), F32),
            vmem((LAT // 128, count, 128), F32),
            vmem((count, VDIM), F32),
            vmem((count, VDIM), F32),
            vmem((LAT // 128, rows_all, 128), F32),
            vmem((rows_all, NOPE), F32),
            vmem((rows_all, length), F32),
            vmem((rows_all, length), BF16),
            vmem((LAT // 128, rows_all, 128), F32),
            vmem((32 * size, VDIM), F32),
            vmem((slots, 32, VDIM), BF16),
            vmem((slots, 32, VDIM), BF16),
            vmem((count, VDIM), F32),
            vmem((ny, 2 * pairs, heads * VDIM // 2), BF16),
            vmem((ny * pairs, heads * VDIM), F32),
            vmem((ny * pairs, w_out.shape[1]), F32),
            vmem((nh, ny * pairs, width), BF16),
            vmem((nh, ny * pairs, width), BF16),
            dma((len(arrays),)),
            dma((nz,)),
            dma((nz,)),
            dma((ny,)),
            dma((ny,)),
            dma((slots,)),
            dma((slots,)),
            dma((slots,)),
            dma((slots,)),
            dma((ny,)),
            dma((ny,)),
            dma((nh,)),
            dma((nh,)),
        ],
        compiler_params=pltpu.CompilerParams(
            collective_id=0, has_side_effects=True, vmem_limit_bytes=56 * 1024 * 1024
        ),
        cost_estimate=pl.CostEstimate(
            flops=4 * 10**9, bytes_accessed=13 * 10**6, transcendentals=10**6
        ),
    )(sample_prompt, suffix_len, *arrays)
    return result.reshape(ny * samples, 2, width)


def solution(mesh):
    placed = (
        P(("prompt", "sample"), None, "head"),
        P(("prompt", "sample"), None, "head"),
        P(("prompt", "sample"), None, None),
        P(("prompt", "sample"), None, None),
        P(("prompt", "sample"), None, None),
        P(("prompt", "sample"), None, None),
        P(("prompt", "sample"), None, None),
        P(("prompt", "sample"), None, None),
        P(("prompt", "sample")),
        P(("prompt", "sample")),
        P("head", None, None),
        P("head", None, None),
        P("head", "sample"),
    )
    return jax.shard_map(
        shards,
        mesh=mesh,
        in_specs=placed,
        out_specs=P("prompt", None, ("sample", "head")),
        check_vma=False,
    )
```

```python
import functools
import math

import jax
import jax.numpy as jnp
from jax import lax
from jax.experimental import pallas as pl
from jax.experimental.pallas import tpu as pltpu
from jax.sharding import PartitionSpec as P

NOPE = 128
ROPE = 64
LAT = 512
VDIM = 128
F32 = jnp.float32
BF16 = jnp.bfloat16
MESH = pl.DeviceIdType.MESH
FLOOR = -1e30
SCALE = 1.0 / math.sqrt(NOPE + ROPE)
EXP2_SCALE = SCALE * math.log2(math.e)
CHUNKS = 4
NT = (((1,), (1,)), ((), ()))


def dot(left, right):
    return jnp.dot(left, right, preferred_element_type=F32)


def dot_nt(left, right):
    return lax.dot_general(left, right, NT, preferred_element_type=F32)


def put(ref, first, count, stride, value):
    for tile in range(ref.shape[0]):
        ref[tile, pl.ds(first, count, stride=stride), :] = value[:, 128 * tile : 128 * (tile + 1)]


def take(ref, first, count, stride):
    tiles = [ref[tile, pl.ds(first, count, stride=stride), :] for tile in range(ref.shape[0])]
    return jnp.concatenate(tiles, axis=1)


def whole(ref, rows=slice(None)):
    return jnp.concatenate([ref[tile, rows, :] for tile in range(ref.shape[0])], axis=1)


def fill(ref, value, rows=slice(None)):
    for tile in range(ref.shape[0]):
        ref[tile, rows, :] = value[:, 128 * tile : 128 * (tile + 1)]


def iota(shape, axis):
    return lax.broadcasted_iota(jnp.int32, shape, axis)


def kernel(
    sizes,
    sp_ref,
    len_ref,
    q_hbm,
    r_hbm,
    nl_hbm,
    nr_hbm,
    plat_hbm,
    prope_hbm,
    slat_hbm,
    srope_hbm,
    wuk_hbm,
    wuv_hbm,
    wout_hbm,
    out_ref,
    q_ref,
    r_ref,
    nl_ref,
    nr_ref,
    plat,
    prope,
    slat,
    srope,
    wuk,
    wuv,
    wout,
    tok,
    ntok,
    qf,
    qb,
    sb,
    rb,
    xf,
    lqf,
    lrf,
    lsc,
    lnew,
    linv,
    lof,
    lvf,
    lse_col,
    plf,
    prf,
    sc,
    pb,
    pof,
    rvf,
    back,
    rr,
    cf,
    vg,
    lhs,
    part,
    blocks,
    sums,
    load_sem,
    q_send,
    q_recv,
    b_send,
    b_recv,
    v_send,
    v_recv,
    o_send,
    o_recv,
):
    nz, ny, nh = sizes
    slots = nz * ny
    samples = q_ref.shape[0]
    pairs = 2 * samples
    heads = wuk.shape[0]
    wide = 2 * heads
    z = lax.axis_index("prompt")
    y = lax.axis_index("sample")
    head = lax.axis_index("head")
    here = z * ny + y

    def ahead(k):
        step = k // ny
        half = (step + 1) // 2
        shift = jnp.where(step % 2 == 1, half, nz - half)
        return lax.rem(z + shift, nz), lax.rem(y + k % ny, ny)

    def behind(k):
        step = k // ny
        half = (step + 1) // 2
        shift = jnp.where(step % 2 == 1, nz - half, half)
        return lax.rem(z + shift, nz), lax.rem(y + ny - k % ny, ny)

    loads = [
        pltpu.make_async_copy(source, target, load_sem.at[index])
        for index, (source, target) in enumerate(
            (
                (q_hbm, q_ref),
                (r_hbm, r_ref),
                (nl_hbm, nl_ref),
                (nr_hbm, nr_ref),
                (wuk_hbm, wuk),
                (plat_hbm.at[0], plat),
                (prope_hbm.at[0], prope),
                (wuv_hbm, wuv),
                (slat_hbm, slat),
                (srope_hbm, srope),
                (wout_hbm, wout),
            )
        )
    ]
    for load in loads[:2]:
        load.start()
    barrier = pltpu.get_barrier_semaphore()

    @pl.loop(1, slots)
    def _(k):
        to_z, to_y = ahead(k)
        pl.semaphore_signal(
            barrier, inc=1, device_id={"prompt": to_z, "sample": to_y}, device_id_type=MESH
        )

    @pl.loop(1, nh)
    def _(d):
        pl.semaphore_signal(
            barrier, inc=1, device_id={"head": lax.rem(head + d, nh)}, device_id_type=MESH
        )

    for load in loads[2:]:
        load.start()

    loads[0].wait()
    for s in range(samples):
        tok[2 * s : 2 * s + 2, :] = q_ref[s].astype(F32)
    for h in range(heads):
        qf[pl.ds(h, pairs, stride=wide), :] = tok[:, h * NOPE : (h + 1) * NOPE]
    loads[1].wait()
    for s in range(samples):
        tok[2 * s : 2 * s + 2, : heads * ROPE] = r_ref[s].astype(F32)
    low = iota((pairs, NOPE), 1) < ROPE
    for h in range(heads):
        both = tok[:, h // 2 * NOPE : (h // 2 + 1) * NOPE]
        if h % 2 == 1:
            both = pltpu.roll(both, ROPE, 1)
        qf[pl.ds(heads + h, pairs, stride=wide), :] = jnp.where(low, both, 0.0)
    for s in range(samples):
        qb[s] = qf[2 * wide * s : 2 * wide * (s + 1), :].astype(BF16)

    early = nz // 2

    def local_attention():
        for s in range(samples):
            ntok[2 * s : 2 * s + 2, :LAT] = nl_ref[s].astype(F32)
            ntok[2 * s : 2 * s + 2, LAT:] = jnp.zeros((2, NOPE), F32)
            ntok[2 * s : 2 * s + 2, LAT : LAT + ROPE] = nr_ref[s].astype(F32)
        for h in range(heads, 16):
            lrf[pl.ds(h, pairs, stride=16), :] = jnp.zeros((pairs, NOPE), F32)
            put(lqf, h, pairs, 16, jnp.zeros((pairs, LAT), F32))
        for h in range(heads):
            rows = qf[pl.ds(h, pairs, stride=wide), :].astype(BF16)
            put(lqf, h, pairs, 16, dot(rows, wuk[h]))
            lrf[pl.ds(h, pairs, stride=16), :] = qf[pl.ds(heads + h, pairs, stride=wide), :]
        lane = iota((32, 128), 1)
        for s in range(samples):
            rows = slice(32 * s, 32 * s + 32)
            scores = dot_nt(whole(lqf, rows).astype(BF16), slat[s]) + dot(
                lrf[rows, :].astype(BF16)[:, :ROPE], srope[s]
            )
            lsc[rows, :] = jnp.where(lane < len_ref[s], scores, FLOOR)
        new_latent = ntok[:, :LAT].astype(BF16)
        new_rope = ntok[:, LAT:].astype(BF16)
        count = 16 * pairs
        new_scores = dot_nt(whole(lqf).astype(BF16), new_latent) + dot_nt(
            lrf[...].astype(BF16), new_rope
        )
        row, key = iota((count, pairs), 0), iota((count, pairs), 1)
        valid = ((key >> 1) == (row >> 5)) & ((key & 1) <= ((row >> 4) & 1))
        new_scores = jnp.where(valid, new_scores, FLOOR)
        old_scores = lsc[...]
        peak = jnp.maximum(
            jnp.max(old_scores, axis=1, keepdims=True), jnp.max(new_scores, axis=1, keepdims=True)
        )
        old_exp = jnp.exp2((old_scores - peak) * EXP2_SCALE)
        new_exp = jnp.exp2((new_scores - peak) * EXP2_SCALE)
        total = jnp.sum(old_exp, axis=1, keepdims=True) + jnp.sum(new_exp, axis=1, keepdims=True)
        lse_col[...] = jnp.broadcast_to(peak * SCALE + jnp.log(total), lse_col.shape)
        linv[...] = jnp.broadcast_to(1.0 / total, linv.shape)
        lsc[...] = old_exp
        lnew[...] = new_exp
        new_out = dot(lnew[...].astype(BF16), ntok[:, :LAT].astype(BF16))
        for s in range(samples):
            rows = slice(32 * s, 32 * s + 32)
            own_out = new_out[rows] + dot(lsc[rows, :].astype(BF16), slat[s])
            fill(lof, own_out * linv[rows, :1], rows)
        for h in range(heads):
            lvf[pl.ds(h, pairs, stride=16), :] = dot(take(lof, h, pairs, 16).astype(BF16), wuv[h])
        for h in range(heads, 16):
            lvf[pl.ds(h, pairs, stride=16), :] = jnp.zeros((pairs, VDIM), F32)

    @pl.when(z < early)
    def _():
        for index in (2, 3, 4, 7, 8, 9):
            loads[index].wait()
        local_attention()

    pl.semaphore_wait(barrier, slots - 1 + nh - 1)

    def query_copy(k):
        to_z, to_y = ahead(k)
        return pltpu.make_async_remote_copy(
            src_ref=sb.at[k],
            dst_ref=rb.at[k],
            send_sem=q_send.at[k],
            recv_sem=q_recv.at[k],
            device_id={"prompt": to_z, "sample": to_y},
            device_id_type=MESH,
        )

    names = [sp_ref[s] for s in range(samples)]

    def sample_for(owner):
        found = 0
        for s in range(samples):
            found = jnp.where(names[s] == owner, s, found)
        return found

    @pl.loop(1, slots)
    def _(k):
        to_z, to_y = ahead(k)
        sb[k] = qb[sample_for(to_z * ny + to_y)]
        query_copy(k).start()

    rb[0] = qb[sample_for(here)]

    loads[5].wait()
    loads[6].wait()

    @pl.when(z >= early)
    def _():
        loads[4].wait()
        loads[7].wait()

    size = slots // CHUNKS
    duo = 2 * size
    rows_all = wide * size
    for h in range(heads, 16):
        rvf[pl.ds(h, duo, stride=16), :] = jnp.zeros((duo, VDIM), F32)

    def back_copy(k):
        to_z, to_y = behind(k)
        return pltpu.make_async_remote_copy(
            src_ref=back.at[k],
            dst_ref=rr.at[here],
            send_sem=b_send.at[k],
            recv_sem=b_recv.at[k],
            device_id={"prompt": to_z, "sample": to_y},
            device_id_type=MESH,
        )

    @pl.loop(0, CHUNKS)
    def _(chunk):
        base = chunk * size

        @pl.loop(0, size)
        def _(i):
            @pl.when(base + i > 0)
            def _():
                query_copy(base + i).wait_recv()

        xf[...] = rb[pl.ds(base, size)].astype(F32).reshape(xf.shape)
        for h in range(heads):
            rows = xf[pl.ds(h, duo, stride=wide), :].astype(BF16)
            put(plf, h, duo, heads, dot(rows, wuk[h]))
            prf[pl.ds(h, duo, stride=heads), :] = xf[pl.ds(heads + h, duo, stride=wide), :]
        lat_rows = whole(plf).astype(BF16)
        rope_rows = prf[...].astype(BF16)[:, :ROPE]
        length = plat.shape[0]
        tile = min(512, length)
        top = None
        for at in range(0, length, tile):
            scores = dot_nt(lat_rows, plat[at : at + tile, :]) + dot(
                rope_rows, prope[:, at : at + tile]
            )
            sc[:, at : at + tile] = scores
            for lanes in range(0, tile, 128):
                piece = scores[:, lanes : lanes + 128]
                top = piece if top is None else jnp.maximum(top, piece)
        peak = jnp.max(top, axis=1, keepdims=True)
        sums_of = jnp.zeros((rows_all, 128), F32)
        for at in range(0, length, tile):
            probs = jnp.exp2((sc[:, at : at + tile] - peak) * EXP2_SCALE)
            for lanes in range(0, tile, 128):
                sums_of = sums_of + probs[:, lanes : lanes + 128]
            pb[:, at : at + tile] = probs.astype(BF16)
        total = jnp.sum(sums_of, axis=1, keepdims=True)
        fill(pof, dot(pb[...], plat[...]) * (1.0 / total))
        for h in range(heads):
            rows = take(pof, h, duo, heads).astype(BF16)
            rvf[pl.ds(h, duo, stride=16), :] = dot(rows, wuv[h])
        lse = peak * SCALE + jnp.log(total)
        first = lse.astype(BF16).astype(F32)
        second = (lse - first).astype(BF16).astype(F32)
        third = lse - first - second
        row, lane = iota((rows_all, 128), 0), iota((rows_all, 128), 1)
        place = row - heads * ((row * 43691) >> 19)
        spread = (
            jnp.where(lane == place, first, 0.0)
            + jnp.where(lane == place + 16, second, 0.0)
            + jnp.where(lane == place + 32, third, 0.0)
        ).astype(BF16)
        at, of = iota((duo, rows_all), 0) * heads, iota((duo, rows_all), 1)
        pick = jnp.where((of >= at) & (of < at + heads), 1.0, 0.0).astype(BF16)
        rvf[pl.ds(heads, duo, stride=16), :] = dot(pick, spread)
        back[pl.ds(base, size)] = rvf[...].reshape(size, 32, VDIM).astype(BF16)

        @pl.loop(0, size)
        def _(i):
            @pl.when(base + i > 0)
            def _():
                back_copy(base + i).start()

    rr[here] = back[0]

    @pl.when(z >= early)
    def _():
        for index in (2, 3, 8, 9):
            loads[index].wait()
        local_attention()

    @pl.loop(1, slots)
    def _(k):
        query_copy(k).wait_send()

    loads[10].wait()

    @pl.loop(1, slots)
    def _(k):
        back_copy(k).wait_recv()

    for s in range(samples):
        cf[32 * s : 32 * s + 32, :] = rr[sp_ref[s]].astype(F32)
    row, lane = iota((16, 128), 0), iota((16, 128), 1)
    mine = (lane == row) | (lane == row + 16) | (lane == row + 32)
    for pair in range(pairs):
        rows = slice(16 * pair, 16 * pair + 16)
        stat = jnp.broadcast_to(cf[16 * pair + heads : 16 * pair + heads + 1, :], (16, 128))
        lse_prompt = jnp.sum(jnp.where(mine, stat, 0.0), axis=1, keepdims=True)
        lse_local = lse_col[rows, :]
        top = jnp.maximum(lse_prompt, lse_local)
        weight_prompt = jnp.exp(lse_prompt - top)
        weight_local = jnp.exp(lse_local - top)
        lvf[rows, :] = (weight_prompt * cf[rows, :] + weight_local * lvf[rows, :]) / (
            weight_prompt + weight_local
        )
    half = heads // 2
    columns = [
        jnp.concatenate(
            [lvf[pl.ds(h, pairs, stride=16), :], lvf[pl.ds(h + half, pairs, stride=16), :]], axis=0
        )
        for h in range(half)
    ]
    vg[y] = jnp.concatenate(columns, axis=1).astype(BF16)

    def value_copy(d):
        return pltpu.make_async_remote_copy(
            src_ref=vg.at[y],
            dst_ref=vg.at[y],
            send_sem=v_send.at[d],
            recv_sem=v_recv.at[d],
            device_id={"sample": lax.rem(y + d, ny)},
            device_id_type=MESH,
        )

    for d in range(1, ny):
        value_copy(d).start()
    for d in range(1, ny):
        value_copy(d).wait_recv()

    for d in range(ny):
        gathered = vg[d].astype(F32)
        lhs[pairs * d : pairs * (d + 1), : half * VDIM] = gathered[:pairs]
        lhs[pairs * d : pairs * (d + 1), half * VDIM :] = gathered[pairs:]
    left = lhs[...].astype(BF16)
    columns_all = wout.shape[1]
    width = columns_all // nh

    def sum_copy(j):
        return pltpu.make_async_remote_copy(
            src_ref=blocks.at[j],
            dst_ref=sums.at[head],
            send_sem=o_send.at[j],
            recv_sem=o_recv.at[head],
            device_id={"head": j},
            device_id_type=MESH,
        )

    chip, core = head // 2, lax.rem(head, 2)
    side = chip + 1 - 2 * lax.rem(chip, 2)
    blocks_half = nh // 2
    columns_half = columns_all // 2
    far = 1 - chip // 2
    orders = (
        (
            2 * lax.rem(chip + 2, 4) + core,
            2 * lax.rem(chip + 2, 4) + 1 - core,
            2 * (3 - chip) + core,
            2 * (3 - chip) + 1 - core,
        ),
        (2 * side + core, 2 * side + 1 - core, 2 * chip + 1 - core),
    )
    tile = 256
    for turn, select in enumerate((far, 1 - far)):
        first_column = select * columns_half
        for at in range(0, columns_half, tile):
            stop = min(at + tile, columns_half)
            start = pl.multiple_of(first_column + at, 128)
            part[turn, :, at:stop] = dot(left, wout[:, pl.ds(start, stop - at)])
        for j in range(blocks_half):
            start = j * width
            floor = start // 128 * 128
            ceil = min(-(-(start + width) // 128) * 128, columns_half)
            block = part[turn, :, floor:ceil]
            if start > floor:
                block = pltpu.roll(block, ceil - start, 1)
            blocks[select * blocks_half + j] = block[:, :width].astype(BF16)
        for target in orders[turn]:
            sum_copy(target).start()

    @pl.loop(1, slots)
    def _(k):
        back_copy(k).wait_send()

    for d in range(1, ny):
        value_copy(d).wait_send()
    result = blocks[head].astype(F32)
    for d in range(1, nh):
        source = lax.rem(head + d, nh)
        pltpu.make_async_remote_copy(
            src_ref=blocks.at[source],
            dst_ref=sums.at[source],
            send_sem=o_send.at[source],
            recv_sem=o_recv.at[source],
            device_id={"head": source},
            device_id_type=MESH,
        ).wait_recv()
        result = result + sums[source].astype(F32)
    out_ref[...] = result.astype(BF16)


    @pl.loop(1, nh)
    def _(d):
        sum_copy(lax.rem(head + d, nh)).wait_send()


def shards(
    q_nope,
    q_rope,
    new_latent,
    new_rope,
    prompt_latent,
    prompt_rope,
    suffix_latent,
    suffix_rope,
    sample_prompt,
    suffix_len,
    w_uk,
    w_uv,
    w_out,
):
    nz, ny, nh = (lax.axis_size(name) for name in ("prompt", "sample", "head"))
    slots = nz * ny
    samples = q_nope.shape[0]
    pairs = 2 * samples
    heads = w_uk.shape[0]
    length = prompt_latent.shape[1]
    width = w_out.shape[1] // nh
    size = slots // CHUNKS
    duo = 2 * size
    rows_all = duo * heads
    count = 16 * pairs
    vmem = pltpu.VMEM
    dma = pltpu.SemaphoreType.DMA
    in_vmem = pl.BlockSpec(memory_space=pltpu.VMEM)
    in_smem = pl.BlockSpec(memory_space=pltpu.SMEM)
    in_hbm = pl.BlockSpec(memory_space=pltpu.HBM)
    arrays = (
        q_nope,
        q_rope,
        new_latent,
        new_rope,
        prompt_latent,
        prompt_rope,
        suffix_latent,
        suffix_rope,
        w_uk,
        w_uv,
        w_out,
    )
    result = pl.pallas_call(
        functools.partial(kernel, (nz, ny, nh)),
        out_shape=jax.ShapeDtypeStruct((ny * pairs, width), BF16),
        in_specs=[in_smem] * 2 + [in_hbm] * 11,
        out_specs=in_vmem,
        scratch_shapes=[
            vmem(q_nope.shape, BF16),
            vmem(q_rope.shape, BF16),
            vmem(new_latent.shape, BF16),
            vmem(new_rope.shape, BF16),
            vmem(prompt_latent.shape[1:], BF16),
            vmem(prompt_rope.shape[1:], BF16),
            vmem(suffix_latent.shape, BF16),
            vmem(suffix_rope.shape, BF16),
            vmem(w_uk.shape, BF16),
            vmem(w_uv.shape, BF16),
            vmem(w_out.shape, BF16),
            vmem((pairs, heads * NOPE), F32),
            vmem((pairs, LAT + NOPE), F32),
            vmem((pairs * 2 * heads, NOPE), F32),
            vmem((samples, 4 * heads, NOPE), BF16),
            vmem((slots, 4 * heads, NOPE), BF16),
            vmem((slots, 4 * heads, NOPE), BF16),
            vmem((size * 4 * heads, NOPE), F32),
            vmem((LAT // 128, count, 128), F32),
            vmem((count, NOPE), F32),
            vmem((count, suffix_latent.shape[1]), F32),
            vmem((count, pairs), F32),
            vmem((count, VDIM), F32),
            vmem((LAT // 128, count, 128), F32),
            vmem((count, VDIM), F32),
            vmem((count, VDIM), F32),
            vmem((LAT // 128, rows_all, 128), F32),
            vmem((rows_all, NOPE), F32),
            vmem((rows_all, length), F32),
            vmem((rows_all, length), BF16),
            vmem((LAT // 128, rows_all, 128), F32),
            vmem((32 * size, VDIM), F32),
            vmem((slots, 32, VDIM), BF16),
            vmem((slots, 32, VDIM), BF16),
            vmem((count, VDIM), F32),
            vmem((ny, 2 * pairs, heads * VDIM // 2), BF16),
            vmem((ny * pairs, heads * VDIM), F32),
            vmem((2, ny * pairs, w_out.shape[1] // 2), F32),
            vmem((nh, ny * pairs, width), BF16),
            vmem((nh, ny * pairs, width), BF16),
            dma((len(arrays),)),
            dma((slots,)),
            dma((slots,)),
            dma((slots,)),
            dma((slots,)),
            dma((ny,)),
            dma((ny,)),
            dma((nh,)),
            dma((nh,)),
        ],
        compiler_params=pltpu.CompilerParams(
            collective_id=0, has_side_effects=True, vmem_limit_bytes=56 * 1024 * 1024
        ),
        cost_estimate=pl.CostEstimate(
            flops=4 * 10**9, bytes_accessed=13 * 10**6, transcendentals=10**6
        ),
    )(sample_prompt, suffix_len, *arrays)
    return result.reshape(ny * samples, 2, width)


def solution(mesh):
    placed = (
        P(("prompt", "sample"), None, "head"),
        P(("prompt", "sample"), None, "head"),
        P(("prompt", "sample"), None, None),
        P(("prompt", "sample"), None, None),
        P(("prompt", "sample"), None, None),
        P(("prompt", "sample"), None, None),
        P(("prompt", "sample"), None, None),
        P(("prompt", "sample"), None, None),
        P(("prompt", "sample")),
        P(("prompt", "sample")),
        P("head", None, None),
        P("head", None, None),
        P("head", "sample"),
    )
    return jax.shard_map(
        shards,
        mesh=mesh,
        in_specs=placed,
        out_specs=P("prompt", None, ("sample", "head")),
        check_vma=False,
    )
```

```python
import functools
import math

import jax
import jax.numpy as jnp
from jax import lax
from jax.experimental import pallas as pl
from jax.experimental.pallas import tpu as pltpu
from jax.sharding import PartitionSpec as P

NOPE = 128
ROPE = 64
LAT = 512
VDIM = 128
F32 = jnp.float32
BF16 = jnp.bfloat16
MESH = pl.DeviceIdType.MESH
FLOOR = -1e30
SCALE = 1.0 / math.sqrt(NOPE + ROPE)
EXP2_SCALE = SCALE * math.log2(math.e)
CHUNKS = 4
NT = (((1,), (1,)), ((), ()))


def dot(left, right):
    return jnp.dot(left, right, preferred_element_type=F32)


def dot_nt(left, right):
    return lax.dot_general(left, right, NT, preferred_element_type=F32)


def put(ref, first, count, stride, value):
    for tile in range(ref.shape[0]):
        ref[tile, pl.ds(first, count, stride=stride), :] = value[:, 128 * tile : 128 * (tile + 1)]


def take(ref, first, count, stride):
    tiles = [ref[tile, pl.ds(first, count, stride=stride), :] for tile in range(ref.shape[0])]
    return jnp.concatenate(tiles, axis=1)


def whole(ref, rows=slice(None)):
    return jnp.concatenate([ref[tile, rows, :] for tile in range(ref.shape[0])], axis=1)


def fill(ref, value, rows=slice(None)):
    for tile in range(ref.shape[0]):
        ref[tile, rows, :] = value[:, 128 * tile : 128 * (tile + 1)]


def iota(shape, axis):
    return lax.broadcasted_iota(jnp.int32, shape, axis)


def kernel(
    sizes,
    sp_ref,
    len_ref,
    q_hbm,
    r_hbm,
    nl_hbm,
    nr_hbm,
    plat_hbm,
    prope_hbm,
    slat_hbm,
    srope_hbm,
    wuk_hbm,
    wuv_hbm,
    wout_hbm,
    out_ref,
    q_ref,
    r_ref,
    nl_ref,
    nr_ref,
    plat,
    prope,
    slat,
    srope,
    wuk,
    wuv,
    wout,
    tok,
    ntok,
    qf,
    qb,
    sb,
    rb,
    xf,
    lqf,
    lrf,
    lsc,
    lnew,
    linv,
    lof,
    lvf,
    lse_col,
    plf,
    prf,
    sc,
    pb,
    pof,
    rvf,
    back,
    rr,
    cf,
    vg,
    lhs,
    part,
    blocks,
    sums,
    load_sem,
    q_send,
    q_recv,
    b_send,
    b_recv,
    v_send,
    v_recv,
    o_send,
    o_recv,
):
    nz, ny, nh = sizes
    slots = nz * ny
    samples = q_ref.shape[0]
    pairs = 2 * samples
    heads = wuk.shape[0]
    wide = 2 * heads
    z = lax.axis_index("prompt")
    y = lax.axis_index("sample")
    head = lax.axis_index("head")
    here = z * ny + y
    own = slots - ny

    def other(i):
        return jnp.where(i <= own, i - 1, i)

    def ahead(k):
        step = nz - 1 - k // ny
        half = (step + 1) // 2
        shift = jnp.where(step % 2 == 1, half, nz - half)
        return lax.rem(z + shift, nz), lax.rem(y + k % ny, ny)

    def behind(k):
        step = nz - 1 - k // ny
        half = (step + 1) // 2
        shift = jnp.where(step % 2 == 1, nz - half, half)
        return lax.rem(z + shift, nz), lax.rem(y + ny - k % ny, ny)

    loads = [
        pltpu.make_async_copy(source, target, load_sem.at[index])
        for index, (source, target) in enumerate(
            (
                (q_hbm, q_ref),
                (r_hbm, r_ref),
                (nl_hbm, nl_ref),
                (nr_hbm, nr_ref),
                (wuk_hbm, wuk),
                (plat_hbm.at[0], plat),
                (prope_hbm.at[0], prope),
                (wuv_hbm, wuv),
                (slat_hbm, slat),
                (srope_hbm, srope),
                (wout_hbm, wout),
            )
        )
    ]
    for load in loads[:2]:
        load.start()
    barrier = pltpu.get_barrier_semaphore()

    @pl.loop(1, slots)
    def _(i):
        to_z, to_y = ahead(other(i))
        pl.semaphore_signal(
            barrier, inc=1, device_id={"prompt": to_z, "sample": to_y}, device_id_type=MESH
        )

    @pl.loop(1, nh)
    def _(d):
        pl.semaphore_signal(
            barrier, inc=1, device_id={"head": lax.rem(head + d, nh)}, device_id_type=MESH
        )

    for load in loads[2:]:
        load.start()

    loads[0].wait()
    for s in range(samples):
        tok[2 * s : 2 * s + 2, :] = q_ref[s].astype(F32)
    for h in range(heads):
        qf[pl.ds(h, pairs, stride=wide), :] = tok[:, h * NOPE : (h + 1) * NOPE]
    loads[1].wait()
    for s in range(samples):
        tok[2 * s : 2 * s + 2, : heads * ROPE] = r_ref[s].astype(F32)
    low = iota((pairs, NOPE), 1) < ROPE
    for h in range(heads):
        both = tok[:, h // 2 * NOPE : (h // 2 + 1) * NOPE]
        if h % 2 == 1:
            both = pltpu.roll(both, ROPE, 1)
        qf[pl.ds(heads + h, pairs, stride=wide), :] = jnp.where(low, both, 0.0)
    for s in range(samples):
        qb[s] = qf[2 * wide * s : 2 * wide * (s + 1), :].astype(BF16)

    early = nz // 2

    def local_attention():
        for s in range(samples):
            ntok[2 * s : 2 * s + 2, :LAT] = nl_ref[s].astype(F32)
            ntok[2 * s : 2 * s + 2, LAT:] = jnp.zeros((2, NOPE), F32)
            ntok[2 * s : 2 * s + 2, LAT : LAT + ROPE] = nr_ref[s].astype(F32)
        for h in range(heads, 16):
            lrf[pl.ds(h, pairs, stride=16), :] = jnp.zeros((pairs, NOPE), F32)
            put(lqf, h, pairs, 16, jnp.zeros((pairs, LAT), F32))
        for h in range(heads):
            rows = qf[pl.ds(h, pairs, stride=wide), :].astype(BF16)
            put(lqf, h, pairs, 16, dot(rows, wuk[h]))
            lrf[pl.ds(h, pairs, stride=16), :] = qf[pl.ds(heads + h, pairs, stride=wide), :]
        lane = iota((32, 128), 1)
        for s in range(samples):
            rows = slice(32 * s, 32 * s + 32)
            scores = dot_nt(whole(lqf, rows).astype(BF16), slat[s]) + dot(
                lrf[rows, :].astype(BF16)[:, :ROPE], srope[s]
            )
            lsc[rows, :] = jnp.where(lane < len_ref[s], scores, FLOOR)
        new_latent = ntok[:, :LAT].astype(BF16)
        new_rope = ntok[:, LAT:].astype(BF16)
        count = 16 * pairs
        new_scores = dot_nt(whole(lqf).astype(BF16), new_latent) + dot_nt(
            lrf[...].astype(BF16), new_rope
        )
        row, key = iota((count, pairs), 0), iota((count, pairs), 1)
        valid = ((key >> 1) == (row >> 5)) & ((key & 1) <= ((row >> 4) & 1))
        new_scores = jnp.where(valid, new_scores, FLOOR)
        old_scores = lsc[...]
        peak = jnp.maximum(
            jnp.max(old_scores, axis=1, keepdims=True), jnp.max(new_scores, axis=1, keepdims=True)
        )
        old_exp = jnp.exp2((old_scores - peak) * EXP2_SCALE)
        new_exp = jnp.exp2((new_scores - peak) * EXP2_SCALE)
        total = jnp.sum(old_exp, axis=1, keepdims=True) + jnp.sum(new_exp, axis=1, keepdims=True)
        lse_col[...] = jnp.broadcast_to(peak * SCALE + jnp.log(total), lse_col.shape)
        linv[...] = jnp.broadcast_to(1.0 / total, linv.shape)
        lsc[...] = old_exp
        lnew[...] = new_exp
        new_out = dot(lnew[...].astype(BF16), ntok[:, :LAT].astype(BF16))
        for s in range(samples):
            rows = slice(32 * s, 32 * s + 32)
            own_out = new_out[rows] + dot(lsc[rows, :].astype(BF16), slat[s])
            fill(lof, own_out * linv[rows, :1], rows)
        for h in range(heads):
            lvf[pl.ds(h, pairs, stride=16), :] = dot(take(lof, h, pairs, 16).astype(BF16), wuv[h])
        for h in range(heads, 16):
            lvf[pl.ds(h, pairs, stride=16), :] = jnp.zeros((pairs, VDIM), F32)

    @pl.when(z < early)
    def _():
        for index in (2, 3, 4, 7, 8, 9):
            loads[index].wait()
        local_attention()

    pl.semaphore_wait(barrier, slots - 1 + nh - 1)

    def query_copy(k):
        to_z, to_y = ahead(k)
        return pltpu.make_async_remote_copy(
            src_ref=sb.at[k],
            dst_ref=rb.at[k],
            send_sem=q_send.at[k],
            recv_sem=q_recv.at[k],
            device_id={"prompt": to_z, "sample": to_y},
            device_id_type=MESH,
        )

    names = [sp_ref[s] for s in range(samples)]

    def sample_for(owner):
        found = 0
        for s in range(samples):
            found = jnp.where(names[s] == owner, s, found)
        return found

    @pl.loop(1, slots)
    def _(i):
        k = other(i)
        to_z, to_y = ahead(k)
        sb[k] = qb[sample_for(to_z * ny + to_y)]
        query_copy(k).start()

    rb[own] = qb[sample_for(here)]

    loads[5].wait()
    loads[6].wait()

    @pl.when(z >= early)
    def _():
        loads[4].wait()
        loads[7].wait()

    size = slots // CHUNKS
    duo = 2 * size
    rows_all = wide * size
    for h in range(heads, 16):
        rvf[pl.ds(h, duo, stride=16), :] = jnp.zeros((duo, VDIM), F32)

    def back_copy(k):
        to_z, to_y = behind(k)
        return pltpu.make_async_remote_copy(
            src_ref=back.at[k],
            dst_ref=rr.at[here],
            send_sem=b_send.at[k],
            recv_sem=b_recv.at[k],
            device_id={"prompt": to_z, "sample": to_y},
            device_id_type=MESH,
        )

    @pl.loop(0, CHUNKS)
    def _(chunk):
        base = chunk * size

        @pl.loop(0, size)
        def _(i):
            @pl.when(base + i != own)
            def _():
                query_copy(base + i).wait_recv()

        xf[...] = rb[pl.ds(base, size)].astype(F32).reshape(xf.shape)
        for h in range(heads):
            rows = xf[pl.ds(h, duo, stride=wide), :].astype(BF16)
            put(plf, h, duo, heads, dot(rows, wuk[h]))
            prf[pl.ds(h, duo, stride=heads), :] = xf[pl.ds(heads + h, duo, stride=wide), :]
        lat_rows = whole(plf).astype(BF16)
        rope_rows = prf[...].astype(BF16)[:, :ROPE]
        length = plat.shape[0]
        tile = min(512, length)
        top = None
        for at in range(0, length, tile):
            scores = dot_nt(lat_rows, plat[at : at + tile, :]) + dot(
                rope_rows, prope[:, at : at + tile]
            )
            sc[:, at : at + tile] = scores
            for lanes in range(0, tile, 128):
                piece = scores[:, lanes : lanes + 128]
                top = piece if top is None else jnp.maximum(top, piece)
        peak = jnp.max(top, axis=1, keepdims=True)
        sums_of = jnp.zeros((rows_all, 128), F32)
        for at in range(0, length, tile):
            probs = jnp.exp2((sc[:, at : at + tile] - peak) * EXP2_SCALE)
            for lanes in range(0, tile, 128):
                sums_of = sums_of + probs[:, lanes : lanes + 128]
            pb[:, at : at + tile] = probs.astype(BF16)
        total = jnp.sum(sums_of, axis=1, keepdims=True)
        fill(pof, dot(pb[...], plat[...]) * (1.0 / total))
        for h in range(heads):
            rows = take(pof, h, duo, heads).astype(BF16)
            rvf[pl.ds(h, duo, stride=16), :] = dot(rows, wuv[h])
        lse = peak * SCALE + jnp.log(total)
        first = lse.astype(BF16).astype(F32)
        second = (lse - first).astype(BF16).astype(F32)
        third = lse - first - second
        row, lane = iota((rows_all, 128), 0), iota((rows_all, 128), 1)
        place = row - heads * ((row * 43691) >> 19)
        spread = (
            jnp.where(lane == place, first, 0.0)
            + jnp.where(lane == place + 16, second, 0.0)
            + jnp.where(lane == place + 32, third, 0.0)
        ).astype(BF16)
        at, of = iota((duo, rows_all), 0) * heads, iota((duo, rows_all), 1)
        pick = jnp.where((of >= at) & (of < at + heads), 1.0, 0.0).astype(BF16)
        rvf[pl.ds(heads, duo, stride=16), :] = dot(pick, spread)
        back[pl.ds(base, size)] = rvf[...].reshape(size, 32, VDIM).astype(BF16)

        @pl.loop(0, size)
        def _(i):
            @pl.when(base + i != own)
            def _():
                back_copy(base + i).start()

    rr[here] = back[own]

    @pl.when(z >= early)
    def _():
        for index in (2, 3, 8, 9):
            loads[index].wait()
        local_attention()

    @pl.loop(1, slots)
    def _(i):
        query_copy(other(i)).wait_send()

    loads[10].wait()

    @pl.loop(1, slots)
    def _(i):
        back_copy(other(i)).wait_recv()

    for s in range(samples):
        cf[32 * s : 32 * s + 32, :] = rr[sp_ref[s]].astype(F32)
    row, lane = iota((16, 128), 0), iota((16, 128), 1)
    mine = (lane == row) | (lane == row + 16) | (lane == row + 32)
    for pair in range(pairs):
        rows = slice(16 * pair, 16 * pair + 16)
        stat = jnp.broadcast_to(cf[16 * pair + heads : 16 * pair + heads + 1, :], (16, 128))
        lse_prompt = jnp.sum(jnp.where(mine, stat, 0.0), axis=1, keepdims=True)
        lse_local = lse_col[rows, :]
        top = jnp.maximum(lse_prompt, lse_local)
        weight_prompt = jnp.exp(lse_prompt - top)
        weight_local = jnp.exp(lse_local - top)
        lvf[rows, :] = (weight_prompt * cf[rows, :] + weight_local * lvf[rows, :]) / (
            weight_prompt + weight_local
        )
    half = heads // 2
    columns = [
        jnp.concatenate(
            [lvf[pl.ds(h, pairs, stride=16), :], lvf[pl.ds(h + half, pairs, stride=16), :]], axis=0
        )
        for h in range(half)
    ]
    vg[y] = jnp.concatenate(columns, axis=1).astype(BF16)

    def value_copy(d):
        return pltpu.make_async_remote_copy(
            src_ref=vg.at[y],
            dst_ref=vg.at[y],
            send_sem=v_send.at[d],
            recv_sem=v_recv.at[d],
            device_id={"sample": lax.rem(y + d, ny)},
            device_id_type=MESH,
        )

    for d in sorted(range(1, ny), key=lambda d: abs(d - ny // 2)):
        value_copy(d).start()
    for d in range(1, ny):
        value_copy(d).wait_recv()

    for d in range(ny):
        gathered = vg[d].astype(F32)
        lhs[pairs * d : pairs * (d + 1), : half * VDIM] = gathered[:pairs]
        lhs[pairs * d : pairs * (d + 1), half * VDIM :] = gathered[pairs:]
    left = lhs[...].astype(BF16)
    columns_all = wout.shape[1]
    width = columns_all // nh

    def sum_copy(j):
        return pltpu.make_async_remote_copy(
            src_ref=blocks.at[j],
            dst_ref=sums.at[head],
            send_sem=o_send.at[j],
            recv_sem=o_recv.at[head],
            device_id={"head": j},
            device_id_type=MESH,
        )

    chip, core = head // 2, lax.rem(head, 2)
    side = chip + 1 - 2 * lax.rem(chip, 2)
    blocks_half = nh // 2
    columns_half = columns_all // 2
    far = 1 - chip // 2
    orders = (
        (
            2 * lax.rem(chip + 2, 4) + core,
            2 * lax.rem(chip + 2, 4) + 1 - core,
            2 * (3 - chip) + core,
            2 * (3 - chip) + 1 - core,
        ),
        (2 * side + core, 2 * side + 1 - core, 2 * chip + 1 - core),
    )
    tile = 256
    for turn, select in enumerate((far, 1 - far)):
        first_column = select * columns_half
        for at in range(0, columns_half, tile):
            stop = min(at + tile, columns_half)
            start = pl.multiple_of(first_column + at, 128)
            part[turn, :, at:stop] = dot(left, wout[:, pl.ds(start, stop - at)])
        for j in range(blocks_half):
            start = j * width
            floor = start // 128 * 128
            ceil = min(-(-(start + width) // 128) * 128, columns_half)
            block = part[turn, :, floor:ceil]
            if start > floor:
                block = pltpu.roll(block, ceil - start, 1)
            blocks[select * blocks_half + j] = block[:, :width].astype(BF16)
        for target in orders[turn]:
            sum_copy(target).start()

    @pl.loop(1, slots)
    def _(i):
        back_copy(other(i)).wait_send()

    for d in range(1, ny):
        value_copy(d).wait_send()
    result = blocks[head].astype(F32)
    for d in range(1, nh):
        source = lax.rem(head + d, nh)
        pltpu.make_async_remote_copy(
            src_ref=blocks.at[source],
            dst_ref=sums.at[source],
            send_sem=o_send.at[source],
            recv_sem=o_recv.at[source],
            device_id={"head": source},
            device_id_type=MESH,
        ).wait_recv()
        result = result + sums[source].astype(F32)
    out_ref[...] = result.astype(BF16)


    @pl.loop(1, nh)
    def _(d):
        sum_copy(lax.rem(head + d, nh)).wait_send()


def shards(
    q_nope,
    q_rope,
    new_latent,
    new_rope,
    prompt_latent,
    prompt_rope,
    suffix_latent,
    suffix_rope,
    sample_prompt,
    suffix_len,
    w_uk,
    w_uv,
    w_out,
):
    nz, ny, nh = (lax.axis_size(name) for name in ("prompt", "sample", "head"))
    slots = nz * ny
    samples = q_nope.shape[0]
    pairs = 2 * samples
    heads = w_uk.shape[0]
    length = prompt_latent.shape[1]
    width = w_out.shape[1] // nh
    size = slots // CHUNKS
    duo = 2 * size
    rows_all = duo * heads
    count = 16 * pairs
    vmem = pltpu.VMEM
    dma = pltpu.SemaphoreType.DMA
    in_vmem = pl.BlockSpec(memory_space=pltpu.VMEM)
    in_smem = pl.BlockSpec(memory_space=pltpu.SMEM)
    in_hbm = pl.BlockSpec(memory_space=pltpu.HBM)
    arrays = (
        q_nope,
        q_rope,
        new_latent,
        new_rope,
        prompt_latent,
        prompt_rope,
        suffix_latent,
        suffix_rope,
        w_uk,
        w_uv,
        w_out,
    )
    result = pl.pallas_call(
        functools.partial(kernel, (nz, ny, nh)),
        out_shape=jax.ShapeDtypeStruct((ny * pairs, width), BF16),
        in_specs=[in_smem] * 2 + [in_hbm] * 11,
        out_specs=in_vmem,
        scratch_shapes=[
            vmem(q_nope.shape, BF16),
            vmem(q_rope.shape, BF16),
            vmem(new_latent.shape, BF16),
            vmem(new_rope.shape, BF16),
            vmem(prompt_latent.shape[1:], BF16),
            vmem(prompt_rope.shape[1:], BF16),
            vmem(suffix_latent.shape, BF16),
            vmem(suffix_rope.shape, BF16),
            vmem(w_uk.shape, BF16),
            vmem(w_uv.shape, BF16),
            vmem(w_out.shape, BF16),
            vmem((pairs, heads * NOPE), F32),
            vmem((pairs, LAT + NOPE), F32),
            vmem((pairs * 2 * heads, NOPE), F32),
            vmem((samples, 4 * heads, NOPE), BF16),
            vmem((slots, 4 * heads, NOPE), BF16),
            vmem((slots, 4 * heads, NOPE), BF16),
            vmem((size * 4 * heads, NOPE), F32),
            vmem((LAT // 128, count, 128), F32),
            vmem((count, NOPE), F32),
            vmem((count, suffix_latent.shape[1]), F32),
            vmem((count, pairs), F32),
            vmem((count, VDIM), F32),
            vmem((LAT // 128, count, 128), F32),
            vmem((count, VDIM), F32),
            vmem((count, VDIM), F32),
            vmem((LAT // 128, rows_all, 128), F32),
            vmem((rows_all, NOPE), F32),
            vmem((rows_all, length), F32),
            vmem((rows_all, length), BF16),
            vmem((LAT // 128, rows_all, 128), F32),
            vmem((32 * size, VDIM), F32),
            vmem((slots, 32, VDIM), BF16),
            vmem((slots, 32, VDIM), BF16),
            vmem((count, VDIM), F32),
            vmem((ny, 2 * pairs, heads * VDIM // 2), BF16),
            vmem((ny * pairs, heads * VDIM), F32),
            vmem((2, ny * pairs, w_out.shape[1] // 2), F32),
            vmem((nh, ny * pairs, width), BF16),
            vmem((nh, ny * pairs, width), BF16),
            dma((len(arrays),)),
            dma((slots,)),
            dma((slots,)),
            dma((slots,)),
            dma((slots,)),
            dma((ny,)),
            dma((ny,)),
            dma((nh,)),
            dma((nh,)),
        ],
        compiler_params=pltpu.CompilerParams(
            collective_id=0, has_side_effects=True, vmem_limit_bytes=56 * 1024 * 1024
        ),
        cost_estimate=pl.CostEstimate(
            flops=4 * 10**9, bytes_accessed=13 * 10**6, transcendentals=10**6
        ),
    )(sample_prompt, suffix_len, *arrays)
    return result.reshape(ny * samples, 2, width)


def solution(mesh):
    placed = (
        P(("prompt", "sample"), None, "head"),
        P(("prompt", "sample"), None, "head"),
        P(("prompt", "sample"), None, None),
        P(("prompt", "sample"), None, None),
        P(("prompt", "sample"), None, None),
        P(("prompt", "sample"), None, None),
        P(("prompt", "sample"), None, None),
        P(("prompt", "sample"), None, None),
        P(("prompt", "sample")),
        P(("prompt", "sample")),
        P("head", None, None),
        P("head", None, None),
        P("head", "sample"),
    )
    return jax.shard_map(
        shards,
        mesh=mesh,
        in_specs=placed,
        out_specs=P("prompt", None, ("sample", "head")),
        check_vma=False,
    )
```
